32 devices in a mesh: dp: 8 (over z, x), tensor: 4 (over y, core).
Axes of the slice: x: 2, y: 2, z: 4, core: 2. Of those that a mesh axis runs over, the one named last changes fastest.
Arguments:
- tokens: bfloat16 [7680, 4096], P('dp'), may hold values from -70 to 70
- dense_weight: bfloat16 [4096, 14336], P('dp', 'tensor'), may hold values from -0.09375 to 0.09375
- left_factor: bfloat16 [64, 4096], P(None, 'tensor'), may hold values from -0.75 to 0.75
- right_factor: bfloat16 [64, 14336], P(None, 'tensor'), may hold values from -0.75 to 0.75
Outputs:
- dir_left: float32 [64, 4096], P('dp', 'tensor')
- dir_right: float32 [64, 14336], P('dp', 'tensor')
- loss: float32 [], replicated
The draws below stay inside these ranges and needn't reach their ends.
All inputs are finite; a program needn't handle non-finite values.
Results may differ from the reference program's by a relative error of at most 0.0009.
Values may be sent and summed in bfloat16 or wider, within the bound.
No kernel may reach another device: no remote copies, remote signals or barrier semaphores. Data moves between devices by JAX's collectives and lax.ppermute only.
A program may use at most 128 MiB of HBM per device.

```python
import jax
import jax.numpy as jnp
from jax import lax

D = 4096
F = 14336
NB = 64
SI = 64
SO = 224
MID = 4096
TOK_DEV = 960
TOKENS = 7680
N_DP = 8


def draw_tokens(key, part):
    key_base, key_rows, key_cols = jax.random.split(key, 3)
    positions = jnp.arange(TOKENS, dtype=jnp.float32) / TOKENS
    row_scale = 0.5 * jnp.exp(jnp.log(3.0) * positions) * jnp.exp(jnp.log(10.0) * 0.5 * jax.random.uniform(key_rows, (TOKENS,), jnp.float32))
    col_scale = jnp.exp(jnp.log(10.0) * (jax.random.uniform(key_cols, (D,), jnp.float32) - 0.5))
    base = jnp.clip(jax.random.normal(key_base, (TOKENS, D), jnp.float32), -4.0, 4.0)
    return (base * row_scale[:, None] * col_scale[None, :]).astype(jnp.bfloat16)


def shard_levels(own_key, extent, pieces, smallest, high):
    loudness, own = 1.0, jax.random.fold_in(own_key, 6)
    for position, blocks in pieces:
        steps = jnp.exp(jax.random.uniform(jax.random.fold_in(own, position), (blocks,), jnp.float32, smallest / len(pieces), high / len(pieces)))
        loudness = loudness * jnp.repeat(steps, extent[position] // blocks).reshape([-1 if axis == position else 1 for axis in range(len(extent))])
    return loudness


def noise(rng, shape, scale, reach, cuts=(), kind=jnp.bfloat16):
    entries = jax.random.normal(rng, shape, jnp.float32) * scale
    if len(cuts) > 0:
        entries = shard_levels(rng, shape, cuts, -0.22, 0.18) * entries
    return jnp.clip(entries, min=-reach, max=reach).astype(kind)


def setup_inputs(seed: int = 0) -> dict:
    key_of = jax.random.split(jax.random.key(seed), 5)
    tokens = draw_tokens(jax.random.fold_in(key_of[4], 71), 0)
    dense_weight = noise(key_of[1], (D, F), D ** -0.5, 0.09375, ((0, 8), (1, 4)))
    left_factor = noise(key_of[2], (SI, MID), SI ** -0.5, 0.75, ((1, 4),))
    right_factor = noise(key_of[3], (NB, F), NB ** -0.5, 0.75, ((1, 4),))
    return {"tokens": tokens, "dense_weight": dense_weight, "left_factor": left_factor, "right_factor": right_factor}


epsilon = 1e-06

def round_half(values):
    rounded = values.astype(jnp.bfloat16)
    rounded = lax.optimization_barrier(rounded)
    return rounded.astype(jnp.float32)

def block_terms(token_block, dense_weight, left_blocks, right_blocks):
    tok_rows = token_block.shape[0]
    features = token_block.reshape(tok_rows, NB, SI).astype(jnp.float32)
    first_mix = round_half(jnp.einsum('tik,kij->tji', features, left_blocks.astype(jnp.float32)))
    output = jnp.einsum('tji,ijo->tjo', first_mix, right_blocks.astype(jnp.float32)).reshape(tok_rows, F)
    targets = jnp.dot(token_block, dense_weight, preferred_element_type=jnp.float32)
    residual = output - targets
    slope_rows = round_half(residual / TOKENS).reshape(tok_rows, NB, SO)
    grad_right = jnp.einsum('tji,tjo->ijo', first_mix, slope_rows).reshape(NB, F)
    back_mix = round_half(jnp.einsum('tjo,ijo->tji', slope_rows, right_blocks.astype(jnp.float32)))
    grad_left = jnp.einsum('tik,tji->kij', features, back_mix).reshape(SI, MID)
    return (grad_left, grad_right, jnp.sum(residual * residual))

def reference(tokens, dense_weight, left_factor, right_factor):
    left_blocks = left_factor.reshape(SI, NB, NB)
    right_blocks = right_factor.reshape(NB, NB, SO)
    token_blocks = tokens.reshape(N_DP, TOK_DEV, D)

    def accumulate(carry, token_block):
        terms = block_terms(token_block, dense_weight, left_blocks, right_blocks)
        return ((carry[0] + terms[0], carry[1] + terms[1], carry[2] + terms[2]), None)
    start = (jnp.zeros((SI, MID), jnp.float32), jnp.zeros((NB, F), jnp.float32), jnp.zeros((), jnp.float32))
    totals, unused = lax.scan(accumulate, start, token_blocks)
    grad_left, grad_right, squares = totals
    dir_left = grad_left * lax.rsqrt(jnp.mean(grad_left * grad_left) + epsilon)
    dir_right = grad_right * lax.rsqrt(jnp.mean(grad_right * grad_right) + epsilon)
    loss = squares / (2.0 * TOKENS)
    return (dir_left, dir_right, loss)
```

```python
import jax
import jax.numpy as jnp
from jax import lax
from jax.sharding import PartitionSpec as P

epsilon = 1e-06


def swap(value, axis, stride):
    size = lax.axis_size(axis)
    return lax.ppermute(value, axis, [(a, a ^ stride) for a in range(size)])


def ordered(value, axis, strides):
    position = lax.axis_index(axis)
    for stride in strides:
        other = swap(value, axis, stride)
        high = (position // stride) % 2 == 1
        value = jnp.concatenate([jnp.where(high, other, value), jnp.where(high, value, other)], 0)
    return value


def local(tokens, dense_weight, left_factor, right_factor):
    tok_rows, features = tokens.shape
    weight_rows, columns = dense_weight.shape
    dp_count = lax.axis_size("dp")
    tensor_count = lax.axis_size("tensor")
    dp_pos = lax.axis_index("dp")
    tensor_pos = lax.axis_index("tensor")
    in_size = left_factor.shape[0]
    mids = right_factor.shape[0]
    blocks = left_factor.shape[1] * tensor_count // mids
    own_blocks = blocks // tensor_count
    out_size = columns // own_blocks
    total_tokens = tok_rows * dp_count

    bits = dp_count.bit_length() - 1
    strides = [1 << b for b in range(bits)]
    grouped = max(bits - 3, 0)
    pair = strides[grouped:][len(strides[grouped:]) // 2]
    others = [s for s in reversed(strides[grouped:]) if s != pair]
    pair_bit = (dp_pos // pair) % 2
    unit_rows = weight_rows << grouped

    half_blocks = own_blocks // 2
    chunks = 2 if half_blocks % 2 == 0 else 1
    chunk_blocks = half_blocks // chunks
    chunk_columns = chunk_blocks * out_size
    half_columns = half_blocks * out_size

    def weight_piece(half, chunk):
        start = half * half_columns + chunk * chunk_columns
        return lax.dynamic_slice_in_dim(dense_weight, start, chunk_columns, 1)

    gathered = []
    for chunk in range(chunks):
        mine = ordered(weight_piece(pair_bit, chunk), "dp", strides[:grouped])
        theirs = ordered(weight_piece(1 - pair_bit, chunk), "dp", strides[:grouped])
        held = {0: mine, pair: swap(theirs, "dp", pair)}
        for stride in others:
            for mask in list(held):
                held[mask ^ stride] = swap(held[mask], "dp", stride)
        gathered.append(held)

    share = tok_rows // tensor_count
    part = lax.dynamic_slice_in_dim(tokens, tensor_pos * share, share, 0)
    part = swap(part, "dp", pair)
    partner = ordered(part, "tensor", [1 << b for b in range(tensor_count.bit_length() - 1)])

    left_blocks = left_factor.reshape(in_size, mids // tensor_count, blocks)
    left_blocks = lax.all_to_all(left_blocks, "tensor", split_axis=2, concat_axis=1, tiled=True)
    left_blocks = lax.dynamic_slice_in_dim(left_blocks, pair_bit * half_blocks, half_blocks, 2)
    eye_left = jnp.eye(mids, dtype=jnp.bfloat16)
    left_rows = left_blocks.transpose(1, 0, 2)
    left_diag = (left_rows[:, :, :, None] * eye_left[:, None, None, :]).reshape(features, half_blocks * mids)
    right_half = lax.dynamic_slice_in_dim(right_factor, pair_bit * half_columns, half_columns, 1)

    column_block = jnp.arange(chunk_columns) // out_size
    row_block = jnp.arange(chunk_blocks * mids) // mids
    same_block = row_block[:, None] == column_block[None, :]
    feature_block = jnp.arange(features) // in_size
    same_mid = jnp.arange(mids)[:, None] == feature_block[None, :]

    token_sets = (tokens, partner)
    mixes = [
        jnp.dot(rows, left_diag, preferred_element_type=jnp.float32).astype(jnp.bfloat16) for rows in token_sets
    ]

    loss_part = jnp.zeros((), jnp.float32)
    right_parts, left_parts = [], []
    for chunk in range(chunks):
        right_chunk = right_half[:, chunk * chunk_columns : (chunk + 1) * chunk_columns]
        right_diag = jnp.where(same_block, jnp.tile(right_chunk, (chunk_blocks, 1)), jnp.bfloat16(0))
        grad_right, grad_left = 0.0, 0.0
        for rows, mix in zip(token_sets, mixes):
            mix_chunk = mix[:, chunk * chunk_blocks * mids : (chunk + 1) * chunk_blocks * mids]
            residual = jnp.dot(mix_chunk, right_diag, preferred_element_type=jnp.float32)
            for mask, piece in gathered[chunk].items():
                start = ((dp_pos ^ mask) >> grouped) * unit_rows
                some = lax.dynamic_slice_in_dim(rows, start, unit_rows, 1)
                residual = residual - jnp.dot(some, piece, preferred_element_type=jnp.float32)
            loss_part = loss_part + jnp.sum(residual * residual)
            slope = (residual / total_tokens).astype(jnp.bfloat16)
            grad_right = grad_right + lax.dot_general(
                mix_chunk, slope, (((0,), (0,)), ((), ())), preferred_element_type=jnp.float32
            )
            back_mix = lax.dot_general(
                slope, right_diag, (((1,), (1,)), ((), ())), preferred_element_type=jnp.float32
            ).astype(jnp.bfloat16)
            grad_left = grad_left + lax.dot_general(
                back_mix, rows, (((0,), (0,)), ((), ())), preferred_element_type=jnp.float32
            )
        right_parts.append(
            jnp.concatenate(
                [
                    grad_right[b * mids : (b + 1) * mids, b * out_size : (b + 1) * out_size]
                    for b in range(chunk_blocks)
                ],
                1,
            )
        )
        left_parts.append(
            jnp.sum(jnp.where(same_mid[None], grad_left.reshape(chunk_blocks, mids, features), 0.0), 1)
        )

    left_sum = jnp.concatenate(left_parts, 0).reshape(half_blocks, mids, in_size).transpose(2, 0, 1)
    both = jnp.concatenate([*right_parts, left_sum.reshape(in_size, half_blocks * mids)], 1)
    width = both.shape[1]
    both = both.reshape((2,) * bits + (both.shape[0] // dp_count, width))
    order = [s for s in reversed(strides)]
    for stride in others + strides[:grouped]:
        at = order.index(stride)
        bit = (dp_pos // stride) % 2
        away = lax.dynamic_index_in_dim(both, 1 - bit, at, keepdims=False)
        kept = lax.dynamic_index_in_dim(both, bit, at, keepdims=False)
        both = kept + swap(away, "dp", stride)
        order.remove(stride)
    away = lax.dynamic_index_in_dim(both, 1 - pair_bit, 0, keepdims=False)
    kept = lax.dynamic_index_in_dim(both, pair_bit, 0, keepdims=False)
    other = swap(away, "dp", pair)
    low = jnp.where(pair_bit == 0, kept, other)
    high = jnp.where(pair_bit == 0, other, kept)
    right_rows = jnp.concatenate([low[:, :half_columns], high[:, :half_columns]], 1)
    left_low = low[:, half_columns:].reshape(-1, half_blocks, mids)
    left_high = high[:, half_columns:].reshape(-1, half_blocks, mids)
    left_rows = jnp.concatenate([left_low, left_high], 1)

    sq_left, sq_right, loss_all = lax.psum(
        (jnp.sum(left_rows * left_rows), jnp.sum(right_rows * right_rows), loss_part), ("dp", "tensor")
    )
    left_rows = lax.all_to_all(left_rows, "tensor", split_axis=2, concat_axis=1, tiled=True)
    left_rows = left_rows.transpose(0, 2, 1).reshape(left_rows.shape[0], -1)
    dir_left = left_rows * lax.rsqrt(sq_left / (features * blocks) + epsilon)
    dir_right = right_rows * lax.rsqrt(sq_right / (mids * columns * tensor_count) + epsilon)
    loss = loss_all / (2.0 * total_tokens)
    return (dir_left, dir_right, loss)


def solution(mesh):
    in_specs = (P("dp", None), P("dp", "tensor"), P(None, "tensor"), P(None, "tensor"))
    out_specs = (P("dp", "tensor"), P("dp", "tensor"), P())
    return jax.shard_map(local, mesh=mesh, in_specs=in_specs, out_specs=out_specs, check_vma=False)
```

```python
import functools

import jax
import jax.numpy as jnp
from jax import lax
from jax.experimental import pallas as pl
from jax.experimental.pallas import tpu as pltpu
from jax.sharding import PartitionSpec as P

epsilon = 1e-06
VMEM_BYTES = 56 * 1024 * 1024


def swap(value, axis, stride):
    size = lax.axis_size(axis)
    return lax.ppermute(value, axis, [(a, a ^ stride) for a in range(size)])


class Lane:
    def __init__(self, depth):
        self.depth = depth
        self.sent = []

    def swap(self, value, axis, stride):
        if len(self.sent) >= self.depth:
            value, _ = lax.optimization_barrier((value, self.sent[-self.depth]))
        result = swap(value, axis, stride)
        self.sent.append(result)
        return result


def ordered(value, axis, strides):
    position = lax.axis_index(axis)
    for stride in strides:
        other = swap(value, axis, stride)
        high = (position // stride) % 2 == 1
        value = jnp.concatenate([jnp.where(high, other, value), jnp.where(high, value, other)], 0)
    return value


def contract(a, b, a_dim, b_dim):
    return lax.dot_general(a, b, (((a_dim,), (b_dim,)), ((), ())), preferred_element_type=jnp.float32)


def products_kernel(count, resume, finish, blocks, total_tokens, starts_ref, *refs):
    rows_ref, mix_ref, right_ref = refs[:3]
    pieces = refs[3 : 3 + count]
    rest = refs[3 + count :]
    if resume:
        residual = rest[0][...]
        rest = rest[1:]
    else:
        residual = contract(mix_ref[...], right_ref[...], 1, 0)
    for index in range(count):
        depth = pieces[index].shape[0]
        start = pl.multiple_of(starts_ref[index] * depth, depth)
        residual = residual - contract(rows_ref[:, pl.ds(start, depth)], pieces[index][...], 1, 0)
    if not finish:
        rest[0][...] = residual
        return
    right_out, left_out, loss_out = rest
    columns = right_ref.shape[1]
    mids = right_ref.shape[0] // blocks
    features = rows_ref.shape[1]
    in_size = features // mids

    @pl.when(pl.program_id(0) == 0)
    def _():
        right_out[...] = jnp.zeros_like(right_out)
        left_out[...] = jnp.zeros_like(left_out)
        loss_out[...] = jnp.zeros_like(loss_out)

    loss_out[...] += jnp.sum(residual * residual, axis=0, keepdims=True)
    slope = (residual / total_tokens).astype(jnp.bfloat16)
    full_right = contract(mix_ref[...], slope, 0, 0)
    column_block = lax.broadcasted_iota(jnp.int32, (mids, columns), 1) // (columns // blocks)
    grad_right = jnp.zeros((mids, columns), jnp.float32)
    for b in range(blocks):
        grad_right = jnp.where(column_block == b, full_right[b * mids : (b + 1) * mids], grad_right)
    right_out[...] += grad_right
    back_mix = contract(slope, right_ref[...], 1, 1).astype(jnp.bfloat16)
    span = min(features, 1024)
    for at in range(0, features, span):
        full_left = contract(back_mix, rows_ref[:, at : at + span], 0, 0)
        feature_block = (lax.broadcasted_iota(jnp.int32, (mids, span), 1) + at) // in_size
        same = lax.broadcasted_iota(jnp.int32, (mids, span), 0) == feature_block
        for b in range(blocks):
            part = jnp.where(same, full_left[b * mids : (b + 1) * mids], 0.0)
            left_out[b : b + 1, at : at + span] += jnp.sum(part, axis=0, keepdims=True)


def products(rows, mix, right_diag, pieces, starts, blocks, total_tokens, partial=None, finish=True):
    count = len(pieces)
    tokens, features = rows.shape
    mid_columns, columns = right_diag.shape
    steps = 1 if tokens <= 480 else 2
    tile = tokens // steps
    whole = lambda shape: pl.BlockSpec(shape, lambda t, starts: (0, 0))
    tiled = lambda width: pl.BlockSpec((tile, width), lambda t, starts: (t, 0))
    operands = [rows, mix, right_diag, *pieces]
    in_specs = [tiled(features), tiled(mid_columns), whole(right_diag.shape), *[whole(p.shape) for p in pieces]]
    if partial is not None:
        operands.append(partial)
        in_specs.append(tiled(columns))
    if finish:
        shapes = [(mid_columns // blocks, columns), (blocks, features), (1, columns)]
        out_specs = [whole(shape) for shape in shapes]
    else:
        shapes = [(tokens, columns)]
        out_specs = [tiled(columns)]
    depth = sum(p.shape[0] for p in pieces)
    flops = 2 * tokens * columns * (depth + 2 * mid_columns) + 2 * tokens * mid_columns * features
    results = pl.pallas_call(
        functools.partial(products_kernel, count, partial is not None, finish, blocks, total_tokens),
        out_shape=[jax.ShapeDtypeStruct(shape, jnp.float32) for shape in shapes],
        grid_spec=pltpu.PrefetchScalarGridSpec(
            num_scalar_prefetch=1, grid=(steps,), in_specs=in_specs, out_specs=out_specs
        ),
        compiler_params=pltpu.CompilerParams(vmem_limit_bytes=VMEM_BYTES),
        cost_estimate=pl.CostEstimate(
            flops=flops, bytes_accessed=2 * (tokens * features + depth * columns), transcendentals=0
        ),
    )(starts, *operands)
    return results if finish else results[0]


def local(tokens, dense_weight, left_factor, right_factor):
    tok_rows, features = tokens.shape
    weight_rows, columns = dense_weight.shape
    dp_count = lax.axis_size("dp")
    tensor_count = lax.axis_size("tensor")
    dp_pos = lax.axis_index("dp")
    tensor_pos = lax.axis_index("tensor")
    in_size = left_factor.shape[0]
    mids = right_factor.shape[0]
    blocks = left_factor.shape[1] * tensor_count // mids
    own_blocks = blocks // tensor_count
    out_size = columns // own_blocks
    total_tokens = tok_rows * dp_count

    bits = dp_count.bit_length() - 1
    strides = [1 << b for b in range(bits)]
    grouped = max(bits - 3, 0)
    pair = strides[grouped:][len(strides[grouped:]) // 2]
    others = [s for s in reversed(strides[grouped:]) if s != pair]
    pair_bit = (dp_pos // pair) % 2
    unit_rows = weight_rows << grouped

    half_blocks = own_blocks // 2
    chunks = 2 if half_blocks % 2 == 0 else 1
    chunk_blocks = half_blocks // chunks
    chunk_columns = chunk_blocks * out_size
    half_columns = half_blocks * out_size

    def weight_piece(half, chunk):
        start = half * half_columns + chunk * chunk_columns
        return lax.dynamic_slice_in_dim(dense_weight, start, chunk_columns, 1)

    held = [{} for _ in range(chunks)]
    theirs = []
    for chunk in range(chunks):
        held[chunk][0] = ordered(weight_piece(pair_bit, chunk), "dp", strides[:grouped])
        theirs.append(ordered(weight_piece(1 - pair_bit, chunk), "dp", strides[:grouped]))
    far, near = others
    far_lane, near_lane, pair_lane = Lane(2), Lane(2), Lane(1)

    def send(lane, stride, chunk, mask):
        held[chunk][mask ^ stride] = lane.swap(held[chunk][mask], "dp", stride)

    share = tok_rows // tensor_count
    late = max(16, (share // 4 + 8) // 16 * 16)
    token_parts = [(0, share - late), (share - late, late)]

    def fetch_tokens(which):
        begin, size = token_parts[which]
        part = lax.dynamic_slice_in_dim(tokens, tensor_pos * share + begin, size, 0)
        part = pair_lane.swap(part, "dp", pair)
        stride = tensor_count // 2
        while stride:
            part = jnp.concatenate([part, swap(part, "tensor", stride)], 0)
            stride //= 2
        return part

    last = chunks - 1
    held[0][pair] = pair_lane.swap(theirs[0], "dp", pair)
    send(far_lane, far, 0, 0)
    for chunk in range(chunks):
        send(near_lane, near, chunk, 0)
    send(far_lane, far, 0, pair)
    send(near_lane, near, 0, pair)
    send(near_lane, near, 0, far)
    early_rows = fetch_tokens(0)
    if last:
        held[last][pair] = pair_lane.swap(theirs[last], "dp", pair)
        send(far_lane, far, last, 0)
        send(far_lane, far, last, pair)
    send(near_lane, near, 0, far ^ pair)
    late_rows = fetch_tokens(1)
    if last:
        send(near_lane, near, last, pair)
        send(near_lane, near, last, far)
        send(near_lane, near, last, far ^ pair)

    left_blocks = left_factor.reshape(in_size, mids // tensor_count, blocks)
    left_blocks = lax.all_to_all(left_blocks, "tensor", split_axis=2, concat_axis=1, tiled=True)
    left_blocks = lax.dynamic_slice_in_dim(left_blocks, pair_bit * half_blocks, half_blocks, 2)
    eye_left = jnp.eye(mids, dtype=jnp.bfloat16)
    left_rows = left_blocks.transpose(1, 0, 2)
    left_diag = (left_rows[:, :, :, None] * eye_left[:, None, None, :]).reshape(features, half_blocks * mids)
    right_half = lax.dynamic_slice_in_dim(right_factor, pair_bit * half_columns, half_columns, 1)

    row_block = jnp.arange(chunk_blocks * mids) // mids
    column_block = jnp.arange(chunk_columns) // out_size
    same_block = row_block[:, None] == column_block[None, :]

    token_sets = (tokens, early_rows, late_rows)
    mixes = [
        jnp.dot(rows, left_diag, preferred_element_type=jnp.float32).astype(jnp.bfloat16) for rows in token_sets
    ]
    late_masks = (far ^ pair, far ^ pair ^ near)
    order = sorted(held[0], key=lambda mask: mask in late_masks)

    loss_part = jnp.zeros((), jnp.float32)
    right_parts, left_parts = [], []
    for chunk in range(chunks):
        right_chunk = right_half[:, chunk * chunk_columns : (chunk + 1) * chunk_columns]
        right_diag = jnp.where(same_block, jnp.tile(right_chunk, (chunk_blocks, 1)), jnp.bfloat16(0))
        sums = None
        for which, (rows, mix) in enumerate(zip(token_sets, mixes)):
            mix_chunk = mix[:, chunk * chunk_blocks * mids : (chunk + 1) * chunk_blocks * mids]
            pieces = [held[chunk][mask] for mask in order]
            starts = jnp.stack([(dp_pos ^ mask) >> grouped for mask in order]).astype(jnp.int32)
            call = functools.partial(products, rows, mix_chunk, right_diag, blocks=chunk_blocks, total_tokens=total_tokens)
            if which < 2 and chunk == last:
                cut = len(order) - 2
                partial = call(pieces=pieces[:cut], starts=starts[:cut], finish=False)
                terms = call(pieces=pieces[cut:], starts=starts[cut:], partial=partial)
            else:
                terms = call(pieces=pieces, starts=starts)
            sums = terms if sums is None else [a + b for a, b in zip(sums, terms)]
        right_parts.append(sums[0])
        left_parts.append(sums[1])
        loss_part = loss_part + jnp.sum(sums[2])

    left_sum = jnp.concatenate(left_parts, 0).reshape(half_blocks, mids, in_size).transpose(2, 0, 1)
    both = jnp.concatenate([*right_parts, left_sum.reshape(in_size, half_blocks * mids)], 1)
    width = both.shape[1]
    both = both.reshape((2,) * bits + (both.shape[0] // dp_count, width))
    order = [s for s in reversed(strides)]
    for stride in [near, far] + strides[:grouped]:
        at = order.index(stride)
        bit = (dp_pos // stride) % 2
        away = lax.dynamic_index_in_dim(both, 1 - bit, at, keepdims=False)
        kept = lax.dynamic_index_in_dim(both, bit, at, keepdims=False)
        both = kept + swap(away, "dp", stride)
        order.remove(stride)

    squares = both * both
    scalars = jnp.stack([jnp.sum(squares[..., half_columns:]), jnp.sum(squares[..., :half_columns]), loss_part])
    devices = dp_count * tensor_count
    scalars = jnp.broadcast_to(scalars[None], (devices, 3))
    sq_left, sq_right, loss_all = jnp.sum(lax.all_to_all(scalars, ("dp", "tensor"), 0, 0, tiled=True), 0)

    away = lax.dynamic_index_in_dim(both, 1 - pair_bit, 0, keepdims=False)
    kept = lax.dynamic_index_in_dim(both, pair_bit, 0, keepdims=False)
    other = swap(away, "dp", pair)
    low = jnp.where(pair_bit == 0, kept, other)
    high = jnp.where(pair_bit == 0, other, kept)
    right_rows = jnp.concatenate([low[:, :half_columns], high[:, :half_columns]], 1)
    left_low = low[:, half_columns:].reshape(-1, half_blocks, mids)
    left_high = high[:, half_columns:].reshape(-1, half_blocks, mids)
    left_rows = jnp.concatenate([left_low, left_high], 1)
    left_rows = lax.all_to_all(left_rows, "tensor", split_axis=2, concat_axis=1, tiled=True)
    left_rows = left_rows.transpose(0, 2, 1).reshape(left_rows.shape[0], -1)
    dir_left = left_rows * lax.rsqrt(sq_left / (features * blocks) + epsilon)
    dir_right = right_rows * lax.rsqrt(sq_right / (mids * columns * tensor_count) + epsilon)
    loss = loss_all / (2.0 * total_tokens)
    return (dir_left, dir_right, loss)


def solution(mesh):
    in_specs = (P("dp", None), P("dp", "tensor"), P(None, "tensor"), P(None, "tensor"))
    out_specs = (P("dp", "tensor"), P("dp", "tensor"), P())
    return jax.shard_map(local, mesh=mesh, in_specs=in_specs, out_specs=out_specs, check_vma=False)
```

```python
import functools

import jax
import jax.numpy as jnp
from jax import lax
from jax.experimental import pallas as pl
from jax.experimental.pallas import tpu as pltpu
from jax.sharding import PartitionSpec as P

epsilon = 1e-06
VMEM_BYTES = 56 * 1024 * 1024


def swap(value, axis, stride):
    size = lax.axis_size(axis)
    return lax.ppermute(value, axis, [(a, a ^ stride) for a in range(size)])


def after(value, results):
    return lax.optimization_barrier((value, *results))[0] if results else value


def ordered(value, axis, strides):
    position = lax.axis_index(axis)
    for stride in strides:
        other = swap(value, axis, stride)
        high = (position // stride) % 2 == 1
        value = jnp.concatenate([jnp.where(high, other, value), jnp.where(high, value, other)], 0)
    return value


def contract(a, b, a_dim, b_dim):
    return lax.dot_general(a, b, (((a_dim,), (b_dim,)), ((), ())), preferred_element_type=jnp.float32)


AHEAD = 3


def products_kernel(count, resume, finish, blocks, scale, starts_ref, mix_ref, right_ref, rows_hbm, *refs):
    pieces = refs[:count]
    refs = refs[count:]
    if resume:
        partial_hbm, refs = refs[0], refs[1:]
    if finish:
        right_out, left_out, loss_out, total, rows_buf, piece_buf, sems = refs
    else:
        total, rows_buf, piece_buf, sems = refs
    slots, _, depth = rows_buf.shape

    def start_of(slot):
        return pl.multiple_of(starts_ref[slot] * depth, depth)

    def copies(slot):
        found = [pltpu.make_async_copy(rows_hbm.at[:, pl.ds(start_of(slot), depth)], rows_buf.at[slot], sems.at[2 * slot])]
        if slot < count:
            found.append(pltpu.make_async_copy(pieces[slot], piece_buf.at[slot], sems.at[2 * slot + 1]))
        return found

    def begin(slot):
        if slot < slots:
            for copy in copies(slot):
                copy.start()

    def await_slot(slot):
        for copy in copies(slot):
            copy.wait()

    if resume:
        fetch = pltpu.make_async_copy(partial_hbm, total, sems.at[2 * slots])
        fetch.start()
    for slot in range(AHEAD):
        begin(slot)
    if resume:
        fetch.wait()
    else:
        total[...] = contract(mix_ref[...], right_ref[...], 1, 0)
    for slot in range(count):
        begin(slot + AHEAD)
        await_slot(slot)
        total[...] -= contract(rows_buf[slot], piece_buf[slot], 1, 0)
    if not finish:
        return

    columns = right_ref.shape[1]
    mids = right_ref.shape[0] // blocks
    in_size = left_out.shape[1] // mids
    residual = total[...]
    loss_out[...] = jnp.sum(residual * residual, axis=0, keepdims=True)
    slope = (residual * scale).astype(jnp.bfloat16)
    full_right = contract(mix_ref[...], slope, 0, 0)
    column_block = lax.broadcasted_iota(jnp.int32, (1, columns), 1) // (columns // blocks)
    grad_right = full_right[:mids]
    for b in range(1, blocks):
        grad_right = jnp.where(column_block == b, full_right[b * mids : (b + 1) * mids], grad_right)
    right_out[...] = grad_right
    back_mix = contract(slope, right_ref[...], 1, 1).T.astype(jnp.bfloat16)
    mid = lax.broadcasted_iota(jnp.int32, (mids, 1), 0)
    lane = lax.broadcasted_iota(jnp.int32, (1, depth), 1)
    for slot in range(slots):
        if slot >= count:
            begin(slot + AHEAD)
            await_slot(slot)
        full_left = contract(back_mix, rows_buf[slot], 1, 0)
        same = mid == (lane + start_of(slot)) // in_size
        sums = [
            jnp.sum(jnp.where(same, full_left[b * mids : (b + 1) * mids], 0.0), axis=0, keepdims=True)
            for b in range(blocks)
        ]
        left_out[:, pl.ds(start_of(slot), depth)] = jnp.concatenate(sums, 0)


def products(rows, mix, right_diag, pieces, starts, blocks, scale, partial=None, finish=True):
    count = len(pieces)
    tokens, features = rows.shape
    mid_columns, columns = right_diag.shape
    depth = pieces[0].shape[0]
    slots = starts.shape[0]
    vmem = pl.BlockSpec(memory_space=pltpu.VMEM)
    far_away = pl.BlockSpec(memory_space=pl.ANY)
    operands = [starts, mix, right_diag, rows, *pieces]
    if partial is not None:
        operands.append(partial)
    in_specs = [pl.BlockSpec(memory_space=pltpu.SMEM), vmem, vmem] + [far_away] * (len(operands) - 3)
    scratch = [
        pltpu.VMEM((slots, tokens, depth), jnp.bfloat16),
        pltpu.VMEM((count, depth, columns), jnp.bfloat16),
        pltpu.SemaphoreType.DMA((2 * slots + 1,)),
    ]
    flops = 2 * tokens * columns * depth * count
    if finish:
        shapes = [(mid_columns // blocks, columns), (blocks, features), (1, columns)]
        scratch = [pltpu.VMEM((tokens, columns), jnp.float32)] + scratch
        flops += 4 * tokens * columns * mid_columns + 2 * tokens * mid_columns * features
    else:
        shapes = [(tokens, columns)]
    results = pl.pallas_call(
        functools.partial(products_kernel, count, partial is not None, finish, blocks, scale),
        out_shape=[jax.ShapeDtypeStruct(shape, jnp.float32) for shape in shapes],
        in_specs=in_specs,
        out_specs=[vmem] * len(shapes),
        scratch_shapes=scratch,
        compiler_params=pltpu.CompilerParams(vmem_limit_bytes=VMEM_BYTES),
        cost_estimate=pl.CostEstimate(
            flops=flops, bytes_accessed=2 * depth * (tokens * slots + columns * count), transcendentals=0
        ),
    )(*operands)
    return results if finish else results[0]


def local(tokens, dense_weight, left_factor, right_factor):
    tok_rows, features = tokens.shape
    weight_rows, columns = dense_weight.shape
    dp_count = lax.axis_size("dp")
    tensor_count = lax.axis_size("tensor")
    dp_pos = lax.axis_index("dp")
    tensor_pos = lax.axis_index("tensor")
    in_size = left_factor.shape[0]
    mids = right_factor.shape[0]
    blocks = left_factor.shape[1] * tensor_count // mids
    own_blocks = blocks // tensor_count
    out_size = columns // own_blocks
    total_tokens = tok_rows * dp_count

    bits = dp_count.bit_length() - 1
    strides = [1 << b for b in range(bits)]
    grouped = max(bits - 3, 0)
    pair = strides[grouped:][len(strides[grouped:]) // 2]
    others = [s for s in reversed(strides[grouped:]) if s != pair]
    pair_bit = (dp_pos // pair) % 2
    unit_rows = weight_rows << grouped

    half_blocks = own_blocks // 2
    chunks = 2 if half_blocks % 2 == 0 else 1
    chunk_blocks = half_blocks // chunks
    chunk_columns = chunk_blocks * out_size
    half_columns = half_blocks * out_size

    def weight_piece(half, chunk):
        start = half * half_columns + chunk * chunk_columns
        return lax.dynamic_slice_in_dim(dense_weight, start, chunk_columns, 1)

    held = [{} for _ in range(chunks)]
    theirs = []
    for chunk in range(chunks):
        held[chunk][0] = ordered(weight_piece(pair_bit, chunk), "dp", strides[:grouped])
        theirs.append(ordered(weight_piece(1 - pair_bit, chunk), "dp", strides[:grouped]))
    far, near = others

    def send(chunk, mask, stride, waits=()):
        held[chunk][mask ^ stride] = swap(after(held[chunk][mask], waits), "dp", stride)
        return held[chunk][mask ^ stride]

    def send_pair(chunk, waits=()):
        held[chunk][pair] = swap(after(theirs[chunk], waits), "dp", pair)
        return held[chunk][pair]

    share = tok_rows // tensor_count
    first_cut = share * 7 // 15 // 16 * 16
    cuts = [0, first_cut, first_cut + (share - first_cut) // 2 // 16 * 16, share]

    def fetch_tokens(which, waits=()):
        begin, size = cuts[which], cuts[which + 1] - cuts[which]
        part = lax.dynamic_slice_in_dim(tokens, tensor_pos * share + begin, size, 0)
        return swap(after(part, waits), "dp", pair)

    def share_tokens(part):
        stride = tensor_count // 2
        while stride:
            part = jnp.concatenate([part, swap(part, "tensor", stride)], 0)
            stride //= 2
        return part

    last = chunks - 1
    parts = [None] * 3
    done = [send(0, 0, far), send_pair(0), send(0, 0, near)]
    if last:
        done.append(send(last, 0, near))
    done = [send(0, pair, far, done), send(0, pair, near, done), send(0, far, near, done)] + (
        [send_pair(last, done)] if last else []
    )
    parts[0] = fetch_tokens(0, done)
    done = [parts[0], send(0, far ^ pair, near, done)] + (
        [send(last, 0, far, done), send(last, pair, near, done)] if last else []
    )
    early_done = done

    left_blocks = left_factor.reshape(in_size, mids // tensor_count, blocks)
    left_blocks = lax.all_to_all(left_blocks, "tensor", split_axis=2, concat_axis=1, tiled=True)
    left_blocks = lax.dynamic_slice_in_dim(left_blocks, pair_bit * half_blocks, half_blocks, 2)
    eye_left = jnp.eye(mids, dtype=jnp.bfloat16)
    left_rows = left_blocks.transpose(1, 0, 2)
    left_diag = (left_rows[:, :, :, None] * eye_left[:, None, None, :]).reshape(features, half_blocks * mids)
    right_half = lax.dynamic_slice_in_dim(right_factor, pair_bit * half_columns, half_columns, 1)

    row_block = jnp.arange(chunk_blocks * mids) // mids
    column_block = jnp.arange(chunk_columns) // out_size
    same_block = row_block[:, None] == column_block[None, :]

    token_sets = [tokens]
    order = [0, near, pair, far, far ^ near, pair ^ near, far ^ pair, far ^ pair ^ near]
    starts = jnp.stack([(dp_pos ^ mask) >> grouped for mask in order]).astype(jnp.int32)
    right_diags = []
    for chunk in range(chunks):
        right_chunk = right_half[:, chunk * chunk_columns : (chunk + 1) * chunk_columns]
        right_diags.append(jnp.where(same_block, jnp.tile(right_chunk, (chunk_blocks, 1)), jnp.bfloat16(0)))
    mixes = {}
    partials = {}
    sums = [None] * chunks
    previous = None

    def run(which, chunk, begin=0, end=len(order), waits=()):
        nonlocal previous
        rows = token_sets[which]
        if which not in mixes:
            mixes[which] = jnp.dot(rows, left_diag, preferred_element_type=jnp.float32).astype(jnp.bfloat16)
        mix = mixes[which][:, chunk * chunk_blocks * mids : (chunk + 1) * chunk_blocks * mids]
        mix = after(mix, [*waits, *([] if previous is None else [previous])])
        pieces = [held[chunk][mask] for mask in order[begin:end]]
        finish = end == len(order)
        places = jnp.concatenate([starts[begin:], starts[:begin]]) if finish else starts[begin:end]
        terms = products(
            rows, mix, right_diags[chunk], pieces, places, chunk_blocks, 1.0 / total_tokens,
            partial=partials[which, chunk] if begin else None, finish=finish,
        )
        if not finish:
            previous = partials[which, chunk] = terms
            return
        previous = terms[2]
        sums[chunk] = terms if sums[chunk] is None else [a + b for a, b in zip(sums[chunk], terms)]

    if last:
        run(0, 0, 0, 6)
        parts[1] = fetch_tokens(1, [previous, *early_done])
        send(last, pair, far, early_done)
        send(last, far, near, early_done)
        parts[2] = fetch_tokens(2, [parts[1]])
        token_sets += [share_tokens(parts[0]), share_tokens(parts[1])]
        run(0, 0, 6, waits=[parts[1]])
        run(0, last, 0, 4)
        run(1, 0)
        send(last, far ^ pair, near, [previous])
        token_sets.append(share_tokens(after(parts[2], [previous])))
        run(1, last, 0, 6)
        run(2, 0)
        run(2, last, 0, 6)
        run(0, last, 4)
        run(1, last, 6)
        run(2, last, 6)
        run(3, 0)
        run(3, last)
    else:
        token_sets += [share_tokens(fetch_tokens(which, early_done)) for which in range(3)]
        for which in range(4):
            run(which, 0)
    loss_part = sum(jnp.sum(terms[2]) for terms in sums)
    right_parts = [terms[0] for terms in sums]
    left_parts = [terms[1] for terms in sums]

    left_sum = jnp.concatenate(left_parts, 0).reshape(half_blocks, mids, in_size).transpose(2, 0, 1)
    both = jnp.concatenate([*right_parts, left_sum.reshape(in_size, half_blocks * mids)], 1)
    width = both.shape[1]
    both = both.reshape((2,) * bits + (both.shape[0] // dp_count, width))
    order = [s for s in reversed(strides)]
    for stride in [near, far] + strides[:grouped]:
        at = order.index(stride)
        bit = (dp_pos // stride) % 2
        away = lax.dynamic_index_in_dim(both, 1 - bit, at, keepdims=False)
        kept = lax.dynamic_index_in_dim(both, bit, at, keepdims=False)
        both = kept + swap(away, "dp", stride)
        order.remove(stride)

    squares = both * both
    scalars = jnp.stack([jnp.sum(squares[..., half_columns:]), jnp.sum(squares[..., :half_columns]), loss_part])
    devices = dp_count * tensor_count
    scalars = jnp.broadcast_to(scalars[None], (devices, 3))
    sq_left, sq_right, loss_all = jnp.sum(lax.all_to_all(scalars, ("dp", "tensor"), 0, 0, tiled=True), 0)

    right_both = both[..., :half_columns]
    away = lax.dynamic_index_in_dim(right_both, 1 - pair_bit, 0, keepdims=False)
    kept = lax.dynamic_index_in_dim(right_both, pair_bit, 0, keepdims=False)
    other = swap(away, "dp", pair)
    right_rows = jnp.concatenate([jnp.where(pair_bit == 0, kept, other), jnp.where(pair_bit == 0, other, kept)], 1)

    left_both = both[..., half_columns:].reshape(2, -1, half_blocks, tensor_count, mids // tensor_count)
    left_both = left_both.transpose(0, 3, 1, 4, 2)
    groups = []
    for base in range(dp_count):
        if not base & pair:
            groups.append([d * tensor_count + t for d in (base, base | pair) for t in range(tensor_count)])
    left_both = left_both.reshape((2 * tensor_count,) + left_both.shape[2:])
    left_both = lax.all_to_all(left_both, ("dp", "tensor"), 0, 0, axis_index_groups=groups, tiled=True)
    left_both = left_both.reshape((2, tensor_count) + left_both.shape[1:])
    left_rows = left_both.transpose(2, 3, 1, 0, 4)
    left_rows = left_rows.reshape(left_rows.shape[0], -1)
    dir_left = left_rows * lax.rsqrt(sq_left / (features * blocks) + epsilon)
    dir_right = right_rows * lax.rsqrt(sq_right / (mids * columns * tensor_count) + epsilon)
    loss = loss_all / (2.0 * total_tokens)
    return (dir_left, dir_right, loss)


def solution(mesh):
    in_specs = (P("dp", None), P("dp", "tensor"), P(None, "tensor"), P(None, "tensor"))
    out_specs = (P("dp", "tensor"), P("dp", "tensor"), P())
    return jax.shard_map(local, mesh=mesh, in_specs=in_specs, out_specs=out_specs, check_vma=False)
```

```python
import functools

import jax
import jax.numpy as jnp
from jax import lax
from jax.experimental import pallas as pl
from jax.experimental.pallas import tpu as pltpu
from jax.sharding import PartitionSpec as P

epsilon = 1e-06
VMEM_BYTES = 56 * 1024 * 1024


def swap(value, axis, stride):
    size = lax.axis_size(axis)
    return lax.ppermute(value, axis, [(a, a ^ stride) for a in range(size)])


def after(value, results):
    return lax.optimization_barrier((value, *results))[0] if results else value


def ordered(value, axis, strides):
    position = lax.axis_index(axis)
    for stride in strides:
        other = swap(value, axis, stride)
        high = (position // stride) % 2 == 1
        value = jnp.concatenate([jnp.where(high, other, value), jnp.where(high, value, other)], 0)
    return value


def contract(a, b, a_dim, b_dim):
    return lax.dot_general(a, b, (((a_dim,), (b_dim,)), ((), ())), preferred_element_type=jnp.float32)


AHEAD = 4


def row_tile(tokens):
    return max(tile for tile in range(16, 257, 16) if tokens % tile == 0)


def groups_of(count):
    cuts = [0, min(2, count)]
    while cuts[-1] < count:
        cuts.append(min(cuts[-1] + 3, count))
    return list(zip(cuts[:-1], cuts[1:]))


def products_kernel(parts, resume, finish, blocks, scale, starts_ref, mix_ref, right_ref, rows_hbm, *refs):
    count = len(parts)
    pieces, refs = refs[: sum(parts)], refs[sum(parts) :]
    if resume:
        partial_hbm, refs = refs[0], refs[1:]
    if finish:
        right_out, left_out, loss_out, total, rows_buf, piece_buf, sems, slope_buf, back_buf, turned_buf = refs
    else:
        total, rows_buf, piece_buf, sems = refs
    tokens = rows_buf.shape[0]
    depth = piece_buf.shape[0] // count
    slots = rows_buf.shape[1] // depth
    tile = row_tile(tokens)

    def start_of(slot):
        return pl.multiple_of(starts_ref[slot] * depth, depth)

    def copies(slot):
        source = rows_hbm.at[:, pl.ds(start_of(slot), depth)]
        found = [pltpu.make_async_copy(source, rows_buf.at[:, pl.ds(slot * depth, depth)], sems.at[slot])]
        if slot < count:
            first, size = sum(parts[:slot]), depth // parts[slot]
            for part in range(parts[slot]):
                target = piece_buf.at[pl.ds(slot * depth + part * size, size)]
                found.append(pltpu.make_async_copy(pieces[first + part], target, sems.at[slots + 1 + first + part]))
        return found

    def begin(slots_now):
        for slot in slots_now:
            if slot < slots:
                for copy in copies(slot):
                    copy.start()

    def await_slots(slots_now):
        for slot in slots_now:
            for copy in copies(slot):
                copy.wait()

    if resume:
        fetch = pltpu.make_async_copy(partial_hbm, total, sems.at[slots])
        fetch.start()
    begun = AHEAD
    begin(range(begun))
    if resume:
        fetch.wait()
    for low, high in groups_of(count):
        begin(range(begun, high + AHEAD))
        begun = max(begun, high + AHEAD)
        await_slots(range(low, high))
        here = slice(low * depth, high * depth)

        @pl.loop(0, tokens // tile)
        def _(step):
            at = pl.ds(pl.multiple_of(step * tile, tile), tile)
            term = contract(rows_buf[at, here], piece_buf[here], 1, 0)
            if low or resume:
                total[at] = total[at] - term
            else:
                total[at] = contract(mix_ref[at], right_ref[...], 1, 0) - term

    if not finish:
        return

    columns = right_ref.shape[1]
    mids = right_ref.shape[0] // blocks
    in_size = left_out.shape[1] // mids
    loss_out[...] = jnp.zeros_like(loss_out)
    begin(range(begun, slots))

    @pl.loop(0, tokens // tile)
    def _(step):
        at = pl.ds(pl.multiple_of(step * tile, tile), tile)
        residual = total[at]
        loss_out[...] += jnp.sum(residual * residual, axis=0, keepdims=True)
        slope = (residual * scale).astype(jnp.bfloat16)
        slope_buf[at] = slope
        back_buf[at] = contract(slope, right_ref[...], 1, 1)

    full_right = contract(mix_ref[...], slope_buf[...], 0, 0)
    column_block = lax.broadcasted_iota(jnp.int32, (1, columns), 1) // (columns // blocks)
    grad_right = full_right[:mids]
    for b in range(1, blocks):
        grad_right = jnp.where(column_block == b, full_right[b * mids : (b + 1) * mids], grad_right)
    right_out[...] = grad_right
    turned_buf[...] = back_buf[...].T.astype(jnp.bfloat16)
    await_slots(range(count, slots))
    mid = lax.broadcasted_iota(jnp.int32, (mids, 1), 0)
    lane = lax.broadcasted_iota(jnp.int32, (1, depth), 1)

    @pl.loop(0, slots)
    def _(slot):
        full_left = contract(turned_buf[...], rows_buf[:, pl.ds(pl.multiple_of(slot * depth, depth), depth)], 1, 0)
        same = mid == (lane + start_of(slot)) // in_size
        sums = [
            jnp.sum(jnp.where(same, full_left[b * mids : (b + 1) * mids], 0.0), axis=0, keepdims=True)
            for b in range(blocks)
        ]
        left_out[:, pl.ds(start_of(slot), depth)] = jnp.concatenate(sums, 0)


def products(rows, mix, right_diag, pieces, starts, blocks, scale, partial=None, finish=True):
    count = len(pieces)
    parts = tuple(len(piece) for piece in pieces)
    tokens, features = rows.shape
    mid_columns, columns = right_diag.shape
    depth = sum(part.shape[0] for part in pieces[0])
    slots = starts.shape[0]
    vmem = pl.BlockSpec(memory_space=pltpu.VMEM)
    far_away = pl.BlockSpec(memory_space=pl.ANY)
    operands = [starts, mix, right_diag, rows, *[part for piece in pieces for part in piece]]
    if partial is not None:
        operands.append(partial)
    in_specs = [pl.BlockSpec(memory_space=pltpu.SMEM), vmem, vmem] + [far_away] * (len(operands) - 3)
    scratch = [
        pltpu.VMEM((tokens, slots * depth), jnp.bfloat16),
        pltpu.VMEM((count * depth, columns), jnp.bfloat16),
        pltpu.SemaphoreType.DMA((slots + 1 + sum(parts),)),
    ]
    flops = 2 * tokens * columns * depth * count
    if finish:
        shapes = [(mid_columns // blocks, columns), (blocks, features), (1, columns)]
        scratch = [pltpu.VMEM((tokens, columns), jnp.float32)] + scratch
        scratch += [
            pltpu.VMEM((tokens, columns), jnp.bfloat16),
            pltpu.VMEM((tokens, mid_columns), jnp.float32),
            pltpu.VMEM((mid_columns, tokens), jnp.bfloat16),
        ]
        flops += 4 * tokens * columns * mid_columns + 2 * tokens * mid_columns * features
    else:
        shapes = [(tokens, columns)]
    results = pl.pallas_call(
        functools.partial(products_kernel, parts, partial is not None, finish, blocks, scale),
        out_shape=[jax.ShapeDtypeStruct(shape, jnp.float32) for shape in shapes],
        in_specs=in_specs,
        out_specs=[vmem] * len(shapes),
        scratch_shapes=scratch,
        compiler_params=pltpu.CompilerParams(vmem_limit_bytes=VMEM_BYTES),
        cost_estimate=pl.CostEstimate(
            flops=flops, bytes_accessed=2 * depth * (tokens * slots + columns * count), transcendentals=0
        ),
    )(*operands)
    return results if finish else results[0]


def local(tokens, dense_weight, left_factor, right_factor):
    tok_rows, features = tokens.shape
    weight_rows, columns = dense_weight.shape
    dp_count = lax.axis_size("dp")
    tensor_count = lax.axis_size("tensor")
    dp_pos = lax.axis_index("dp")
    tensor_pos = lax.axis_index("tensor")
    in_size = left_factor.shape[0]
    mids = right_factor.shape[0]
    blocks = left_factor.shape[1] * tensor_count // mids
    own_blocks = blocks // tensor_count
    out_size = columns // own_blocks
    total_tokens = tok_rows * dp_count

    bits = dp_count.bit_length() - 1
    strides = [1 << b for b in range(bits)]
    grouped = max(bits - 3, 0)
    pair = strides[grouped:][len(strides[grouped:]) // 2]
    others = [s for s in reversed(strides[grouped:]) if s != pair]
    pair_bit = (dp_pos // pair) % 2
    unit_rows = weight_rows << grouped

    half_blocks = own_blocks // 2
    chunks = 2 if half_blocks % 2 == 0 else 1
    chunk_blocks = half_blocks // chunks
    chunk_columns = chunk_blocks * out_size
    half_columns = half_blocks * out_size

    def weight_piece(half, chunk):
        start = half * half_columns + chunk * chunk_columns
        return lax.dynamic_slice_in_dim(dense_weight, start, chunk_columns, 1)

    held = [{} for _ in range(chunks)]
    theirs = []
    for chunk in range(chunks):
        held[chunk][0] = ordered(weight_piece(pair_bit, chunk), "dp", strides[:grouped])
        theirs.append(ordered(weight_piece(1 - pair_bit, chunk), "dp", strides[:grouped]))
    far, near = others

    def send(chunk, mask, stride, waits=()):
        held[chunk][mask ^ stride] = swap(after(held[chunk][mask], waits), "dp", stride)
        return held[chunk][mask ^ stride]

    def send_pair(chunk, waits=()):
        held[chunk][pair] = swap(after(theirs[chunk], waits), "dp", pair)
        return held[chunk][pair]

    share = tok_rows // tensor_count
    first_cut = share * 7 // 15 // 16 * 16
    cuts = [0, first_cut, first_cut + (share - first_cut) // 2 // 16 * 16, share]

    def fetch_tokens(which, waits=()):
        begin, size = cuts[which], cuts[which + 1] - cuts[which]
        part = lax.dynamic_slice_in_dim(tokens, tensor_pos * share + begin, size, 0)
        return swap(after(part, waits), "dp", pair)

    def share_tokens(part):
        stride = tensor_count // 2
        while stride:
            part = jnp.concatenate([part, swap(part, "tensor", stride)], 0)
            stride //= 2
        return part

    last = chunks - 1
    parts = [None] * 3
    done = [send(0, 0, far), send_pair(0), send(0, 0, near)]
    if last:
        done.append(send(last, 0, near))
    first_done = done
    done = [send(0, pair, far, done), send(0, pair, near, done), send(0, far, near, done)] + (
        [send_pair(last, done)] if last else []
    )
    parts[0] = fetch_tokens(0, done)
    done = [parts[0], send(0, far ^ pair, near, done)] + (
        [send(last, 0, far, done), send(last, pair, near, done)] if last else []
    )
    early_done = done

    left_blocks = after(left_factor, first_done).reshape(in_size, mids // tensor_count, blocks)
    left_blocks = lax.all_to_all(left_blocks, "tensor", split_axis=2, concat_axis=1, tiled=True)
    left_blocks = lax.dynamic_slice_in_dim(left_blocks, pair_bit * half_blocks, half_blocks, 2)
    eye_left = jnp.eye(mids, dtype=jnp.bfloat16)
    left_rows = left_blocks.transpose(1, 0, 2)
    left_diag = (left_rows[:, :, :, None] * eye_left[:, None, None, :]).reshape(features, half_blocks * mids)
    right_half = lax.dynamic_slice_in_dim(right_factor, pair_bit * half_columns, half_columns, 1)

    row_block = jnp.arange(chunk_blocks * mids) // mids
    column_block = jnp.arange(chunk_columns) // out_size
    same_block = row_block[:, None] == column_block[None, :]

    token_sets = [tokens]
    order = [0, near, pair, far, far ^ near, pair ^ near, far ^ pair, far ^ pair ^ near]
    starts = jnp.stack([(dp_pos ^ mask) >> grouped for mask in order]).astype(jnp.int32)
    right_diags = []
    for chunk in range(chunks):
        right_chunk = right_half[:, chunk * chunk_columns : (chunk + 1) * chunk_columns]
        right_diags.append(jnp.where(same_block, jnp.tile(right_chunk, (chunk_blocks, 1)), jnp.bfloat16(0)))
    mixes = {}
    partials = {}
    sums = [None] * chunks
    previous = None

    def run(which, chunk, begin=0, end=len(order), waits=()):
        nonlocal previous
        rows = token_sets[which]
        if which not in mixes:
            mixes[which] = jnp.dot(rows, left_diag, preferred_element_type=jnp.float32).astype(jnp.bfloat16)
        mix = mixes[which][:, chunk * chunk_blocks * mids : (chunk + 1) * chunk_blocks * mids]
        mix = after(mix, [*waits, *([] if previous is None else [previous])])
        pieces = [halves.get((chunk, mask), [held[chunk].get(mask)]) for mask in order[begin:end]]
        finish = end == len(order)
        places = jnp.concatenate([starts[begin:], starts[:begin]]) if finish else starts[begin:end]
        terms = products(
            rows, mix, right_diags[chunk], pieces, places, chunk_blocks, 1.0 / total_tokens,
            partial=partials[which, chunk] if begin else None, finish=finish,
        )
        if not finish:
            previous = partials[which, chunk] = terms
            return
        previous = terms[2]
        sums[chunk] = terms if sums[chunk] is None else [a + b for a, b in zip(sums[chunk], terms)]

    halves = {}
    if last:
        run(0, 0, 0, 6)
        parts[1] = fetch_tokens(1, [previous, *early_done])
        source = held[last][pair]
        cut = unit_rows // 2
        upper = swap(after(source[:cut], early_done), "dp", far)
        done = [send(last, far, near, early_done), upper]
        token_sets += [share_tokens(parts[0])]
        parts[2] = fetch_tokens(2, [parts[1]])
        lower = swap(after(source[cut:], done), "dp", far)
        upper_near = swap(after(upper, done), "dp", near)
        run(0, 0, 6, waits=[parts[1]])
        token_sets += [share_tokens(parts[1])]
        run(0, last, 0, 4)
        run(1, 0)
        lower_near = swap(after(lower, [upper_near, previous]), "dp", near)
        halves[last, far ^ pair] = [upper, lower]
        halves[last, far ^ pair ^ near] = [upper_near, lower_near]
        token_sets.append(share_tokens(after(parts[2], [previous])))
        run(1, last, 0, 6)
        run(2, 0)
        run(2, last, 0, 6)
        run(0, last, 4)
        run(1, last, 6)
        run(2, last, 6)
        run(3, 0)
        run(3, last)
    else:
        token_sets += [share_tokens(fetch_tokens(which, early_done)) for which in range(3)]
        for which in range(4):
            run(which, 0)
    loss_part = sum(jnp.sum(terms[2]) for terms in sums)
    right_parts = [terms[0] for terms in sums]
    left_parts = [terms[1] for terms in sums]

    left_sum = jnp.concatenate(left_parts, 0).reshape(half_blocks, mids, in_size).transpose(2, 0, 1)
    both = jnp.concatenate([*right_parts, left_sum.reshape(in_size, half_blocks * mids)], 1)
    width = both.shape[1]
    both = both.reshape((2,) * bits + (both.shape[0] // dp_count, width))
    order = [s for s in reversed(strides)]
    for stride in [near, far] + strides[:grouped]:
        at = order.index(stride)
        bit = (dp_pos // stride) % 2
        away = lax.dynamic_index_in_dim(both, 1 - bit, at, keepdims=False)
        kept = lax.dynamic_index_in_dim(both, bit, at, keepdims=False)
        both = kept + swap(away, "dp", stride)
        order.remove(stride)

    squares = both * both
    scalars = jnp.stack([jnp.sum(squares[..., half_columns:]), jnp.sum(squares[..., :half_columns]), loss_part])
    devices = dp_count * tensor_count
    scalars = jnp.broadcast_to(scalars[None], (devices, 3))
    sq_left, sq_right, loss_all = jnp.sum(lax.all_to_all(scalars, ("dp", "tensor"), 0, 0, tiled=True), 0)

    right_both = both[..., :half_columns]
    away = lax.dynamic_index_in_dim(right_both, 1 - pair_bit, 0, keepdims=False)
    kept = lax.dynamic_index_in_dim(right_both, pair_bit, 0, keepdims=False)
    other = swap(away, "dp", pair)
    right_rows = jnp.concatenate([jnp.where(pair_bit == 0, kept, other), jnp.where(pair_bit == 0, other, kept)], 1)

    left_both = both[..., half_columns:].reshape(2, -1, half_blocks, tensor_count, mids // tensor_count)
    left_both = left_both.transpose(0, 3, 1, 4, 2)
    groups = []
    for base in range(dp_count):
        if not base & pair:
            groups.append([d * tensor_count + t for d in (base, base | pair) for t in range(tensor_count)])
    left_both = left_both.reshape((2 * tensor_count,) + left_both.shape[2:])
    left_both = lax.all_to_all(left_both, ("dp", "tensor"), 0, 0, axis_index_groups=groups, tiled=True)
    left_both = left_both.reshape((2, tensor_count) + left_both.shape[1:])
    left_rows = left_both.transpose(2, 3, 1, 0, 4)
    left_rows = left_rows.reshape(left_rows.shape[0], -1)
    dir_left = left_rows * lax.rsqrt(sq_left / (features * blocks) + epsilon)
    dir_right = right_rows * lax.rsqrt(sq_right / (mids * columns * tensor_count) + epsilon)
    loss = loss_all / (2.0 * total_tokens)
    return (dir_left, dir_right, loss)


def solution(mesh):
    in_specs = (P("dp", None), P("dp", "tensor"), P(None, "tensor"), P(None, "tensor"))
    out_specs = (P("dp", "tensor"), P("dp", "tensor"), P())
    return jax.shard_map(local, mesh=mesh, in_specs=in_specs, out_specs=out_specs, check_vma=False)
```

```python
import functools

import jax
import jax.numpy as jnp
from jax import lax
from jax.experimental import pallas as pl
from jax.experimental.pallas import tpu as pltpu
from jax.sharding import PartitionSpec as P

epsilon = 1e-06
VMEM_BYTES = 56 * 1024 * 1024


def swap(value, axis, stride):
    size = lax.axis_size(axis)
    return lax.ppermute(value, axis, [(a, a ^ stride) for a in range(size)])


def after(value, results):
    return lax.optimization_barrier((value, *results))[0] if results else value


def ordered(value, axis, strides):
    position = lax.axis_index(axis)
    for stride in strides:
        other = swap(value, axis, stride)
        high = (position // stride) % 2 == 1
        value = jnp.concatenate([jnp.where(high, other, value), jnp.where(high, value, other)], 0)
    return value


def contract(a, b, a_dim, b_dim):
    return lax.dot_general(a, b, (((a_dim,), (b_dim,)), ((), ())), preferred_element_type=jnp.float32)


AHEAD = 4


def row_tile(rows):
    return max(tile for tile in range(16, 513, 16) if rows % tile == 0)


def groups_of(low, high):
    cuts = [low, min(low + 2, high)] if low < high else [low]
    while cuts[-1] < high:
        cuts.append(min(cuts[-1] + 3, high))
    return list(zip(cuts[:-1], cuts[1:]))


def products_kernel(spans, parts, resumed, finish, blocks, scale, starts_ref, right_ref, *refs):
    count = len(parts)
    sets, refs = refs[: len(spans)], refs[len(spans) :]
    mixes, refs = refs[: len(spans)], refs[len(spans) :]
    pieces, refs = refs[: sum(parts)], refs[sum(parts) :]
    if resumed:
        partial_hbm, refs = refs[0], refs[1:]
    if finish:
        right_out, left_out, loss_out, total, rows_buf, mix_buf, piece_buf, sems, slope_buf, back_buf, turned_buf = refs
    else:
        total, rows_buf, mix_buf, piece_buf, sems = refs
    tokens = rows_buf.shape[0]
    depth = piece_buf.shape[0] // count
    slots = rows_buf.shape[1] // depth
    offsets = [sum(spans[:which]) for which in range(len(spans))]
    early = count - 2 if resumed else 0

    def start_of(slot):
        return pl.multiple_of(starts_ref[slot] * depth, depth)

    def copies(slot):
        found = []
        for which, span in enumerate(spans):
            target = rows_buf.at[pl.ds(offsets[which], span), pl.ds(slot * depth, depth)]
            source = sets[which].at[:, pl.ds(start_of(slot), depth)]
            found.append(pltpu.make_async_copy(source, target, sems.at[slot * len(spans) + which]))
        if slot < count:
            first, size = sum(parts[:slot]), depth // parts[slot]
            for part in range(parts[slot]):
                target = piece_buf.at[pl.ds(slot * depth + part * size, size)]
                sem = sems.at[(slots + 1) * len(spans) + 1 + first + part]
                found.append(pltpu.make_async_copy(pieces[first + part], target, sem))
        return found

    def begin(slots_now):
        for slot in slots_now:
            if slot < slots:
                for copy in copies(slot):
                    copy.start()

    def await_slots(slots_now):
        for slot in slots_now:
            for copy in copies(slot):
                copy.wait()

    def each_tile(low, high, body):
        if low < high:
            tile = row_tile(high - low)

            @pl.loop(0, (high - low) // tile)
            def _(step):
                body(pl.ds(pl.multiple_of(low + step * tile, 16), tile))

    first = [
        pltpu.make_async_copy(mixes[which], mix_buf.at[pl.ds(offsets[which], span)], sems.at[slots * len(spans) + which])
        for which, span in enumerate(spans)
    ]
    if resumed:
        sem = sems.at[(slots + 1) * len(spans)]
        first.append(pltpu.make_async_copy(partial_hbm, total.at[pl.ds(0, resumed)], sem))
    for copy in first:
        copy.start()
    begun = AHEAD
    begin(range(begun))
    for copy in first:
        copy.wait()
    for low, high in groups_of(0, early) + groups_of(early, count):
        begin(range(begun, high + AHEAD))
        begun = max(begun, high + AHEAD)
        await_slots(range(low, high))
        here = slice(low * depth, high * depth)

        def start_rows(at):
            term = contract(rows_buf[at, here], piece_buf[here], 1, 0)
            total[at] = contract(mix_buf[at], right_ref[...], 1, 0) - term

        def go_on(at):
            total[at] = total[at] - contract(rows_buf[at, here], piece_buf[here], 1, 0)

        if low < early:
            each_tile(resumed, tokens, go_on if low else start_rows)
        elif low:
            each_tile(0, resumed, go_on)
            each_tile(resumed, tokens, go_on)
        else:
            each_tile(0, tokens, start_rows)
    if not finish:
        return

    columns = right_ref.shape[1]
    mids = right_ref.shape[0] // blocks
    in_size = left_out.shape[1] // mids
    loss_out[...] = jnp.zeros_like(loss_out)
    begin(range(begun, slots))

    def slopes(at):
        residual = total[at]
        loss_out[...] += jnp.sum(residual * residual, axis=0, keepdims=True)
        slope = (residual * scale).astype(jnp.bfloat16)
        slope_buf[at] = slope
        back_buf[at] = contract(slope, right_ref[...], 1, 1)

    each_tile(0, tokens, slopes)
    full_right = contract(mix_buf[...], slope_buf[...], 0, 0)
    column_block = lax.broadcasted_iota(jnp.int32, (1, columns), 1) // (columns // blocks)
    grad_right = full_right[:mids]
    for b in range(1, blocks):
        grad_right = jnp.where(column_block == b, full_right[b * mids : (b + 1) * mids], grad_right)
    right_out[...] = grad_right
    turned_buf[...] = back_buf[...].T.astype(jnp.bfloat16)
    await_slots(range(count, slots))
    mid = lax.broadcasted_iota(jnp.int32, (mids, 1), 0)
    lane = lax.broadcasted_iota(jnp.int32, (1, depth), 1)

    @pl.loop(0, slots)
    def _(slot):
        full_left = contract(turned_buf[...], rows_buf[:, pl.ds(pl.multiple_of(slot * depth, depth), depth)], 1, 0)
        same = mid == (lane + start_of(slot)) // in_size
        sums = [
            jnp.sum(jnp.where(same, full_left[b * mids : (b + 1) * mids], 0.0), axis=0, keepdims=True)
            for b in range(blocks)
        ]
        left_out[:, pl.ds(start_of(slot), depth)] = jnp.concatenate(sums, 0)


def products(sets, mixes, right_diag, pieces, starts, blocks, scale, partial=None, finish=True):
    count = len(pieces)
    parts = tuple(len(piece) for piece in pieces)
    spans = tuple(rows.shape[0] for rows in sets)
    tokens, features = sum(spans), sets[0].shape[1]
    mid_columns, columns = right_diag.shape
    depth = sum(part.shape[0] for part in pieces[0])
    slots = starts.shape[0]
    resumed = 0 if partial is None else partial.shape[0]
    vmem = pl.BlockSpec(memory_space=pltpu.VMEM)
    operands = [starts, right_diag, *sets, *mixes, *[part for piece in pieces for part in piece]]
    if partial is not None:
        operands.append(partial)
    in_specs = [pl.BlockSpec(memory_space=pltpu.SMEM), vmem]
    in_specs += [pl.BlockSpec(memory_space=pl.ANY)] * (len(operands) - 2)
    scratch = [
        pltpu.VMEM((tokens, slots * depth), jnp.bfloat16),
        pltpu.VMEM((tokens, mid_columns), jnp.bfloat16),
        pltpu.VMEM((count * depth, columns), jnp.bfloat16),
        pltpu.SemaphoreType.DMA(((slots + 1) * len(spans) + 1 + sum(parts),)),
    ]
    flops = 2 * columns * depth * (tokens * count - resumed * (count - 2))
    if finish:
        shapes = [(mid_columns // blocks, columns), (blocks, features), (1, columns)]
        scratch = [pltpu.VMEM((tokens, columns), jnp.float32)] + scratch
        scratch += [
            pltpu.VMEM((tokens, columns), jnp.bfloat16),
            pltpu.VMEM((tokens, mid_columns), jnp.float32),
            pltpu.VMEM((mid_columns, tokens), jnp.bfloat16),
        ]
        flops += 4 * tokens * columns * mid_columns + 2 * tokens * mid_columns * features
    else:
        shapes = [(tokens, columns)]
    results = pl.pallas_call(
        functools.partial(products_kernel, spans, parts, resumed, finish, blocks, scale),
        out_shape=[jax.ShapeDtypeStruct(shape, jnp.float32) for shape in shapes],
        in_specs=in_specs,
        out_specs=[vmem] * len(shapes),
        scratch_shapes=scratch,
        compiler_params=pltpu.CompilerParams(vmem_limit_bytes=VMEM_BYTES),
        cost_estimate=pl.CostEstimate(
            flops=flops, bytes_accessed=2 * depth * (tokens * slots + columns * count), transcendentals=0
        ),
    )(*operands)
    return results if finish else results[0]


def local(tokens, dense_weight, left_factor, right_factor):
    tok_rows, features = tokens.shape
    weight_rows, columns = dense_weight.shape
    dp_count = lax.axis_size("dp")
    tensor_count = lax.axis_size("tensor")
    dp_pos = lax.axis_index("dp")
    tensor_pos = lax.axis_index("tensor")
    in_size = left_factor.shape[0]
    mids = right_factor.shape[0]
    blocks = left_factor.shape[1] * tensor_count // mids
    own_blocks = blocks // tensor_count
    out_size = columns // own_blocks
    total_tokens = tok_rows * dp_count

    bits = dp_count.bit_length() - 1
    strides = [1 << b for b in range(bits)]
    grouped = max(bits - 3, 0)
    pair = strides[grouped:][len(strides[grouped:]) // 2]
    others = [s for s in reversed(strides[grouped:]) if s != pair]
    pair_bit = (dp_pos // pair) % 2
    unit_rows = weight_rows << grouped

    half_blocks = own_blocks // 2
    chunks = 2 if half_blocks % 2 == 0 else 1
    chunk_blocks = half_blocks // chunks
    chunk_columns = chunk_blocks * out_size
    half_columns = half_blocks * out_size

    def weight_piece(half, chunk):
        start = half * half_columns + chunk * chunk_columns
        return lax.dynamic_slice_in_dim(dense_weight, start, chunk_columns, 1)

    held = [{} for _ in range(chunks)]
    theirs = []
    for chunk in range(chunks):
        held[chunk][0] = ordered(weight_piece(pair_bit, chunk), "dp", strides[:grouped])
        theirs.append(ordered(weight_piece(1 - pair_bit, chunk), "dp", strides[:grouped]))
    far, near = others

    def send(chunk, mask, stride, waits=()):
        held[chunk][mask ^ stride] = swap(after(held[chunk][mask], waits), "dp", stride)
        return held[chunk][mask ^ stride]

    def send_pair(chunk, waits=()):
        held[chunk][pair] = swap(after(theirs[chunk], waits), "dp", pair)
        return held[chunk][pair]

    share = tok_rows // tensor_count
    first_cut = share * 7 // 15 // 16 * 16
    cuts = [0, first_cut, share]

    def fetch_tokens(which, waits=()):
        begin, size = cuts[which], cuts[which + 1] - cuts[which]
        part = lax.dynamic_slice_in_dim(tokens, tensor_pos * share + begin, size, 0)
        return swap(after(part, waits), "dp", pair)

    def share_tokens(part, waits=((), ())):
        stride, stage = tensor_count // 2, 0
        while stride:
            moved = swap(after(part, waits[min(stage, 1)]), "tensor", stride)
            part = jnp.concatenate([part, moved], 0)
            stride, stage = stride // 2, stage + 1
        return part

    last = chunks - 1
    parts = [None] * 2
    done = [send(0, 0, far), send_pair(0), send(0, 0, near)]
    if last:
        done.append(send(last, 0, near))
    first_done = done
    done = [send(0, pair, far, done), send(0, pair, near, done), send(0, far, near, done)] + (
        [send_pair(last, done)] if last else []
    )
    parts[0] = fetch_tokens(0, done)
    whole_first = send(0, far ^ pair, near, done)
    done = [parts[0], whole_first] + (
        [send(last, 0, far, done), send(last, pair, near, [whole_first])] if last else []
    )
    early_done = done

    left_blocks = after(left_factor, first_done).reshape(in_size, mids // tensor_count, blocks)
    left_blocks = lax.all_to_all(left_blocks, "tensor", split_axis=2, concat_axis=1, tiled=True)
    left_blocks = lax.dynamic_slice_in_dim(left_blocks, pair_bit * half_blocks, half_blocks, 2)
    eye_left = jnp.eye(mids, dtype=jnp.bfloat16)
    left_rows = left_blocks.transpose(1, 0, 2)
    left_diag = (left_rows[:, :, :, None] * eye_left[:, None, None, :]).reshape(features, half_blocks * mids)
    right_half = lax.dynamic_slice_in_dim(right_factor, pair_bit * half_columns, half_columns, 1)

    row_block = jnp.arange(chunk_blocks * mids) // mids
    column_block = jnp.arange(chunk_columns) // out_size
    same_block = row_block[:, None] == column_block[None, :]

    token_sets = [tokens]
    order = [0, near, pair, far, far ^ near, pair ^ near, far ^ pair, far ^ pair ^ near]
    starts = jnp.stack([(dp_pos ^ mask) >> grouped for mask in order]).astype(jnp.int32)
    right_diags = []
    for chunk in range(chunks):
        right_chunk = right_half[:, chunk * chunk_columns : (chunk + 1) * chunk_columns]
        right_diags.append(jnp.where(same_block, jnp.tile(right_chunk, (chunk_blocks, 1)), jnp.bfloat16(0)))
    mixes = {}
    sums = [[] for _ in range(chunks)]
    halves = {}
    previous = None

    def run(which, chunk, end=len(order), partial=None, waits=()):
        nonlocal previous
        for item in which:
            if item not in mixes:
                mixes[item] = jnp.dot(token_sets[item], left_diag, preferred_element_type=jnp.float32).astype(jnp.bfloat16)
        waits = [*waits, *([] if previous is None else [previous])]
        mine = [mixes[item][:, chunk * chunk_blocks * mids : (chunk + 1) * chunk_blocks * mids] for item in which]
        mine[0] = after(mine[0], waits)
        pieces = [halves.get((chunk, mask), [held[chunk].get(mask)]) for mask in order[:end]]
        finish = end == len(order)
        terms = products(
            [token_sets[item] for item in which], mine, right_diags[chunk], pieces, starts[:end], chunk_blocks,
            1.0 / total_tokens, partial=partial, finish=finish,
        )
        if not finish:
            previous = terms
            return terms
        previous = terms[2]
        sums[chunk].append(terms)

    if last:
        run([0], 0)
        parts[1] = fetch_tokens(1, early_done)
        source, cut = held[last][pair], unit_rows // 2
        upper = swap(after(source[:cut], early_done), "dp", far)
        send(last, far, near, early_done)
        token_sets.append(share_tokens(parts[0], ([previous], [])))
        run([1], 0, waits=[upper])
        lower = swap(after(source[cut:], [upper, previous]), "dp", far)
        upper_near = swap(after(upper, [previous]), "dp", near)
        partial = run([0, 1], last, end=6)
        lower_near = swap(lower, "dp", near)
        halves[last, far ^ pair] = [upper, lower]
        halves[last, far ^ pair ^ near] = [upper_near, lower_near]
        token_sets.append(share_tokens(parts[1], ([partial, lower, upper_near], [lower_near])))
        run([2], 0)
        run([0, 1, 2], last, partial=partial)
    else:
        token_sets += [share_tokens(fetch_tokens(which, early_done)) for which in range(2)]
        run(range(3), 0)

    loss_part = 0.0
    summed = []
    for terms in sums:
        right_sum, left_sum = sum(term[0] for term in terms), sum(term[1] for term in terms)
        loss_part = loss_part + sum(jnp.sum(term[2]) for term in terms)
        left_sum = left_sum.reshape(chunk_blocks, mids, in_size).transpose(2, 0, 1).reshape(in_size, chunk_blocks * mids)
        both = jnp.concatenate([right_sum, left_sum], 1)
        both = both.reshape((2,) * bits + (both.shape[0] // dp_count, both.shape[1]))
        places = [s for s in reversed(strides)]
        for stride in [near, far] + strides[:grouped]:
            at = places.index(stride)
            bit = (dp_pos // stride) % 2
            away = lax.dynamic_index_in_dim(both, 1 - bit, at, keepdims=False)
            kept = lax.dynamic_index_in_dim(both, bit, at, keepdims=False)
            both = kept + swap(away, "dp", stride)
            places.remove(stride)
        summed.append(both)
    right_both = jnp.concatenate([both[..., :chunk_columns] for both in summed], -1)
    left_both = jnp.concatenate([both[..., chunk_columns:] for both in summed], -1)

    scalars = jnp.stack(
        [
            sum(jnp.sum(jnp.square(both[..., chunk_columns:])) for both in summed),
            sum(jnp.sum(jnp.square(both[..., :chunk_columns])) for both in summed),
            loss_part,
        ]
    )
    devices = dp_count * tensor_count
    scalars = jnp.broadcast_to(scalars[None], (devices, 3))
    sq_left, sq_right, loss_all = jnp.sum(lax.all_to_all(scalars, ("dp", "tensor"), 0, 0, tiled=True), 0)

    away = lax.dynamic_index_in_dim(right_both, 1 - pair_bit, 0, keepdims=False)
    kept = lax.dynamic_index_in_dim(right_both, pair_bit, 0, keepdims=False)
    other = swap(away, "dp", pair)
    right_rows = jnp.concatenate([jnp.where(pair_bit == 0, kept, other), jnp.where(pair_bit == 0, other, kept)], 1)

    left_both = left_both.reshape(2, -1, half_blocks, tensor_count, mids // tensor_count)
    left_both = left_both.transpose(0, 3, 1, 4, 2)
    groups = []
    for base in range(dp_count):
        if not base & pair:
            groups.append([d * tensor_count + t for d in (base, base | pair) for t in range(tensor_count)])
    left_both = left_both.reshape((2 * tensor_count,) + left_both.shape[2:])
    left_both = lax.all_to_all(left_both, ("dp", "tensor"), 0, 0, axis_index_groups=groups, tiled=True)
    left_both = left_both.reshape((2, tensor_count) + left_both.shape[1:])
    left_rows = left_both.transpose(2, 3, 1, 0, 4)
    left_rows = left_rows.reshape(left_rows.shape[0], -1)
    dir_left = left_rows * lax.rsqrt(sq_left / (features * blocks) + epsilon)
    dir_right = right_rows * lax.rsqrt(sq_right / (mids * columns * tensor_count) + epsilon)
    loss = loss_all / (2.0 * total_tokens)
    return (dir_left, dir_right, loss)


def solution(mesh):
    in_specs = (P("dp", None), P("dp", "tensor"), P(None, "tensor"), P(None, "tensor"))
    out_specs = (P("dp", "tensor"), P("dp", "tensor"), P())
    return jax.shard_map(local, mesh=mesh, in_specs=in_specs, out_specs=out_specs, check_vma=False)
```

```python
import functools

import jax
import jax.numpy as jnp
from jax import lax
from jax.experimental import pallas as pl
from jax.experimental.pallas import tpu as pltpu
from jax.sharding import PartitionSpec as P

epsilon = 1e-06
VMEM_BYTES = 56 * 1024 * 1024


def swap(value, axis, stride):
    size = lax.axis_size(axis)
    return lax.ppermute(value, axis, [(a, a ^ stride) for a in range(size)])


def after(value, results):
    return lax.optimization_barrier((value, *results))[0] if results else value


def ordered(value, axis, strides):
    position = lax.axis_index(axis)
    for stride in strides:
        other = swap(value, axis, stride)
        high = (position // stride) % 2 == 1
        value = jnp.concatenate([jnp.where(high, other, value), jnp.where(high, value, other)], 0)
    return value


def contract(a, b, a_dim, b_dim):
    return lax.dot_general(a, b, (((a_dim,), (b_dim,)), ((), ())), preferred_element_type=jnp.float32)


AHEAD = 4


def row_tile(rows):
    return max(tile for tile in range(16, 513, 16) if rows % tile == 0)


def groups_of(low, high):
    cuts = [low, min(low + 2, high)] if low < high else [low]
    while cuts[-1] < high:
        cuts.append(min(cuts[-1] + 3, high))
    return list(zip(cuts[:-1], cuts[1:]))


def products_kernel(spans, parts, resumed, finish, blocks, scale, starts_ref, right_ref, *refs):
    count = len(parts)
    sets, refs = refs[: len(spans)], refs[len(spans) :]
    mixes, refs = refs[: len(spans)], refs[len(spans) :]
    pieces, refs = refs[: sum(parts)], refs[sum(parts) :]
    if resumed:
        partial_hbm, refs = refs[0], refs[1:]
    if finish:
        right_out, left_out, loss_out, total, rows_buf, mix_buf, piece_buf, sems, slope_buf, back_buf, turned_buf = refs
    else:
        total, rows_buf, mix_buf, piece_buf, sems = refs
    tokens = rows_buf.shape[0]
    depth = piece_buf.shape[0] // count
    slots = rows_buf.shape[1] // depth
    offsets = [sum(spans[:which]) for which in range(len(spans))]
    early = count - 2 if resumed else 0

    def start_of(slot):
        return pl.multiple_of(starts_ref[slot] * depth, depth)

    def copies(slot):
        found = []
        for which, span in enumerate(spans):
            target = rows_buf.at[pl.ds(offsets[which], span), pl.ds(slot * depth, depth)]
            source = sets[which].at[:, pl.ds(start_of(slot), depth)]
            found.append(pltpu.make_async_copy(source, target, sems.at[slot * len(spans) + which]))
        if slot < count:
            first, size = sum(parts[:slot]), depth // parts[slot]
            for part in range(parts[slot]):
                target = piece_buf.at[pl.ds(slot * depth + part * size, size)]
                sem = sems.at[(slots + 1) * len(spans) + 1 + first + part]
                found.append(pltpu.make_async_copy(pieces[first + part], target, sem))
        return found

    def begin(slots_now):
        for slot in slots_now:
            if slot < slots:
                for copy in copies(slot):
                    copy.start()

    def await_slots(slots_now):
        for slot in slots_now:
            for copy in copies(slot):
                copy.wait()

    def each_tile(low, high, body):
        if low < high:
            tile = row_tile(high - low)

            @pl.loop(0, (high - low) // tile)
            def _(step):
                body(pl.ds(pl.multiple_of(low + step * tile, 16), tile))

    first = [
        pltpu.make_async_copy(mixes[which], mix_buf.at[pl.ds(offsets[which], span)], sems.at[slots * len(spans) + which])
        for which, span in enumerate(spans)
    ]
    if resumed:
        sem = sems.at[(slots + 1) * len(spans)]
        first.append(pltpu.make_async_copy(partial_hbm, total.at[pl.ds(0, resumed)], sem))
    for copy in first:
        copy.start()
    begun = AHEAD
    begin(range(begun))
    for copy in first:
        copy.wait()
    for low, high in groups_of(0, early) + groups_of(early, count):
        begin(range(begun, high + AHEAD))
        begun = max(begun, high + AHEAD)
        await_slots(range(low, high))
        here = slice(low * depth, high * depth)

        def start_rows(at):
            term = contract(rows_buf[at, here], piece_buf[here], 1, 0)
            total[at] = contract(mix_buf[at], right_ref[...], 1, 0) - term

        def go_on(at):
            total[at] = total[at] - contract(rows_buf[at, here], piece_buf[here], 1, 0)

        if low < early:
            each_tile(resumed, tokens, go_on if low else start_rows)
        elif low:
            each_tile(0, resumed, go_on)
            each_tile(resumed, tokens, go_on)
        else:
            each_tile(0, tokens, start_rows)
    if not finish:
        return

    columns = right_ref.shape[1]
    mids = right_ref.shape[0] // blocks
    in_size = left_out.shape[1] // mids
    loss_out[...] = jnp.zeros_like(loss_out)
    begin(range(begun, slots))

    def slopes(at):
        residual = total[at]
        loss_out[...] += jnp.sum(residual * residual, axis=0, keepdims=True)
        slope = (residual * scale).astype(jnp.bfloat16)
        slope_buf[at] = slope
        back_buf[at] = contract(slope, right_ref[...], 1, 1)

    each_tile(0, tokens, slopes)
    full_right = contract(mix_buf[...], slope_buf[...], 0, 0)
    column_block = lax.broadcasted_iota(jnp.int32, (1, columns), 1) // (columns // blocks)
    grad_right = full_right[:mids]
    for b in range(1, blocks):
        grad_right = jnp.where(column_block == b, full_right[b * mids : (b + 1) * mids], grad_right)
    right_out[...] = grad_right
    turned_buf[...] = back_buf[...].T.astype(jnp.bfloat16)
    await_slots(range(count, slots))
    mid = lax.broadcasted_iota(jnp.int32, (mids, 1), 0)
    lane = lax.broadcasted_iota(jnp.int32, (1, depth), 1)

    @pl.loop(0, slots)
    def _(slot):
        full_left = contract(turned_buf[...], rows_buf[:, pl.ds(pl.multiple_of(slot * depth, depth), depth)], 1, 0)
        same = mid == (lane + start_of(slot)) // in_size
        sums = [
            jnp.sum(jnp.where(same, full_left[b * mids : (b + 1) * mids], 0.0), axis=0, keepdims=True)
            for b in range(blocks)
        ]
        left_out[:, pl.ds(start_of(slot), depth)] = jnp.concatenate(sums, 0)


def products(sets, mixes, right_diag, pieces, starts, blocks, scale, partial=None, finish=True):
    count = len(pieces)
    parts = tuple(len(piece) for piece in pieces)
    spans = tuple(rows.shape[0] for rows in sets)
    tokens, features = sum(spans), sets[0].shape[1]
    mid_columns, columns = right_diag.shape
    depth = sum(part.shape[0] for part in pieces[0])
    slots = starts.shape[0]
    resumed = 0 if partial is None else partial.shape[0]
    vmem = pl.BlockSpec(memory_space=pltpu.VMEM)
    operands = [starts, right_diag, *sets, *mixes, *[part for piece in pieces for part in piece]]
    if partial is not None:
        operands.append(partial)
    in_specs = [pl.BlockSpec(memory_space=pltpu.SMEM), vmem]
    in_specs += [pl.BlockSpec(memory_space=pl.ANY)] * (len(operands) - 2)
    scratch = [
        pltpu.VMEM((tokens, slots * depth), jnp.bfloat16),
        pltpu.VMEM((tokens, mid_columns), jnp.bfloat16),
        pltpu.VMEM((count * depth, columns), jnp.bfloat16),
        pltpu.SemaphoreType.DMA(((slots + 1) * len(spans) + 1 + sum(parts),)),
    ]
    flops = 2 * columns * depth * (tokens * count - resumed * (count - 2))
    if finish:
        shapes = [(mid_columns // blocks, columns), (blocks, features), (1, columns)]
        scratch = [pltpu.VMEM((tokens, columns), jnp.float32)] + scratch
        scratch += [
            pltpu.VMEM((tokens, columns), jnp.bfloat16),
            pltpu.VMEM((tokens, mid_columns), jnp.float32),
            pltpu.VMEM((mid_columns, tokens), jnp.bfloat16),
        ]
        flops += 4 * tokens * columns * mid_columns + 2 * tokens * mid_columns * features
    else:
        shapes = [(tokens, columns)]
    results = pl.pallas_call(
        functools.partial(products_kernel, spans, parts, resumed, finish, blocks, scale),
        out_shape=[jax.ShapeDtypeStruct(shape, jnp.float32) for shape in shapes],
        in_specs=in_specs,
        out_specs=[vmem] * len(shapes),
        scratch_shapes=scratch,
        compiler_params=pltpu.CompilerParams(vmem_limit_bytes=VMEM_BYTES),
        cost_estimate=pl.CostEstimate(
            flops=flops, bytes_accessed=2 * depth * (tokens * slots + columns * count), transcendentals=0
        ),
    )(*operands)
    return results if finish else results[0]


def local(tokens, dense_weight, left_factor, right_factor):
    tok_rows, features = tokens.shape
    weight_rows, columns = dense_weight.shape
    dp_count = lax.axis_size("dp")
    tensor_count = lax.axis_size("tensor")
    dp_pos = lax.axis_index("dp")
    tensor_pos = lax.axis_index("tensor")
    in_size = left_factor.shape[0]
    mids = right_factor.shape[0]
    blocks = left_factor.shape[1] * tensor_count // mids
    own_blocks = blocks // tensor_count
    out_size = columns // own_blocks
    total_tokens = tok_rows * dp_count

    bits = dp_count.bit_length() - 1
    strides = [1 << b for b in range(bits)]
    grouped = max(bits - 3, 0)
    pair = strides[grouped:][len(strides[grouped:]) // 2]
    others = [s for s in reversed(strides[grouped:]) if s != pair]
    pair_bit = (dp_pos // pair) % 2
    unit_rows = weight_rows << grouped

    half_blocks = own_blocks // 2
    chunks = 2 if half_blocks % 2 == 0 else 1
    chunk_blocks = half_blocks // chunks
    chunk_columns = chunk_blocks * out_size
    half_columns = half_blocks * out_size

    def weight_piece(half, chunk):
        start = half * half_columns + chunk * chunk_columns
        return lax.dynamic_slice_in_dim(dense_weight, start, chunk_columns, 1)

    held = [{} for _ in range(chunks)]
    theirs = []
    for chunk in range(chunks):
        held[chunk][0] = ordered(weight_piece(pair_bit, chunk), "dp", strides[:grouped])
        theirs.append(ordered(weight_piece(1 - pair_bit, chunk), "dp", strides[:grouped]))
    far, near = others

    def send(chunk, mask, stride, waits=()):
        held[chunk][mask ^ stride] = swap(after(held[chunk][mask], waits), "dp", stride)
        return held[chunk][mask ^ stride]

    def send_pair(chunk, waits=()):
        held[chunk][pair] = swap(after(theirs[chunk], waits), "dp", pair)
        return held[chunk][pair]

    share = tok_rows // tensor_count
    first_cut = share * 7 // 15 // 16 * 16
    cuts = [0, first_cut, share]

    def fetch_tokens(which, waits=()):
        begin, size = cuts[which], cuts[which + 1] - cuts[which]
        part = lax.dynamic_slice_in_dim(tokens, tensor_pos * share + begin, size, 0)
        return swap(after(part, waits), "dp", pair)

    def share_tokens(part, waits=()):
        first = None
        stride = tensor_count // 2
        while stride:
            part = jnp.concatenate([part, swap(part if first is None else after(part, waits), "tensor", stride)], 0)
            first = part if first is None else first
            stride //= 2
        return part, first

    last = chunks - 1
    parts = [None] * 2
    done = [send(0, 0, far), send_pair(0), send(0, 0, near)]
    if last:
        done.append(send(last, 0, near))
    first_done = done
    done = [send(0, pair, far, done), send(0, pair, near, done), send(0, far, near, done)] + (
        [send_pair(last, done)] if last else []
    )
    second_done = done

    left_blocks = after(left_factor, first_done).reshape(in_size, mids // tensor_count, blocks)
    left_blocks = lax.all_to_all(left_blocks, "tensor", split_axis=2, concat_axis=1, tiled=True)
    left_blocks = lax.dynamic_slice_in_dim(left_blocks, pair_bit * half_blocks, half_blocks, 2)
    eye_left = jnp.eye(mids, dtype=jnp.bfloat16)
    left_rows = left_blocks.transpose(1, 0, 2)
    left_diag = (left_rows[:, :, :, None] * eye_left[:, None, None, :]).reshape(features, half_blocks * mids)
    right_half = lax.dynamic_slice_in_dim(right_factor, pair_bit * half_columns, half_columns, 1)

    done = [*second_done, left_diag]
    parts[0] = fetch_tokens(0, done)
    done = [parts[0], send(0, far ^ pair, near, done)] + (
        [send(last, 0, far, done), send(last, pair, near, done)] if last else []
    )
    early_done = done

    row_block = jnp.arange(chunk_blocks * mids) // mids
    column_block = jnp.arange(chunk_columns) // out_size
    same_block = row_block[:, None] == column_block[None, :]

    token_sets = [tokens]
    order = [0, near, pair, far, far ^ near, pair ^ near, far ^ pair, far ^ pair ^ near]
    starts = jnp.stack([(dp_pos ^ mask) >> grouped for mask in order]).astype(jnp.int32)
    right_diags = []
    for chunk in range(chunks):
        right_chunk = right_half[:, chunk * chunk_columns : (chunk + 1) * chunk_columns]
        right_diags.append(jnp.where(same_block, jnp.tile(right_chunk, (chunk_blocks, 1)), jnp.bfloat16(0)))
    mixes = {}
    sums = [[] for _ in range(chunks)]
    previous = None

    def run(which, chunk, end=len(order), partial=None, waits=()):
        nonlocal previous
        for item in which:
            if item not in mixes:
                mixes[item] = jnp.dot(token_sets[item], left_diag, preferred_element_type=jnp.float32).astype(jnp.bfloat16)
        waits = [*waits, *([] if previous is None else [previous])]
        mine = [mixes[item][:, chunk * chunk_blocks * mids : (chunk + 1) * chunk_blocks * mids] for item in which]
        mine[0] = after(mine[0], waits)
        pieces = [[held[chunk][mask]] for mask in order[:end]]
        finish = end == len(order)
        terms = products(
            [token_sets[item] for item in which], mine, right_diags[chunk], pieces, starts[:end], chunk_blocks,
            1.0 / total_tokens, partial=partial, finish=finish,
        )
        if not finish:
            previous = terms
            return terms
        previous = terms[2]
        sums[chunk].append(terms)

    if last:
        early_rows, early_half = share_tokens(parts[0])
        mixes[0] = jnp.dot(tokens, left_diag, preferred_element_type=jnp.float32).astype(jnp.bfloat16)
        early_done = [*early_done, mixes[0]]
        parts[1] = fetch_tokens(1, early_done)
        third_done = [parts[1], send(last, pair, far, early_done), send(last, far, near, early_done)]
        token_sets.append(early_rows)
        run([0], 0)
        third_done.append(previous)
        run([1], 0)
        third_done.append(previous)
        fourth_done = [send(last, far ^ pair, near, third_done)]
        partial = run([0, 1], last, end=6)
        token_sets.append(share_tokens(after(parts[1], third_done), [partial, *fourth_done])[0])
        run([0, 1], last, partial=partial)
        run([2], 0)
        run([2], last)
    else:
        token_sets += [share_tokens(fetch_tokens(which, early_done))[0] for which in range(2)]
        run(range(3), 0)

    loss_part = 0.0
    summed = []
    for terms in sums:
        right_sum, left_sum = sum(term[0] for term in terms), sum(term[1] for term in terms)
        loss_part = loss_part + sum(jnp.sum(term[2]) for term in terms)
        left_sum = left_sum.reshape(chunk_blocks, mids, in_size).transpose(2, 0, 1).reshape(in_size, chunk_blocks * mids)
        both = jnp.concatenate([right_sum, left_sum], 1)
        both = both.reshape((2,) * bits + (both.shape[0] // dp_count, both.shape[1]))
        places = [s for s in reversed(strides)]
        for stride in [near, far] + strides[:grouped]:
            at = places.index(stride)
            bit = (dp_pos // stride) % 2
            away = lax.dynamic_index_in_dim(both, 1 - bit, at, keepdims=False)
            kept = lax.dynamic_index_in_dim(both, bit, at, keepdims=False)
            both = kept + swap(away, "dp", stride)
            places.remove(stride)
        summed.append(both)
    right_both = jnp.concatenate([both[..., :chunk_columns] for both in summed], -1)
    left_both = jnp.concatenate([both[..., chunk_columns:] for both in summed], -1)

    scalars = jnp.stack(
        [
            sum(jnp.sum(jnp.square(both[..., chunk_columns:])) for both in summed),
            sum(jnp.sum(jnp.square(both[..., :chunk_columns])) for both in summed),
            loss_part,
        ]
    )
    devices = dp_count * tensor_count
    scalars = jnp.broadcast_to(scalars[None], (devices, 3))
    sq_left, sq_right, loss_all = jnp.sum(lax.all_to_all(scalars, ("dp", "tensor"), 0, 0, tiled=True), 0)

    away = lax.dynamic_index_in_dim(right_both, 1 - pair_bit, 0, keepdims=False)
    kept = lax.dynamic_index_in_dim(right_both, pair_bit, 0, keepdims=False)
    other = swap(away, "dp", pair)
    right_rows = jnp.concatenate([jnp.where(pair_bit == 0, kept, other), jnp.where(pair_bit == 0, other, kept)], 1)

    left_both = left_both.reshape(2, -1, half_blocks, tensor_count, mids // tensor_count)
    left_both = left_both.transpose(0, 3, 1, 4, 2)
    groups = []
    for base in range(dp_count):
        if not base & pair:
            groups.append([d * tensor_count + t for d in (base, base | pair) for t in range(tensor_count)])
    left_both = left_both.reshape((2 * tensor_count,) + left_both.shape[2:])
    left_both = lax.all_to_all(left_both, ("dp", "tensor"), 0, 0, axis_index_groups=groups, tiled=True)
    left_both = left_both.reshape((2, tensor_count) + left_both.shape[1:])
    left_rows = left_both.transpose(2, 3, 1, 0, 4)
    left_rows = left_rows.reshape(left_rows.shape[0], -1)
    dir_left = left_rows * lax.rsqrt(sq_left / (features * blocks) + epsilon)
    dir_right = right_rows * lax.rsqrt(sq_right / (mids * columns * tensor_count) + epsilon)
    loss = loss_all / (2.0 * total_tokens)
    return (dir_left, dir_right, loss)


def solution(mesh):
    in_specs = (P("dp", None), P("dp", "tensor"), P(None, "tensor"), P(None, "tensor"))
    out_specs = (P("dp", "tensor"), P("dp", "tensor"), P())
    return jax.shard_map(local, mesh=mesh, in_specs=in_specs, out_specs=out_specs, check_vma=False)
```

```python
import functools

import jax
import jax.numpy as jnp
from jax import lax
from jax.experimental import pallas as pl
from jax.experimental.pallas import tpu as pltpu
from jax.sharding import PartitionSpec as P

epsilon = 1e-06
VMEM_BYTES = 56 * 1024 * 1024


def swap(value, axis, stride):
    size = lax.axis_size(axis)
    return lax.ppermute(value, axis, [(a, a ^ stride) for a in range(size)])


def after(value, results):
    return lax.optimization_barrier((value, *results))[0] if results else value


def ordered(value, axis, strides):
    position = lax.axis_index(axis)
    for stride in strides:
        other = swap(value, axis, stride)
        high = (position // stride) % 2 == 1
        value = jnp.concatenate([jnp.where(high, other, value), jnp.where(high, value, other)], 0)
    return value


def contract(a, b, a_dim, b_dim):
    return lax.dot_general(a, b, (((a_dim,), (b_dim,)), ((), ())), preferred_element_type=jnp.float32)


AHEAD = 4


def row_tile(rows):
    return max(tile for tile in range(16, 513, 16) if rows % tile == 0)


def groups_of(low, high):
    cuts = [low, min(low + 2, high)] if low < high else [low]
    while cuts[-1] < high:
        cuts.append(min(cuts[-1] + 3, high))
    return list(zip(cuts[:-1], cuts[1:]))


def products_kernel(spans, parts, resumed, finish, blocks, scale, starts_ref, right_ref, *refs):
    count = len(parts)
    sets, refs = refs[: len(spans)], refs[len(spans) :]
    mixes, refs = refs[: len(spans)], refs[len(spans) :]
    pieces, refs = refs[: sum(parts)], refs[sum(parts) :]
    if resumed:
        partial_hbm, refs = refs[0], refs[1:]
    if finish:
        right_out, left_out, loss_out, total, rows_buf, mix_buf, piece_buf, sems, slope_buf, back_buf, turned_buf = refs
    else:
        total, rows_buf, mix_buf, piece_buf, sems = refs
    tokens = rows_buf.shape[0]
    depth = piece_buf.shape[0] // count
    slots = rows_buf.shape[1] // depth
    offsets = [sum(spans[:which]) for which in range(len(spans))]
    early = count - 2 if resumed else 0

    def start_of(slot):
        return pl.multiple_of(starts_ref[slot] * depth, depth)

    def copies(slot):
        found = []
        for which, span in enumerate(spans):
            target = rows_buf.at[pl.ds(offsets[which], span), pl.ds(slot * depth, depth)]
            source = sets[which].at[:, pl.ds(start_of(slot), depth)]
            found.append(pltpu.make_async_copy(source, target, sems.at[slot * len(spans) + which]))
        if slot < count:
            first, size = sum(parts[:slot]), depth // parts[slot]
            for part in range(parts[slot]):
                target = piece_buf.at[pl.ds(slot * depth + part * size, size)]
                sem = sems.at[(slots + 1) * len(spans) + 1 + first + part]
                found.append(pltpu.make_async_copy(pieces[first + part], target, sem))
        return found

    def begin(slots_now):
        for slot in slots_now:
            if slot < slots:
                for copy in copies(slot):
                    copy.start()

    def await_slots(slots_now):
        for slot in slots_now:
            for copy in copies(slot):
                copy.wait()

    def each_tile(low, high, body):
        if low < high:
            tile = row_tile(high - low)

            @pl.loop(0, (high - low) // tile)
            def _(step):
                body(pl.ds(pl.multiple_of(low + step * tile, 16), tile))

    first = [
        pltpu.make_async_copy(mixes[which], mix_buf.at[pl.ds(offsets[which], span)], sems.at[slots * len(spans) + which])
        for which, span in enumerate(spans)
    ]
    if resumed:
        sem = sems.at[(slots + 1) * len(spans)]
        first.append(pltpu.make_async_copy(partial_hbm, total.at[pl.ds(0, resumed)], sem))
    for copy in first:
        copy.start()
    begun = AHEAD
    begin(range(begun))
    for copy in first:
        copy.wait()
    for low, high in groups_of(0, early) + groups_of(early, count):
        begin(range(begun, high + AHEAD))
        begun = max(begun, high + AHEAD)
        await_slots(range(low, high))
        here = slice(low * depth, high * depth)

        def start_rows(at):
            term = contract(rows_buf[at, here], piece_buf[here], 1, 0)
            total[at] = contract(mix_buf[at], right_ref[...], 1, 0) - term

        def go_on(at):
            total[at] = total[at] - contract(rows_buf[at, here], piece_buf[here], 1, 0)

        if low < early:
            each_tile(resumed, tokens, go_on if low else start_rows)
        elif low:
            each_tile(0, resumed, go_on)
            each_tile(resumed, tokens, go_on)
        else:
            each_tile(0, tokens, start_rows)
    if not finish:
        return

    columns = right_ref.shape[1]
    mids = right_ref.shape[0] // blocks
    in_size = left_out.shape[1] // mids
    loss_out[...] = jnp.zeros_like(loss_out)
    begin(range(begun, slots))

    def slopes(at):
        residual = total[at]
        loss_out[...] += jnp.sum(residual * residual, axis=0, keepdims=True)
        slope = (residual * scale).astype(jnp.bfloat16)
        slope_buf[at] = slope
        back_buf[at] = contract(slope, right_ref[...], 1, 1)

    each_tile(0, tokens, slopes)
    full_right = contract(mix_buf[...], slope_buf[...], 0, 0)
    column_block = lax.broadcasted_iota(jnp.int32, (1, columns), 1) // (columns // blocks)
    grad_right = full_right[:mids]
    for b in range(1, blocks):
        grad_right = jnp.where(column_block == b, full_right[b * mids : (b + 1) * mids], grad_right)
    right_out[...] = grad_right
    turned_buf[...] = back_buf[...].T.astype(jnp.bfloat16)
    await_slots(range(count, slots))
    mid = lax.broadcasted_iota(jnp.int32, (mids, 1), 0)
    lane = lax.broadcasted_iota(jnp.int32, (1, depth), 1)

    @pl.loop(0, slots)
    def _(slot):
        full_left = contract(turned_buf[...], rows_buf[:, pl.ds(pl.multiple_of(slot * depth, depth), depth)], 1, 0)
        same = mid == (lane + start_of(slot)) // in_size
        sums = [
            jnp.sum(jnp.where(same, full_left[b * mids : (b + 1) * mids], 0.0), axis=0, keepdims=True)
            for b in range(blocks)
        ]
        left_out[:, pl.ds(start_of(slot), depth)] = jnp.concatenate(sums, 0)


def products(sets, mixes, right_diag, pieces, starts, blocks, scale, partial=None, finish=True):
    count = len(pieces)
    parts = tuple(len(piece) for piece in pieces)
    spans = tuple(rows.shape[0] for rows in sets)
    tokens, features = sum(spans), sets[0].shape[1]
    mid_columns, columns = right_diag.shape
    depth = sum(part.shape[0] for part in pieces[0])
    slots = starts.shape[0]
    resumed = 0 if partial is None else partial.shape[0]
    vmem = pl.BlockSpec(memory_space=pltpu.VMEM)
    operands = [starts, right_diag, *sets, *mixes, *[part for piece in pieces for part in piece]]
    if partial is not None:
        operands.append(partial)
    in_specs = [pl.BlockSpec(memory_space=pltpu.SMEM), vmem]
    in_specs += [pl.BlockSpec(memory_space=pl.ANY)] * (len(operands) - 2)
    scratch = [
        pltpu.VMEM((tokens, slots * depth), jnp.bfloat16),
        pltpu.VMEM((tokens, mid_columns), jnp.bfloat16),
        pltpu.VMEM((count * depth, columns), jnp.bfloat16),
        pltpu.SemaphoreType.DMA(((slots + 1) * len(spans) + 1 + sum(parts),)),
    ]
    flops = 2 * columns * depth * (tokens * count - resumed * (count - 2))
    if finish:
        shapes = [(mid_columns // blocks, columns), (blocks, features), (1, columns)]
        scratch = [pltpu.VMEM((tokens, columns), jnp.float32)] + scratch
        scratch += [
            pltpu.VMEM((tokens, columns), jnp.bfloat16),
            pltpu.VMEM((tokens, mid_columns), jnp.float32),
            pltpu.VMEM((mid_columns, tokens), jnp.bfloat16),
        ]
        flops += 4 * tokens * columns * mid_columns + 2 * tokens * mid_columns * features
    else:
        shapes = [(tokens, columns)]
    results = pl.pallas_call(
        functools.partial(products_kernel, spans, parts, resumed, finish, blocks, scale),
        out_shape=[jax.ShapeDtypeStruct(shape, jnp.float32) for shape in shapes],
        in_specs=in_specs,
        out_specs=[vmem] * len(shapes),
        scratch_shapes=scratch,
        compiler_params=pltpu.CompilerParams(vmem_limit_bytes=VMEM_BYTES),
        cost_estimate=pl.CostEstimate(
            flops=flops, bytes_accessed=2 * depth * (tokens * slots + columns * count), transcendentals=0
        ),
    )(*operands)
    return results if finish else results[0]


def mix_of(rows, left_diag):
    return jnp.dot(rows, left_diag, preferred_element_type=jnp.float32).astype(jnp.bfloat16)


def local(tokens, dense_weight, left_factor, right_factor):
    tok_rows, features = tokens.shape
    weight_rows, columns = dense_weight.shape
    dp_count = lax.axis_size("dp")
    tensor_count = lax.axis_size("tensor")
    dp_pos = lax.axis_index("dp")
    tensor_pos = lax.axis_index("tensor")
    in_size = left_factor.shape[0]
    mids = right_factor.shape[0]
    blocks = left_factor.shape[1] * tensor_count // mids
    own_blocks = blocks // tensor_count
    out_size = columns // own_blocks
    total_tokens = tok_rows * dp_count

    bits = dp_count.bit_length() - 1
    strides = [1 << b for b in range(bits)]
    grouped = max(bits - 3, 0)
    pair = strides[grouped:][len(strides[grouped:]) // 2]
    others = [s for s in reversed(strides[grouped:]) if s != pair]
    pair_bit = (dp_pos // pair) % 2
    unit_rows = weight_rows << grouped

    half_blocks = own_blocks // 2
    chunks = 2 if half_blocks % 2 == 0 else 1
    chunk_blocks = half_blocks // chunks
    chunk_columns = chunk_blocks * out_size
    half_columns = half_blocks * out_size

    def weight_piece(half, chunk, waits=()):
        start = half * half_columns + chunk * chunk_columns
        return lax.dynamic_slice_in_dim(after(dense_weight, waits), start, chunk_columns, 1)

    held = [{} for _ in range(chunks)]
    theirs = []
    for chunk in range(chunks):
        held[chunk][0] = ordered(weight_piece(pair_bit, chunk), "dp", strides[:grouped])
        theirs.append(ordered(weight_piece(1 - pair_bit, chunk), "dp", strides[:grouped]))
    far, near = others

    def send(chunk, mask, stride, waits=()):
        held[chunk][mask ^ stride] = swap(after(held[chunk][mask], waits), "dp", stride)
        return held[chunk][mask ^ stride]

    def send_pair(chunk, waits=()):
        held[chunk][pair] = swap(after(theirs[chunk], waits), "dp", pair)
        return held[chunk][pair]

    share = tok_rows // tensor_count
    first_cut = share * 7 // 15 // 16 * 16
    cuts = [0, first_cut, first_cut + (share - first_cut) // 2 // 16 * 16, share]

    def fetch_tokens(which, waits=()):
        begin, size = cuts[which], cuts[which + 1] - cuts[which]
        part = lax.dynamic_slice_in_dim(tokens, tensor_pos * share + begin, size, 0)
        return swap(after(part, waits), "dp", pair)

    def share_tokens(part, waits=()):
        stride = tensor_count // 2
        while stride:
            moved = swap(part, "tensor", stride)
            if stride == 1:
                return [part, moved]
            part = jnp.concatenate([part, after(moved, waits)], 0)
            stride, waits = stride // 2, ()
        return [part]

    last = chunks - 1
    parts = [None] * 2
    done = [send(0, 0, far), send_pair(0), send(0, 0, near)]
    if last:
        done.append(send(last, 0, near))
    first_done = done
    done = [send(0, pair, far, done), send(0, pair, near, done), send(0, far, near, done)] + (
        [send_pair(last, done)] if last else []
    )
    second_done = done

    left_blocks = after(left_factor, first_done).reshape(in_size, mids // tensor_count, blocks)
    left_blocks = lax.all_to_all(left_blocks, "tensor", split_axis=2, concat_axis=1, tiled=True)
    left_blocks = lax.dynamic_slice_in_dim(left_blocks, pair_bit * half_blocks, half_blocks, 2)
    eye_left = jnp.eye(mids, dtype=jnp.bfloat16)
    left_rows = left_blocks.transpose(1, 0, 2)
    left_diag = (left_rows[:, :, :, None] * eye_left[:, None, None, :]).reshape(features, half_blocks * mids)
    right_half = lax.dynamic_slice_in_dim(right_factor, pair_bit * half_columns, half_columns, 1)

    mixes = {0: mix_of(tokens, left_diag)}
    done = [*second_done, mixes[0]]
    parts[0] = fetch_tokens(0, done)
    done = [parts[0], send(0, far ^ pair, near, done)] + (
        [send(last, 0, far, done), send(last, pair, near, done)] if last else []
    )
    early_done = done

    row_block = jnp.arange(chunk_blocks * mids) // mids
    column_block = jnp.arange(chunk_columns) // out_size
    same_block = row_block[:, None] == column_block[None, :]

    token_sets = [tokens]
    order = [0, near, pair, far, far ^ near, pair ^ near, far ^ pair, far ^ pair ^ near]
    starts = jnp.stack([(dp_pos ^ mask) >> grouped for mask in order]).astype(jnp.int32)
    right_diags = []
    for chunk in range(chunks):
        right_chunk = right_half[:, chunk * chunk_columns : (chunk + 1) * chunk_columns]
        right_diags.append(jnp.where(same_block, jnp.tile(right_chunk, (chunk_blocks, 1)), jnp.bfloat16(0)))
    sums = [[] for _ in range(chunks)]
    halves = {}
    previous = None

    def run(which, chunk, end=len(order), partial=None, waits=()):
        nonlocal previous
        for item in which:
            if item not in mixes:
                mixes[item] = mix_of(token_sets[item], left_diag)
        waits = [*waits, *([] if previous is None else [previous])]
        mine = [mixes[item][:, chunk * chunk_blocks * mids : (chunk + 1) * chunk_blocks * mids] for item in which]
        mine[0] = after(mine[0], waits)
        pieces = [halves.get((chunk, mask), [held[chunk].get(mask)]) for mask in order[:end]]
        finish = end == len(order)
        terms = products(
            [token_sets[item] for item in which], mine, right_diags[chunk], pieces, starts[:end], chunk_blocks,
            1.0 / total_tokens, partial=partial, finish=finish,
        )
        if not finish:
            previous = terms
            return terms
        previous = terms[2]
        sums[chunk].append(terms)

    if last:
        source, cut = held[last][pair], unit_rows // 2
        upper = swap(after(source[:cut], early_done), "dp", far)
        late_part = fetch_tokens(1, early_done)
        near_part = send(last, far, near, early_done)
        run([0], 0, waits=early_done)
        token_sets += share_tokens(after(parts[0], early_done), [previous, upper, late_part, near_part])
        lower = swap(after(source[cut:], [upper]), "dp", far)
        last_part = fetch_tokens(2, [late_part])
        third_done = [lower, previous]
        early = list(range(1, len(token_sets)))
        run(early, 0)
        third_done.append(previous)
        parts[1] = jnp.concatenate([late_part, after(last_part, third_done)], 0)
        third_done.append(parts[1])
        fourth_done = [swap(after(half, third_done), "dp", near) for half in (upper, lower)]
        halves[last, far ^ pair] = [upper, lower]
        halves[last, far ^ pair ^ near] = fourth_done
        partial = run([0, *early], last, end=6)
        token_sets += share_tokens(after(parts[1], third_done), [partial, *fourth_done])
        late = list(range(len(early) + 1, len(token_sets)))
        mixes[late[0]] = mix_of(token_sets[late[0]], left_diag)
        run([0, *early], last, partial=partial, waits=[mixes[late[0]]])
        run(late, 0)
        run(late, last)
    else:
        for which in range(3):
            token_sets += share_tokens(fetch_tokens(which, early_done))
        run(range(len(token_sets)), 0)

    loss_part = 0.0
    summed = []
    for terms in sums:
        right_sum, left_sum = sum(term[0] for term in terms), sum(term[1] for term in terms)
        loss_part = loss_part + sum(jnp.sum(term[2]) for term in terms)
        left_sum = left_sum.reshape(chunk_blocks, mids, in_size).transpose(2, 0, 1).reshape(in_size, chunk_blocks * mids)
        both = jnp.concatenate([right_sum, left_sum], 1)
        both = both.reshape((2,) * bits + (both.shape[0] // dp_count, both.shape[1]))
        places = [s for s in reversed(strides)]
        for stride in [near, far] + strides[:grouped]:
            at = places.index(stride)
            bit = (dp_pos // stride) % 2
            away = lax.dynamic_index_in_dim(both, 1 - bit, at, keepdims=False)
            kept = lax.dynamic_index_in_dim(both, bit, at, keepdims=False)
            both = kept + swap(away, "dp", stride)
            places.remove(stride)
        summed.append(both)
    right_both = jnp.concatenate([both[..., :chunk_columns] for both in summed], -1)
    left_both = jnp.concatenate([both[..., chunk_columns:] for both in summed], -1)

    scalars = jnp.stack(
        [
            sum(jnp.sum(jnp.square(both[..., chunk_columns:])) for both in summed),
            sum(jnp.sum(jnp.square(both[..., :chunk_columns])) for both in summed),
            loss_part,
        ]
    )
    away = lax.dynamic_index_in_dim(right_both, 1 - pair_bit, 0, keepdims=False)
    kept = lax.dynamic_index_in_dim(right_both, pair_bit, 0, keepdims=False)
    other = swap(away, "dp", pair)
    right_rows = jnp.concatenate([jnp.where(pair_bit == 0, kept, other), jnp.where(pair_bit == 0, other, kept)], 1)

    rows_here = left_both.shape[1]
    left_both = left_both.reshape(2, rows_here, half_blocks, tensor_count, mids // tensor_count)
    left_both = left_both.transpose(0, 3, 1, 4, 2).reshape(2, tensor_count, -1)
    places = [dp_pos - pair_bit * pair, dp_pos + (1 - pair_bit) * pair]
    place = jnp.arange(dp_count)[:, None, None]
    outgoing = jnp.where(place == places[0], left_both[:1], jnp.where(place == places[1], left_both[1:], 0.0))
    scalars = jnp.pad(scalars, (0, 125))
    outgoing = jnp.concatenate([outgoing, jnp.broadcast_to(scalars, outgoing.shape[:2] + scalars.shape)], 2)
    incoming = lax.all_to_all(outgoing.reshape((-1,) + outgoing.shape[2:]), ("dp", "tensor"), 0, 0, tiled=True)
    sq_left, sq_right, loss_all = jnp.sum(incoming[:, -128:-125], 0)
    incoming = incoming[:, :-128].reshape(dp_count, tensor_count, rows_here, mids // tensor_count, half_blocks)
    left_both = jnp.stack([lax.dynamic_index_in_dim(incoming, p, 0, keepdims=False) for p in places])
    left_rows = left_both.transpose(2, 3, 1, 0, 4).reshape(rows_here, -1)
    dir_left = left_rows * lax.rsqrt(sq_left / (features * blocks) + epsilon)
    dir_right = right_rows * lax.rsqrt(sq_right / (mids * columns * tensor_count) + epsilon)
    loss = loss_all / (2.0 * total_tokens)
    return (dir_left, dir_right, loss)


def solution(mesh):
    in_specs = (P("dp", None), P("dp", "tensor"), P(None, "tensor"), P(None, "tensor"))
    out_specs = (P("dp", "tensor"), P("dp", "tensor"), P())
    return jax.shard_map(local, mesh=mesh, in_specs=in_specs, out_specs=out_specs, check_vma=False)
```

```python
import functools

import jax
import jax.numpy as jnp
from jax import lax
from jax.experimental import pallas as pl
from jax.experimental.pallas import tpu as pltpu
from jax.sharding import PartitionSpec as P

epsilon = 1e-06
VMEM_BYTES = 56 * 1024 * 1024


def swap(value, axis, stride):
    size = lax.axis_size(axis)
    return lax.ppermute(value, axis, [(a, a ^ stride) for a in range(size)])


def after(value, results):
    return lax.optimization_barrier((value, *results))[0] if results else value


def ordered(value, axis, strides):
    position = lax.axis_index(axis)
    for stride in strides:
        other = swap(value, axis, stride)
        high = (position // stride) % 2 == 1
        value = jnp.concatenate([jnp.where(high, other, value), jnp.where(high, value, other)], 0)
    return value


def contract(a, b, a_dim, b_dim):
    return lax.dot_general(a, b, (((a_dim,), (b_dim,)), ((), ())), preferred_element_type=jnp.float32)


AHEAD = 4


def row_tile(rows):
    return max(tile for tile in range(16, 513, 16) if rows % tile == 0)


def groups_of(low, high):
    cuts = [low, min(low + 2, high)] if low < high else [low]
    while cuts[-1] < high:
        cuts.append(min(cuts[-1] + 3, high))
    return list(zip(cuts[:-1], cuts[1:]))


def products_kernel(spans, parts, resumed, finish, blocks, scale, starts_ref, right_ref, *refs):
    count = len(parts)
    sets, refs = refs[: len(spans)], refs[len(spans) :]
    mixes, refs = refs[: len(spans)], refs[len(spans) :]
    pieces, refs = refs[: sum(parts)], refs[sum(parts) :]
    if resumed:
        partial_hbm, refs = refs[0], refs[1:]
    if finish:
        right_out, left_out, loss_out, total, rows_buf, mix_buf, piece_buf, sems, slope_buf, back_buf, turned_buf = refs
    else:
        total, rows_buf, mix_buf, piece_buf, sems = refs
    tokens = rows_buf.shape[0]
    depth = piece_buf.shape[0] // count
    slots = rows_buf.shape[1] // depth
    offsets = [sum(spans[:which]) for which in range(len(spans))]
    early = count - 2 if 0 < resumed < tokens else 0

    def start_of(slot):
        return pl.multiple_of(starts_ref[slot] * depth, depth)

    def copies(slot):
        found = []
        for which, span in enumerate(spans):
            target = rows_buf.at[pl.ds(offsets[which], span), pl.ds(slot * depth, depth)]
            source = sets[which].at[:, pl.ds(start_of(slot), depth)]
            found.append(pltpu.make_async_copy(source, target, sems.at[slot * len(spans) + which]))
        if slot < count:
            first, size = sum(parts[:slot]), depth // parts[slot]
            for part in range(parts[slot]):
                target = piece_buf.at[pl.ds(slot * depth + part * size, size)]
                sem = sems.at[(slots + 1) * len(spans) + 1 + first + part]
                found.append(pltpu.make_async_copy(pieces[first + part], target, sem))
        return found

    def begin(slots_now):
        for slot in slots_now:
            if slot < slots:
                for copy in copies(slot):
                    copy.start()

    def await_slots(slots_now):
        for slot in slots_now:
            for copy in copies(slot):
                copy.wait()

    def each_tile(low, high, body):
        if low < high:
            tile = row_tile(high - low)

            @pl.loop(0, (high - low) // tile)
            def _(step):
                body(pl.ds(pl.multiple_of(low + step * tile, 16), tile))

    first = [
        pltpu.make_async_copy(mixes[which], mix_buf.at[pl.ds(offsets[which], span)], sems.at[slots * len(spans) + which])
        for which, span in enumerate(spans)
    ]
    if resumed:
        sem = sems.at[(slots + 1) * len(spans)]
        first.append(pltpu.make_async_copy(partial_hbm, total.at[pl.ds(0, resumed)], sem))
    for copy in first:
        copy.start()
    begun = AHEAD
    begin(range(begun))
    for copy in first:
        copy.wait()
    for low, high in groups_of(0, early) + groups_of(early, count):
        begin(range(begun, high + AHEAD))
        begun = max(begun, high + AHEAD)
        await_slots(range(low, high))
        here = slice(low * depth, high * depth)

        def start_rows(at):
            term = contract(rows_buf[at, here], piece_buf[here], 1, 0)
            total[at] = contract(mix_buf[at], right_ref[...], 1, 0) - term

        def go_on(at):
            total[at] = total[at] - contract(rows_buf[at, here], piece_buf[here], 1, 0)

        if low >= early:
            each_tile(0, resumed, go_on)
        each_tile(resumed, tokens, go_on if low else start_rows)
    if not finish:
        return

    columns = right_ref.shape[1]
    mids = right_ref.shape[0] // blocks
    in_size = left_out.shape[1] // mids
    loss_out[...] = jnp.zeros_like(loss_out)
    begin(range(begun, slots))

    def slopes(at):
        residual = total[at]
        loss_out[...] += jnp.sum(residual * residual, axis=0, keepdims=True)
        slope = (residual * scale).astype(jnp.bfloat16)
        slope_buf[at] = slope
        back_buf[at] = contract(slope, right_ref[...], 1, 1)

    each_tile(0, tokens, slopes)
    full_right = contract(mix_buf[...], slope_buf[...], 0, 0)
    column_block = lax.broadcasted_iota(jnp.int32, (1, columns), 1) // (columns // blocks)
    grad_right = full_right[:mids]
    for b in range(1, blocks):
        grad_right = jnp.where(column_block == b, full_right[b * mids : (b + 1) * mids], grad_right)
    right_out[...] = grad_right
    turned_buf[...] = back_buf[...].T.astype(jnp.bfloat16)
    await_slots(range(count, slots))
    mid = lax.broadcasted_iota(jnp.int32, (mids, 1), 0)
    lane = lax.broadcasted_iota(jnp.int32, (1, depth), 1)

    @pl.loop(0, slots)
    def _(slot):
        full_left = contract(turned_buf[...], rows_buf[:, pl.ds(pl.multiple_of(slot * depth, depth), depth)], 1, 0)
        same = mid == (lane + start_of(slot)) // in_size
        sums = [
            jnp.sum(jnp.where(same, full_left[b * mids : (b + 1) * mids], 0.0), axis=0, keepdims=True)
            for b in range(blocks)
        ]
        left_out[:, pl.ds(start_of(slot), depth)] = jnp.concatenate(sums, 0)


def products(sets, mixes, right_diag, pieces, starts, blocks, scale, partial=None, finish=True):
    count = len(pieces)
    parts = tuple(len(piece) for piece in pieces)
    spans = tuple(rows.shape[0] for rows in sets)
    tokens, features = sum(spans), sets[0].shape[1]
    mid_columns, columns = right_diag.shape
    depth = sum(part.shape[0] for part in pieces[0])
    slots = starts.shape[0]
    resumed = 0 if partial is None else partial.shape[0]
    vmem = pl.BlockSpec(memory_space=pltpu.VMEM)
    operands = [starts, right_diag, *sets, *mixes, *[part for piece in pieces for part in piece]]
    if partial is not None:
        operands.append(partial)
    in_specs = [pl.BlockSpec(memory_space=pltpu.SMEM), vmem]
    in_specs += [pl.BlockSpec(memory_space=pl.ANY)] * (len(operands) - 2)
    scratch = [
        pltpu.VMEM((tokens, slots * depth), jnp.bfloat16),
        pltpu.VMEM((tokens, mid_columns), jnp.bfloat16),
        pltpu.VMEM((count * depth, columns), jnp.bfloat16),
        pltpu.SemaphoreType.DMA(((slots + 1) * len(spans) + 1 + sum(parts),)),
    ]
    flops = 2 * columns * depth * tokens * count
    if finish:
        shapes = [(mid_columns // blocks, columns), (blocks, features), (1, columns)]
        scratch = [pltpu.VMEM((tokens, columns), jnp.float32)] + scratch
        scratch += [
            pltpu.VMEM((tokens, columns), jnp.bfloat16),
            pltpu.VMEM((tokens, mid_columns), jnp.float32),
            pltpu.VMEM((mid_columns, tokens), jnp.bfloat16),
        ]
        flops += 4 * tokens * columns * mid_columns + 2 * tokens * mid_columns * features
    else:
        shapes = [(tokens, columns)]
    results = pl.pallas_call(
        functools.partial(products_kernel, spans, parts, resumed, finish, blocks, scale),
        out_shape=[jax.ShapeDtypeStruct(shape, jnp.float32) for shape in shapes],
        in_specs=in_specs,
        out_specs=[vmem] * len(shapes),
        scratch_shapes=scratch,
        compiler_params=pltpu.CompilerParams(vmem_limit_bytes=VMEM_BYTES),
        cost_estimate=pl.CostEstimate(
            flops=flops, bytes_accessed=2 * depth * (tokens * slots + columns * count), transcendentals=0
        ),
    )(*operands)
    return results if finish else results[0]


def mix_of(rows, left_diag):
    return jnp.dot(rows, left_diag, preferred_element_type=jnp.float32).astype(jnp.bfloat16)


def local(tokens, dense_weight, left_factor, right_factor):
    tok_rows, features = tokens.shape
    weight_rows, columns = dense_weight.shape
    dp_count = lax.axis_size("dp")
    tensor_count = lax.axis_size("tensor")
    dp_pos = lax.axis_index("dp")
    tensor_pos = lax.axis_index("tensor")
    in_size = left_factor.shape[0]
    mids = right_factor.shape[0]
    blocks = left_factor.shape[1] * tensor_count // mids
    own_blocks = blocks // tensor_count
    out_size = columns // own_blocks
    total_tokens = tok_rows * dp_count

    bits = dp_count.bit_length() - 1
    strides = [1 << b for b in range(bits)]
    grouped = max(bits - 3, 0)
    pair = strides[grouped:][len(strides[grouped:]) // 2]
    others = [s for s in reversed(strides[grouped:]) if s != pair]
    pair_bit = (dp_pos // pair) % 2
    unit_rows = weight_rows << grouped

    half_blocks = own_blocks // 2
    chunks = 2 if half_blocks % 2 == 0 else 1
    chunk_blocks = half_blocks // chunks
    chunk_columns = chunk_blocks * out_size
    half_columns = half_blocks * out_size

    def weight_piece(half, chunk, waits=()):
        start = half * half_columns + chunk * chunk_columns
        return lax.dynamic_slice_in_dim(after(dense_weight, waits), start, chunk_columns, 1)

    held = [{} for _ in range(chunks)]
    theirs = []
    for chunk in range(chunks):
        held[chunk][0] = ordered(weight_piece(pair_bit, chunk), "dp", strides[:grouped])
        theirs.append(ordered(weight_piece(1 - pair_bit, chunk), "dp", strides[:grouped]))
    far, near = others

    def send(chunk, mask, stride, waits=()):
        held[chunk][mask ^ stride] = swap(after(held[chunk][mask], waits), "dp", stride)
        return held[chunk][mask ^ stride]

    def send_pair(chunk, waits=()):
        held[chunk][pair] = swap(after(theirs[chunk], waits), "dp", pair)
        return held[chunk][pair]

    share = tok_rows // tensor_count
    first_cut = share * 7 // 15 // 16 * 16
    cuts = [0, first_cut, first_cut + (share - first_cut) // 2 // 16 * 16, share]

    def fetch_tokens(which, waits=()):
        begin, size = cuts[which], cuts[which + 1] - cuts[which]
        part = lax.dynamic_slice_in_dim(tokens, tensor_pos * share + begin, size, 0)
        return swap(after(part, waits), "dp", pair)

    def share_tokens(part, waits=()):
        stride = tensor_count // 2
        while stride:
            moved = swap(part, "tensor", stride)
            if stride == 1:
                return [part, moved]
            part = jnp.concatenate([part, after(moved, waits)], 0)
            stride, waits = stride // 2, ()
        return [part]

    last = chunks - 1
    parts = [None] * 2
    done = [send(0, 0, far), send_pair(0), send(0, 0, near)]
    if last:
        done.append(send(last, 0, near))
    first_done = done
    done = [send(0, pair, far, done), send(0, pair, near, done), send(0, far, near, done)] + (
        [send_pair(last, done)] if last else []
    )
    second_done = done

    left_blocks = after(left_factor, first_done).reshape(in_size, mids // tensor_count, blocks)
    left_blocks = lax.all_to_all(left_blocks, "tensor", split_axis=2, concat_axis=1, tiled=True)
    left_blocks = lax.dynamic_slice_in_dim(left_blocks, pair_bit * half_blocks, half_blocks, 2)
    eye_left = jnp.eye(mids, dtype=jnp.bfloat16)
    left_rows = left_blocks.transpose(1, 0, 2)
    left_diag = (left_rows[:, :, :, None] * eye_left[:, None, None, :]).reshape(features, half_blocks * mids)
    right_half = lax.dynamic_slice_in_dim(right_factor, pair_bit * half_columns, half_columns, 1)

    mixes = {0: mix_of(tokens, left_diag)}
    done = [*second_done, mixes[0]]
    parts[0] = fetch_tokens(0, done)
    done = [parts[0], send(0, far ^ pair, near, done)] + (
        [send(last, 0, far, done), send(last, pair, near, done)] if last else []
    )
    early_done = done

    row_block = jnp.arange(chunk_blocks * mids) // mids
    column_block = jnp.arange(chunk_columns) // out_size
    same_block = row_block[:, None] == column_block[None, :]

    token_sets = [tokens]
    order = [0, near, pair, far, far ^ near, pair ^ near, far ^ pair, far ^ pair ^ near]
    starts = jnp.stack([(dp_pos ^ mask) >> grouped for mask in order]).astype(jnp.int32)
    right_diags = []
    for chunk in range(chunks):
        right_chunk = right_half[:, chunk * chunk_columns : (chunk + 1) * chunk_columns]
        right_diags.append(jnp.where(same_block, jnp.tile(right_chunk, (chunk_blocks, 1)), jnp.bfloat16(0)))
    sums = [[] for _ in range(chunks)]
    halves = {}
    previous = None

    def run(which, chunk, end=len(order), partial=None, waits=()):
        nonlocal previous
        for item in which:
            if item not in mixes:
                mixes[item] = mix_of(token_sets[item], left_diag)
        waits = [*waits, *([] if previous is None else [previous])]
        mine = [mixes[item][:, chunk * chunk_blocks * mids : (chunk + 1) * chunk_blocks * mids] for item in which]
        mine[0] = after(mine[0], waits)
        pieces = [halves.get((chunk, mask), [held[chunk].get(mask)]) for mask in order[:end]]
        finish = end == len(order)
        places = starts[:end]
        if partial is not None:
            pieces, places = pieces[-2:], jnp.concatenate([starts[-2:], starts[:-2]])
        terms = products(
            [token_sets[item] for item in which], mine, right_diags[chunk], pieces, places, chunk_blocks,
            1.0 / total_tokens, partial=partial, finish=finish,
        )
        if not finish:
            previous = terms
            return terms
        previous = terms[2]
        sums[chunk].append(terms)

    def gather_rows(terms):
        right_sum, left_sum = sum(term[0] for term in terms), sum(term[1] for term in terms)
        left_sum = left_sum.reshape(chunk_blocks, mids, in_size).transpose(2, 0, 1).reshape(in_size, chunk_blocks * mids)
        both = jnp.concatenate([right_sum, left_sum], 1)
        return both.reshape((2,) * bits + (both.shape[0] // dp_count, both.shape[1]))

    def sum_by_halving(both):
        places = [s for s in reversed(strides)]
        for stride in [near, far] + strides[:grouped]:
            at = places.index(stride)
            bit = (dp_pos // stride) % 2
            away = lax.dynamic_index_in_dim(both, 1 - bit, at, keepdims=False)
            kept = lax.dynamic_index_in_dim(both, bit, at, keepdims=False)
            both = kept + swap(away, "dp", stride)
            places.remove(stride)
        return both

    if last:
        source, cut = held[last][pair], unit_rows // 2
        upper = swap(after(source[:cut], early_done), "dp", far)
        late_part = fetch_tokens(1, early_done)
        near_part = send(last, far, near, early_done)
        run([0], 0, waits=early_done)
        token_sets += share_tokens(after(parts[0], early_done), [previous, upper, late_part, near_part])
        lower = swap(after(source[cut:], [upper]), "dp", far)
        last_part = fetch_tokens(2, [late_part])
        third_done = [lower, previous]
        early = list(range(1, len(token_sets)))
        run(early, 0)
        third_done.append(previous)
        parts[1] = jnp.concatenate([late_part, after(last_part, third_done)], 0)
        third_done.append(parts[1])
        fourth_done = [swap(after(half, third_done), "dp", near) for half in (upper, lower)]
        halves[last, far ^ pair] = [upper, lower]
        halves[last, far ^ pair ^ near] = fourth_done
        partial = run([0, *early], last, end=6)
        token_sets += share_tokens(after(parts[1], third_done), [partial, *fourth_done])
        late = list(range(len(early) + 1, len(token_sets)))
        mixes[late[0]] = mix_of(token_sets[late[0]], left_diag)
        run([0, *early], last, partial=partial, waits=[mixes[late[0]]])
        run(late, 0)
        first_rows = gather_rows(sums[0])
        summed = [sum_by_halving(first_rows)]
        run(late, last, waits=[first_rows])
    else:
        for which in range(3):
            token_sets += share_tokens(fetch_tokens(which, early_done))
        run(range(len(token_sets)), 0)
        summed = []
    summed.append(sum_by_halving(gather_rows(sums[last])))
    loss_part = sum(jnp.sum(term[2]) for terms in sums for term in terms)

    right_both = jnp.concatenate([both[..., :chunk_columns] for both in summed], -1)
    left_both = jnp.concatenate([both[..., chunk_columns:] for both in summed], -1)

    scalars = jnp.stack(
        [
            sum(jnp.sum(jnp.square(both[..., chunk_columns:])) for both in summed),
            sum(jnp.sum(jnp.square(both[..., :chunk_columns])) for both in summed),
            loss_part,
        ]
    )
    away = lax.dynamic_index_in_dim(right_both, 1 - pair_bit, 0, keepdims=False)
    kept = lax.dynamic_index_in_dim(right_both, pair_bit, 0, keepdims=False)
    other = swap(away, "dp", pair)
    right_rows = jnp.concatenate([jnp.where(pair_bit == 0, kept, other), jnp.where(pair_bit == 0, other, kept)], 1)

    rows_here = left_both.shape[1]
    left_both = left_both.reshape(2, rows_here, half_blocks, tensor_count, mids // tensor_count)
    left_both = left_both.transpose(0, 3, 1, 4, 2).reshape(2, tensor_count, -1)
    places = [dp_pos - pair_bit * pair, dp_pos + (1 - pair_bit) * pair]
    place = jnp.arange(dp_count)[:, None, None]
    outgoing = jnp.where(place == places[0], left_both[:1], jnp.where(place == places[1], left_both[1:], 0.0))
    scalars = jnp.pad(scalars, (0, 125))
    outgoing = jnp.concatenate([outgoing, jnp.broadcast_to(scalars, outgoing.shape[:2] + scalars.shape)], 2)
    incoming = lax.all_to_all(outgoing.reshape((-1,) + outgoing.shape[2:]), ("dp", "tensor"), 0, 0, tiled=True)
    sq_left, sq_right, loss_all = jnp.sum(incoming[:, -128:-125], 0)
    incoming = incoming[:, :-128].reshape(dp_count, tensor_count, rows_here, mids // tensor_count, half_blocks)
    left_both = jnp.stack([lax.dynamic_index_in_dim(incoming, p, 0, keepdims=False) for p in places])
    left_rows = left_both.transpose(2, 3, 1, 0, 4).reshape(rows_here, -1)
    dir_left = left_rows * lax.rsqrt(sq_left / (features * blocks) + epsilon)
    dir_right = right_rows * lax.rsqrt(sq_right / (mids * columns * tensor_count) + epsilon)
    loss = loss_all / (2.0 * total_tokens)
    return (dir_left, dir_right, loss)


def solution(mesh):
    in_specs = (P("dp", None), P("dp", "tensor"), P(None, "tensor"), P(None, "tensor"))
    out_specs = (P("dp", "tensor"), P("dp", "tensor"), P())
    return jax.shard_map(local, mesh=mesh, in_specs=in_specs, out_specs=out_specs, check_vma=False)
```

```python
import functools

import jax
import jax.numpy as jnp
from jax import lax
from jax.experimental import pallas as pl
from jax.experimental.pallas import tpu as pltpu
from jax.sharding import PartitionSpec as P

epsilon = 1e-06
VMEM_BYTES = 36 * 1024 * 1024


def swap(value, axis, stride):
    size = lax.axis_size(axis)
    return lax.ppermute(value, axis, [(a, a ^ stride) for a in range(size)])


def after(value, results):
    return lax.optimization_barrier((value, *results))[0] if results else value


def ordered(value, axis, strides):
    position = lax.axis_index(axis)
    for stride in strides:
        other = swap(value, axis, stride)
        high = (position // stride) % 2 == 1
        value = jnp.concatenate([jnp.where(high, other, value), jnp.where(high, value, other)], 0)
    return value


def contract(a, b, a_dim, b_dim):
    return lax.dot_general(a, b, (((a_dim,), (b_dim,)), ((), ())), preferred_element_type=jnp.float32)


AHEAD = 4


def row_tile(rows):
    return max(tile for tile in range(16, 513, 16) if rows % tile == 0)


def groups_of(low, high):
    cuts = [low, min(low + 2, high)] if low < high else [low]
    while cuts[-1] < high:
        cuts.append(min(cuts[-1] + 3, high))
    return list(zip(cuts[:-1], cuts[1:]))


def products_kernel(spans, parts, resumed, finish, blocks, scale, starts_ref, right_ref, *refs):
    count = len(parts)
    sets, refs = refs[: len(spans)], refs[len(spans) :]
    mixes, refs = refs[: len(spans)], refs[len(spans) :]
    pieces, refs = refs[: sum(parts)], refs[sum(parts) :]
    if resumed:
        partial_hbm, refs = refs[0], refs[1:]
    if finish:
        right_out, left_out, loss_out, total, rows_buf, mix_buf, piece_buf, sems, slope_buf, back_buf, turned_buf = refs
    else:
        total, rows_buf, mix_buf, piece_buf, sems = refs
    tokens = rows_buf.shape[0]
    depth = piece_buf.shape[0] // count
    slots = rows_buf.shape[1] // depth
    offsets = [sum(spans[:which]) for which in range(len(spans))]
    early = count - 2 if 0 < resumed < tokens else 0

    def start_of(slot):
        return pl.multiple_of(starts_ref[slot] * depth, depth)

    def copies(slot):
        found = []
        for which, span in enumerate(spans):
            target = rows_buf.at[pl.ds(offsets[which], span), pl.ds(slot * depth, depth)]
            source = sets[which].at[:, pl.ds(start_of(slot), depth)]
            found.append(pltpu.make_async_copy(source, target, sems.at[slot * len(spans) + which]))
        if slot < count:
            first, size = sum(parts[:slot]), depth // parts[slot]
            for part in range(parts[slot]):
                target = piece_buf.at[pl.ds(slot * depth + part * size, size)]
                sem = sems.at[(slots + 1) * len(spans) + 1 + first + part]
                found.append(pltpu.make_async_copy(pieces[first + part], target, sem))
        return found

    def begin(slots_now):
        for slot in slots_now:
            if slot < slots:
                for copy in copies(slot):
                    copy.start()

    def await_slots(slots_now):
        for slot in slots_now:
            for copy in copies(slot):
                copy.wait()

    def each_tile(low, high, body):
        if low < high:
            tile = row_tile(high - low)

            @pl.loop(0, (high - low) // tile)
            def _(step):
                body(pl.ds(pl.multiple_of(low + step * tile, 16), tile))

    first = [
        pltpu.make_async_copy(mixes[which], mix_buf.at[pl.ds(offsets[which], span)], sems.at[slots * len(spans) + which])
        for which, span in enumerate(spans)
    ]
    if resumed:
        sem = sems.at[(slots + 1) * len(spans)]
        first.append(pltpu.make_async_copy(partial_hbm, total.at[pl.ds(0, resumed)], sem))
    for copy in first:
        copy.start()
    begun = AHEAD
    begin(range(begun))
    for copy in first:
        copy.wait()
    for low, high in groups_of(0, early) + groups_of(early, count):
        begin(range(begun, high + AHEAD))
        begun = max(begun, high + AHEAD)
        await_slots(range(low, high))
        here = slice(low * depth, high * depth)

        def start_rows(at):
            term = contract(rows_buf[at, here], piece_buf[here], 1, 0)
            total[at] = contract(mix_buf[at], right_ref[...], 1, 0) - term

        def go_on(at):
            total[at] = total[at] - contract(rows_buf[at, here], piece_buf[here], 1, 0)

        if low >= early:
            each_tile(0, resumed, go_on)
        each_tile(resumed, tokens, go_on if low else start_rows)
    if not finish:
        return

    columns = right_ref.shape[1]
    mids = right_ref.shape[0] // blocks
    in_size = left_out.shape[1] // mids
    loss_out[...] = jnp.zeros_like(loss_out)
    begin(range(begun, slots))

    def slopes(at):
        residual = total[at]
        loss_out[...] += jnp.sum(residual * residual, axis=0, keepdims=True)
        slope = (residual * scale).astype(jnp.bfloat16)
        slope_buf[at] = slope
        back_buf[at] = contract(slope, right_ref[...], 1, 1)

    each_tile(0, tokens, slopes)
    full_right = contract(mix_buf[...], slope_buf[...], 0, 0)
    column_block = lax.broadcasted_iota(jnp.int32, (1, columns), 1) // (columns // blocks)
    grad_right = full_right[:mids]
    for b in range(1, blocks):
        grad_right = jnp.where(column_block == b, full_right[b * mids : (b + 1) * mids], grad_right)
    right_out[...] = grad_right
    turned_buf[...] = back_buf[...].T.astype(jnp.bfloat16)
    await_slots(range(count, slots))
    mid = lax.broadcasted_iota(jnp.int32, (mids, 1), 0)
    lane = lax.broadcasted_iota(jnp.int32, (1, depth), 1)

    @pl.loop(0, slots)
    def _(slot):
        full_left = contract(turned_buf[...], rows_buf[:, pl.ds(pl.multiple_of(slot * depth, depth), depth)], 1, 0)
        same = mid == (lane + start_of(slot)) // in_size
        sums = [
            jnp.sum(jnp.where(same, full_left[b * mids : (b + 1) * mids], 0.0), axis=0, keepdims=True)
            for b in range(blocks)
        ]
        left_out[:, pl.ds(start_of(slot), depth)] = jnp.concatenate(sums, 0)


def products(sets, mixes, right_diag, pieces, starts, blocks, scale, partial=None, finish=True):
    count = len(pieces)
    parts = tuple(len(piece) for piece in pieces)
    spans = tuple(rows.shape[0] for rows in sets)
    tokens, features = sum(spans), sets[0].shape[1]
    mid_columns, columns = right_diag.shape
    depth = sum(part.shape[0] for part in pieces[0])
    slots = starts.shape[0]
    resumed = 0 if partial is None else partial.shape[0]
    vmem = pl.BlockSpec(memory_space=pltpu.VMEM)
    operands = [starts, right_diag, *sets, *mixes, *[part for piece in pieces for part in piece]]
    if partial is not None:
        operands.append(partial)
    in_specs = [pl.BlockSpec(memory_space=pltpu.SMEM), vmem]
    in_specs += [pl.BlockSpec(memory_space=pl.ANY)] * (len(operands) - 2)
    scratch = [
        pltpu.VMEM((tokens, slots * depth), jnp.bfloat16),
        pltpu.VMEM((tokens, mid_columns), jnp.bfloat16),
        pltpu.VMEM((count * depth, columns), jnp.bfloat16),
        pltpu.SemaphoreType.DMA(((slots + 1) * len(spans) + 1 + sum(parts),)),
    ]
    flops = 2 * columns * depth * tokens * count
    if finish:
        shapes = [(mid_columns // blocks, columns), (blocks, features), (1, columns)]
        scratch = [pltpu.VMEM((tokens, columns), jnp.float32)] + scratch
        scratch += [
            pltpu.VMEM((tokens, columns), jnp.bfloat16),
            pltpu.VMEM((tokens, mid_columns), jnp.float32),
            pltpu.VMEM((mid_columns, tokens), jnp.bfloat16),
        ]
        flops += 4 * tokens * columns * mid_columns + 2 * tokens * mid_columns * features
    else:
        shapes = [(tokens, columns)]
    results = pl.pallas_call(
        functools.partial(products_kernel, spans, parts, resumed, finish, blocks, scale),
        out_shape=[jax.ShapeDtypeStruct(shape, jnp.float32) for shape in shapes],
        in_specs=in_specs,
        out_specs=[vmem] * len(shapes),
        scratch_shapes=scratch,
        compiler_params=pltpu.CompilerParams(vmem_limit_bytes=VMEM_BYTES),
        cost_estimate=pl.CostEstimate(
            flops=flops, bytes_accessed=2 * depth * (tokens * slots + columns * count), transcendentals=0
        ),
    )(*operands)
    return results if finish else results[0]


def mix_of(rows, left_diag):
    return jnp.dot(rows, left_diag, preferred_element_type=jnp.float32).astype(jnp.bfloat16)


def local(tokens, dense_weight, left_factor, right_factor):
    tok_rows, features = tokens.shape
    weight_rows, columns = dense_weight.shape
    dp_count = lax.axis_size("dp")
    tensor_count = lax.axis_size("tensor")
    dp_pos = lax.axis_index("dp")
    tensor_pos = lax.axis_index("tensor")
    in_size = left_factor.shape[0]
    mids = right_factor.shape[0]
    blocks = left_factor.shape[1] * tensor_count // mids
    own_blocks = blocks // tensor_count
    out_size = columns // own_blocks
    total_tokens = tok_rows * dp_count

    bits = dp_count.bit_length() - 1
    strides = [1 << b for b in range(bits)]
    grouped = max(bits - 3, 0)
    pair = strides[grouped:][len(strides[grouped:]) // 2]
    others = [s for s in reversed(strides[grouped:]) if s != pair]
    pair_bit = (dp_pos // pair) % 2
    unit_rows = weight_rows << grouped

    half_blocks = own_blocks // 2
    chunks = 2 if half_blocks % 2 == 0 else 1
    chunk_blocks = half_blocks // chunks
    chunk_columns = chunk_blocks * out_size
    half_columns = half_blocks * out_size

    def weight_piece(half, chunk, waits=()):
        start = half * half_columns + chunk * chunk_columns
        return lax.dynamic_slice_in_dim(after(dense_weight, waits), start, chunk_columns, 1)

    held = [{} for _ in range(chunks)]
    theirs = []
    for chunk in range(chunks):
        held[chunk][0] = ordered(weight_piece(pair_bit, chunk), "dp", strides[:grouped])
        theirs.append(ordered(weight_piece(1 - pair_bit, chunk), "dp", strides[:grouped]))
    far, near = others

    def send(chunk, mask, stride, waits=()):
        held[chunk][mask ^ stride] = swap(after(held[chunk][mask], waits), "dp", stride)
        return held[chunk][mask ^ stride]

    def send_pair(chunk, waits=()):
        held[chunk][pair] = swap(after(theirs[chunk], waits), "dp", pair)
        return held[chunk][pair]

    share = tok_rows // tensor_count
    first_cut = share * 7 // 15 // 16 * 16
    cuts = [0, first_cut, first_cut + (share - first_cut) // 2 // 16 * 16, share]

    def fetch_tokens(which, waits=()):
        begin, size = cuts[which], cuts[which + 1] - cuts[which]
        part = lax.dynamic_slice_in_dim(tokens, tensor_pos * share + begin, size, 0)
        return swap(after(part, waits), "dp", pair)

    def share_tokens(part, waits=()):
        stride = tensor_count // 2
        while stride:
            moved = swap(part, "tensor", stride)
            if stride == 1:
                return [part, moved]
            part = jnp.concatenate([part, after(moved, waits)], 0)
            stride, waits = stride // 2, ()
        return [part]

    last = chunks - 1
    parts = [None] * 2
    done = [send(0, 0, far), send_pair(0), send(0, 0, near)]
    if last:
        done.append(send(last, 0, near))
    first_done = done
    done = [send(0, pair, far, done), send(0, pair, near, done), send(0, far, near, done)] + (
        [send_pair(last, done)] if last else []
    )
    second_done = done

    left_blocks = after(left_factor, first_done).reshape(in_size, mids // tensor_count, blocks)
    left_blocks = lax.all_to_all(left_blocks, "tensor", split_axis=2, concat_axis=1, tiled=True)
    left_blocks = lax.dynamic_slice_in_dim(left_blocks, pair_bit * half_blocks, half_blocks, 2)
    eye_left = jnp.eye(mids, dtype=jnp.bfloat16)
    left_rows = left_blocks.transpose(1, 0, 2)
    left_diag = (left_rows[:, :, :, None] * eye_left[:, None, None, :]).reshape(features, half_blocks * mids)
    right_half = lax.dynamic_slice_in_dim(right_factor, pair_bit * half_columns, half_columns, 1)

    mixes = {0: mix_of(tokens, left_diag)}
    done = [*second_done, mixes[0]]
    parts[0] = fetch_tokens(0, done)
    done = [parts[0], send(0, far ^ pair, near, done)] + (
        [send(last, 0, far, done), send(last, pair, near, done)] if last else []
    )
    early_done = done

    row_block = jnp.arange(chunk_blocks * mids) // mids
    column_block = jnp.arange(chunk_columns) // out_size
    same_block = row_block[:, None] == column_block[None, :]

    token_sets = [tokens]
    order = [0, near, pair, far, far ^ near, pair ^ near, far ^ pair, far ^ pair ^ near]
    starts = jnp.stack([(dp_pos ^ mask) >> grouped for mask in order]).astype(jnp.int32)
    right_diags = []
    for chunk in range(chunks):
        right_chunk = right_half[:, chunk * chunk_columns : (chunk + 1) * chunk_columns]
        right_diags.append(jnp.where(same_block, jnp.tile(right_chunk, (chunk_blocks, 1)), jnp.bfloat16(0)))
    sums = [[] for _ in range(chunks)]
    halves = {}
    previous = None

    def run(which, chunk, end=len(order), partial=None, waits=()):
        nonlocal previous
        for item in which:
            if item not in mixes:
                mixes[item] = mix_of(token_sets[item], left_diag)
        waits = [*waits, *([] if previous is None else [previous])]
        mine = [mixes[item][:, chunk * chunk_blocks * mids : (chunk + 1) * chunk_blocks * mids] for item in which]
        mine[0] = after(mine[0], waits)
        pieces = [halves.get((chunk, mask), [held[chunk].get(mask)]) for mask in order[:end]]
        finish = end == len(order)
        places = starts[:end]
        if partial is not None:
            pieces, places = pieces[-2:], jnp.concatenate([starts[-2:], starts[:-2]])
        terms = products(
            [token_sets[item] for item in which], mine, right_diags[chunk], pieces, places, chunk_blocks,
            1.0 / total_tokens, partial=partial, finish=finish,
        )
        if not finish:
            previous = terms
            return terms
        previous = terms[2]
        sums[chunk].append(terms)

    def gather_rows(terms):
        right_sum, left_sum = sum(term[0] for term in terms), sum(term[1] for term in terms)
        left_sum = left_sum.reshape(chunk_blocks, mids, in_size).transpose(2, 0, 1).reshape(in_size, chunk_blocks * mids)
        both = jnp.concatenate([right_sum, left_sum], 1)
        return both.reshape((2,) * bits + (both.shape[0] // dp_count, both.shape[1]))

    def sum_by_halving(both):
        places = [s for s in reversed(strides)]
        for stride in [near, far] + strides[:grouped]:
            at = places.index(stride)
            bit = (dp_pos // stride) % 2
            away = lax.dynamic_index_in_dim(both, 1 - bit, at, keepdims=False)
            kept = lax.dynamic_index_in_dim(both, bit, at, keepdims=False)
            both = kept + swap(away, "dp", stride)
            places.remove(stride)
        return both

    if last:
        source, cut = held[last][pair], unit_rows // 2
        upper = swap(after(source[:cut], early_done), "dp", far)
        late_part = fetch_tokens(1, early_done)
        near_part = send(last, far, near, early_done)
        run([0], 0, waits=early_done)
        token_sets += share_tokens(after(parts[0], early_done), [previous, upper, late_part, near_part])
        lower = swap(after(source[cut:], [upper]), "dp", far)
        last_part = fetch_tokens(2, [late_part])
        third_done = [lower, previous]
        early = list(range(1, len(token_sets)))
        run(early, 0)
        third_done.append(previous)
        parts[1] = jnp.concatenate([late_part, after(last_part, third_done)], 0)
        third_done.append(parts[1])
        fourth_done = [swap(after(half, third_done), "dp", near) for half in (upper, lower)]
        halves[last, far ^ pair] = [upper, lower]
        halves[last, far ^ pair ^ near] = fourth_done
        partial = run([0, *early], last, end=6)
        token_sets += share_tokens(after(parts[1], third_done), [partial, *fourth_done])
        late = list(range(len(early) + 1, len(token_sets)))
        mixes[late[0]] = mix_of(token_sets[late[0]], left_diag)
        run([0, *early], last, partial=partial, waits=[mixes[late[0]]])
        run(late, 0)
        first_rows = gather_rows(sums[0])
        summed = [sum_by_halving(first_rows)]
        run(late, last, waits=[first_rows])
    else:
        for which in range(3):
            token_sets += share_tokens(fetch_tokens(which, early_done))
        run(range(len(token_sets)), 0)
        summed = []
    summed.append(sum_by_halving(gather_rows(sums[last])))
    loss_part = sum(jnp.sum(term[2]) for terms in sums for term in terms)

    right_both = jnp.concatenate([both[..., :chunk_columns] for both in summed], -1)
    left_both = jnp.concatenate([both[..., chunk_columns:] for both in summed], -1)

    scalars = jnp.stack(
        [
            sum(jnp.sum(jnp.square(both[..., chunk_columns:])) for both in summed),
            sum(jnp.sum(jnp.square(both[..., :chunk_columns])) for both in summed),
            loss_part,
        ]
    )
    away = lax.dynamic_index_in_dim(right_both, 1 - pair_bit, 0, keepdims=False)
    kept = lax.dynamic_index_in_dim(right_both, pair_bit, 0, keepdims=False)
    other = swap(away, "dp", pair)
    right_rows = jnp.concatenate([jnp.where(pair_bit == 0, kept, other), jnp.where(pair_bit == 0, other, kept)], 1)

    rows_here = left_both.shape[1]
    left_both = left_both.reshape(2, rows_here, half_blocks, tensor_count, mids // tensor_count)
    left_both = left_both.transpose(0, 3, 1, 4, 2).reshape(2, tensor_count, -1)
    places = [dp_pos - pair_bit * pair, dp_pos + (1 - pair_bit) * pair]
    place = jnp.arange(dp_count)[:, None, None]
    outgoing = jnp.where(place == places[0], left_both[:1], jnp.where(place == places[1], left_both[1:], 0.0))
    scalars = jnp.pad(scalars, (0, 125))
    outgoing = jnp.concatenate([outgoing, jnp.broadcast_to(scalars, outgoing.shape[:2] + scalars.shape)], 2)
    incoming = lax.all_to_all(outgoing.reshape((-1,) + outgoing.shape[2:]), ("dp", "tensor"), 0, 0, tiled=True)
    sq_left, sq_right, loss_all = jnp.sum(incoming[:, -128:-125], 0)
    incoming = incoming[:, :-128].reshape(dp_count, tensor_count, rows_here, mids // tensor_count, half_blocks)
    left_both = jnp.stack([lax.dynamic_index_in_dim(incoming, p, 0, keepdims=False) for p in places])
    left_rows = left_both.transpose(2, 3, 1, 0, 4).reshape(rows_here, -1)
    dir_left = left_rows * lax.rsqrt(sq_left / (features * blocks) + epsilon)
    dir_right = right_rows * lax.rsqrt(sq_right / (mids * columns * tensor_count) + epsilon)
    loss = loss_all / (2.0 * total_tokens)
    return (dir_left, dir_right, loss)


def solution(mesh):
    in_specs = (P("dp", None), P("dp", "tensor"), P(None, "tensor"), P(None, "tensor"))
    out_specs = (P("dp", "tensor"), P("dp", "tensor"), P())
    return jax.shard_map(local, mesh=mesh, in_specs=in_specs, out_specs=out_specs, check_vma=False)
```

```python
import functools

import jax
import jax.numpy as jnp
from jax import lax
from jax.experimental import pallas as pl
from jax.experimental.pallas import tpu as pltpu
from jax.sharding import PartitionSpec as P

epsilon = 1e-06
VMEM_BYTES = 56 * 1024 * 1024
LESS_VMEM_BYTES = 36 * 1024 * 1024


def swap(value, axis, stride):
    size = lax.axis_size(axis)
    return lax.ppermute(value, axis, [(a, a ^ stride) for a in range(size)])


def after(value, results):
    return lax.optimization_barrier((value, *results))[0] if results else value


def ordered(value, axis, strides):
    position = lax.axis_index(axis)
    for stride in strides:
        other = swap(value, axis, stride)
        high = (position // stride) % 2 == 1
        value = jnp.concatenate([jnp.where(high, other, value), jnp.where(high, value, other)], 0)
    return value


def contract(a, b, a_dim, b_dim):
    return lax.dot_general(a, b, (((a_dim,), (b_dim,)), ((), ())), preferred_element_type=jnp.float32)


AHEAD = 4


def row_tile(rows):
    return max(tile for tile in range(16, 513, 16) if rows % tile == 0)


def groups_of(low, high):
    cuts = [low, min(low + 2, high)] if low < high else [low]
    while cuts[-1] < high:
        cuts.append(min(cuts[-1] + 3, high))
    return list(zip(cuts[:-1], cuts[1:]))


def products_kernel(spans, parts, resumed, finish, blocks, scale, starts_ref, right_ref, *refs):
    count = len(parts)
    sets, refs = refs[: len(spans)], refs[len(spans) :]
    mixes, refs = refs[: len(spans)], refs[len(spans) :]
    pieces, refs = refs[: sum(parts)], refs[sum(parts) :]
    if resumed:
        partial_hbm, refs = refs[0], refs[1:]
    if finish:
        right_out, left_out, loss_out, total, rows_buf, mix_buf, piece_buf, sems, slope_buf, back_buf, turned_buf = refs
    else:
        total, rows_buf, mix_buf, piece_buf, sems = refs
    tokens = rows_buf.shape[0]
    depth = piece_buf.shape[0] // count
    slots = rows_buf.shape[1] // depth
    offsets = [sum(spans[:which]) for which in range(len(spans))]
    early = count - 2 if 0 < resumed < tokens else 0

    def start_of(slot):
        return pl.multiple_of(starts_ref[slot] * depth, depth)

    def copies(slot):
        found = []
        for which, span in enumerate(spans):
            target = rows_buf.at[pl.ds(offsets[which], span), pl.ds(slot * depth, depth)]
            source = sets[which].at[:, pl.ds(start_of(slot), depth)]
            found.append(pltpu.make_async_copy(source, target, sems.at[slot * len(spans) + which]))
        if slot < count:
            first, size = sum(parts[:slot]), depth // parts[slot]
            for part in range(parts[slot]):
                target = piece_buf.at[pl.ds(slot * depth + part * size, size)]
                sem = sems.at[(slots + 1) * len(spans) + 1 + first + part]
                found.append(pltpu.make_async_copy(pieces[first + part], target, sem))
        return found

    def begin(slots_now):
        for slot in slots_now:
            if slot < slots:
                for copy in copies(slot):
                    copy.start()

    def await_slots(slots_now):
        for slot in slots_now:
            for copy in copies(slot):
                copy.wait()

    def each_tile(low, high, body):
        if low < high:
            tile = row_tile(high - low)

            @pl.loop(0, (high - low) // tile)
            def _(step):
                body(pl.ds(pl.multiple_of(low + step * tile, 16), tile))

    first = [
        pltpu.make_async_copy(mixes[which], mix_buf.at[pl.ds(offsets[which], span)], sems.at[slots * len(spans) + which])
        for which, span in enumerate(spans)
    ]
    if resumed:
        sem = sems.at[(slots + 1) * len(spans)]
        first.append(pltpu.make_async_copy(partial_hbm, total.at[pl.ds(0, resumed)], sem))
    for copy in first:
        copy.start()
    begun = AHEAD
    begin(range(begun))
    for copy in first:
        copy.wait()
    for low, high in groups_of(0, early) + groups_of(early, count):
        begin(range(begun, high + AHEAD))
        begun = max(begun, high + AHEAD)
        await_slots(range(low, high))
        here = slice(low * depth, high * depth)

        def start_rows(at):
            term = contract(rows_buf[at, here], piece_buf[here], 1, 0)
            total[at] = contract(mix_buf[at], right_ref[...], 1, 0) - term

        def go_on(at):
            total[at] = total[at] - contract(rows_buf[at, here], piece_buf[here], 1, 0)

        if low >= early:
            each_tile(0, resumed, go_on)
        each_tile(resumed, tokens, go_on if low else start_rows)
    if not finish:
        return

    columns = right_ref.shape[1]
    mids = right_ref.shape[0] // blocks
    in_size = left_out.shape[1] // mids
    loss_out[...] = jnp.zeros_like(loss_out)
    begin(range(begun, slots))

    def slopes(at):
        residual = total[at]
        loss_out[...] += jnp.sum(residual * residual, axis=0, keepdims=True)
        slope = (residual * scale).astype(jnp.bfloat16)
        slope_buf[at] = slope
        back_buf[at] = contract(slope, right_ref[...], 1, 1)

    each_tile(0, tokens, slopes)
    full_right = contract(mix_buf[...], slope_buf[...], 0, 0)
    column_block = lax.broadcasted_iota(jnp.int32, (1, columns), 1) // (columns // blocks)
    grad_right = full_right[:mids]
    for b in range(1, blocks):
        grad_right = jnp.where(column_block == b, full_right[b * mids : (b + 1) * mids], grad_right)
    right_out[...] = grad_right
    turned_buf[...] = back_buf[...].T.astype(jnp.bfloat16)
    await_slots(range(count, slots))
    mid = lax.broadcasted_iota(jnp.int32, (mids, 1), 0)
    lane = lax.broadcasted_iota(jnp.int32, (1, depth), 1)

    @pl.loop(0, slots)
    def _(slot):
        full_left = contract(turned_buf[...], rows_buf[:, pl.ds(pl.multiple_of(slot * depth, depth), depth)], 1, 0)
        same = mid == (lane + start_of(slot)) // in_size
        sums = [
            jnp.sum(jnp.where(same, full_left[b * mids : (b + 1) * mids], 0.0), axis=0, keepdims=True)
            for b in range(blocks)
        ]
        left_out[:, pl.ds(start_of(slot), depth)] = jnp.concatenate(sums, 0)


def products(sets, mixes, right_diag, pieces, starts, blocks, scale, partial=None, finish=True):
    count = len(pieces)
    parts = tuple(len(piece) for piece in pieces)
    spans = tuple(rows.shape[0] for rows in sets)
    tokens, features = sum(spans), sets[0].shape[1]
    mid_columns, columns = right_diag.shape
    depth = sum(part.shape[0] for part in pieces[0])
    slots = starts.shape[0]
    resumed = 0 if partial is None else partial.shape[0]
    vmem = pl.BlockSpec(memory_space=pltpu.VMEM)
    operands = [starts, right_diag, *sets, *mixes, *[part for piece in pieces for part in piece]]
    if partial is not None:
        operands.append(partial)
    in_specs = [pl.BlockSpec(memory_space=pltpu.SMEM), vmem]
    in_specs += [pl.BlockSpec(memory_space=pl.ANY)] * (len(operands) - 2)
    scratch = [
        pltpu.VMEM((tokens, slots * depth), jnp.bfloat16),
        pltpu.VMEM((tokens, mid_columns), jnp.bfloat16),
        pltpu.VMEM((count * depth, columns), jnp.bfloat16),
        pltpu.SemaphoreType.DMA(((slots + 1) * len(spans) + 1 + sum(parts),)),
    ]
    flops = 2 * columns * depth * tokens * count
    if finish:
        shapes = [(mid_columns // blocks, columns), (blocks, features), (1, columns)]
        scratch = [pltpu.VMEM((tokens, columns), jnp.float32)] + scratch
        scratch += [
            pltpu.VMEM((tokens, columns), jnp.bfloat16),
            pltpu.VMEM((tokens, mid_columns), jnp.float32),
            pltpu.VMEM((mid_columns, tokens), jnp.bfloat16),
        ]
        flops += 4 * tokens * columns * mid_columns + 2 * tokens * mid_columns * features
    else:
        shapes = [(tokens, columns)]
    results = pl.pallas_call(
        functools.partial(products_kernel, spans, parts, resumed, finish, blocks, scale),
        out_shape=[jax.ShapeDtypeStruct(shape, jnp.float32) for shape in shapes],
        in_specs=in_specs,
        out_specs=[vmem] * len(shapes),
        scratch_shapes=scratch,
        compiler_params=pltpu.CompilerParams(
            vmem_limit_bytes=LESS_VMEM_BYTES if resumed or not finish else VMEM_BYTES
        ),
        cost_estimate=pl.CostEstimate(
            flops=flops, bytes_accessed=2 * depth * (tokens * slots + columns * count), transcendentals=0
        ),
    )(*operands)
    return results if finish else results[0]


def mix_of(rows, left_diag):
    return jnp.dot(rows, left_diag, preferred_element_type=jnp.float32).astype(jnp.bfloat16)


def local(tokens, dense_weight, left_factor, right_factor):
    tok_rows, features = tokens.shape
    weight_rows, columns = dense_weight.shape
    dp_count = lax.axis_size("dp")
    tensor_count = lax.axis_size("tensor")
    dp_pos = lax.axis_index("dp")
    tensor_pos = lax.axis_index("tensor")
    in_size = left_factor.shape[0]
    mids = right_factor.shape[0]
    blocks = left_factor.shape[1] * tensor_count // mids
    own_blocks = blocks // tensor_count
    out_size = columns // own_blocks
    total_tokens = tok_rows * dp_count

    bits = dp_count.bit_length() - 1
    strides = [1 << b for b in range(bits)]
    grouped = max(bits - 3, 0)
    pair = strides[grouped:][len(strides[grouped:]) // 2]
    others = [s for s in reversed(strides[grouped:]) if s != pair]
    pair_bit = (dp_pos // pair) % 2
    unit_rows = weight_rows << grouped

    half_blocks = own_blocks // 2
    chunks = 2 if half_blocks % 2 == 0 else 1
    chunk_blocks = half_blocks // chunks
    chunk_columns = chunk_blocks * out_size
    half_columns = half_blocks * out_size

    def weight_piece(half, chunk, waits=()):
        start = half * half_columns + chunk * chunk_columns
        return lax.dynamic_slice_in_dim(after(dense_weight, waits), start, chunk_columns, 1)

    held = [{} for _ in range(chunks)]
    theirs = []
    for chunk in range(chunks):
        held[chunk][0] = ordered(weight_piece(pair_bit, chunk), "dp", strides[:grouped])
        theirs.append(ordered(weight_piece(1 - pair_bit, chunk), "dp", strides[:grouped]))
    far, near = others

    def send(chunk, mask, stride, waits=()):
        held[chunk][mask ^ stride] = swap(after(held[chunk][mask], waits), "dp", stride)
        return held[chunk][mask ^ stride]

    def send_pair(chunk, waits=()):
        held[chunk][pair] = swap(after(theirs[chunk], waits), "dp", pair)
        return held[chunk][pair]

    share = tok_rows // tensor_count
    first_cut = share * 7 // 15 // 16 * 16
    cuts = [0, first_cut, first_cut + (share - first_cut) // 2 // 16 * 16, share]

    def fetch_tokens(which, waits=()):
        begin, size = cuts[which], cuts[which + 1] - cuts[which]
        part = lax.dynamic_slice_in_dim(tokens, tensor_pos * share + begin, size, 0)
        return swap(after(part, waits), "dp", pair)

    def share_tokens(part, waits=()):
        stride = tensor_count // 2
        while stride:
            moved = swap(part, "tensor", stride)
            if stride == 1:
                return [part, moved]
            part = jnp.concatenate([part, after(moved, waits)], 0)
            stride, waits = stride // 2, ()
        return [part]

    last = chunks - 1
    parts = [None] * 2
    done = [send(0, 0, far), send_pair(0), send(0, 0, near)]
    if last:
        done.append(send(last, 0, near))
    first_done = done
    done = [send(0, pair, far, done), send(0, pair, near, done), send(0, far, near, done)] + (
        [send_pair(last, done)] if last else []
    )
    second_done = done

    left_blocks = after(left_factor, first_done).reshape(in_size, mids // tensor_count, blocks)
    left_blocks = lax.all_to_all(left_blocks, "tensor", split_axis=2, concat_axis=1, tiled=True)
    left_blocks = lax.dynamic_slice_in_dim(left_blocks, pair_bit * half_blocks, half_blocks, 2)
    eye_left = jnp.eye(mids, dtype=jnp.bfloat16)
    left_rows = left_blocks.transpose(1, 0, 2)
    left_diag = (left_rows[:, :, :, None] * eye_left[:, None, None, :]).reshape(features, half_blocks * mids)
    right_half = lax.dynamic_slice_in_dim(right_factor, pair_bit * half_columns, half_columns, 1)

    mixes = {0: mix_of(tokens, left_diag)}
    done = [*second_done, mixes[0]]
    parts[0] = fetch_tokens(0, done)
    done = [parts[0], send(0, far ^ pair, near, done)] + (
        [send(last, 0, far, done), send(last, pair, near, done)] if last else []
    )
    early_done = done

    row_block = jnp.arange(chunk_blocks * mids) // mids
    column_block = jnp.arange(chunk_columns) // out_size
    same_block = row_block[:, None] == column_block[None, :]

    token_sets = [tokens]
    order = [0, near, pair, far, far ^ near, pair ^ near, far ^ pair, far ^ pair ^ near]
    starts = jnp.stack([(dp_pos ^ mask) >> grouped for mask in order]).astype(jnp.int32)
    right_diags = []
    for chunk in range(chunks):
        right_chunk = right_half[:, chunk * chunk_columns : (chunk + 1) * chunk_columns]
        right_diags.append(jnp.where(same_block, jnp.tile(right_chunk, (chunk_blocks, 1)), jnp.bfloat16(0)))
    sums = [[] for _ in range(chunks)]
    halves = {}
    previous = None

    def run(which, chunk, end=len(order), partial=None, waits=()):
        nonlocal previous
        for item in which:
            if item not in mixes:
                mixes[item] = mix_of(token_sets[item], left_diag)
        waits = [*waits, *([] if previous is None else [previous])]
        mine = [mixes[item][:, chunk * chunk_blocks * mids : (chunk + 1) * chunk_blocks * mids] for item in which]
        mine[0] = after(mine[0], waits)
        pieces = [halves.get((chunk, mask), [held[chunk].get(mask)]) for mask in order[:end]]
        finish = end == len(order)
        places = starts[:end]
        if partial is not None:
            pieces, places = pieces[-2:], jnp.concatenate([starts[-2:], starts[:-2]])
        terms = products(
            [token_sets[item] for item in which], mine, right_diags[chunk], pieces, places, chunk_blocks,
            1.0 / total_tokens, partial=partial, finish=finish,
        )
        if not finish:
            previous = terms
            return terms
        previous = terms[2]
        sums[chunk].append(terms)

    def gather_rows(terms):
        right_sum, left_sum = sum(term[0] for term in terms), sum(term[1] for term in terms)
        left_sum = left_sum.reshape(chunk_blocks, mids, in_size).transpose(2, 0, 1).reshape(in_size, chunk_blocks * mids)
        both = jnp.concatenate([right_sum, left_sum], 1)
        return both.reshape((2,) * bits + (both.shape[0] // dp_count, both.shape[1]))

    def sum_by_halving(both):
        places = [s for s in reversed(strides)]
        for stride in [near, far] + strides[:grouped]:
            at = places.index(stride)
            bit = (dp_pos // stride) % 2
            away = lax.dynamic_index_in_dim(both, 1 - bit, at, keepdims=False)
            kept = lax.dynamic_index_in_dim(both, bit, at, keepdims=False)
            both = kept + swap(away, "dp", stride)
            places.remove(stride)
        return both

    if last:
        source, cut = held[last][pair], unit_rows // 2
        upper = swap(after(source[:cut], early_done), "dp", far)
        late_part = fetch_tokens(1, early_done)
        near_part = send(last, far, near, early_done)
        run([0], 0, waits=early_done)
        token_sets += share_tokens(after(parts[0], early_done), [previous, upper, late_part, near_part])
        lower = swap(after(source[cut:], [upper]), "dp", far)
        last_part = fetch_tokens(2, [late_part])
        third_done = [lower, previous]
        early = list(range(1, len(token_sets)))
        run(early, 0)
        third_done.append(previous)
        parts[1] = jnp.concatenate([late_part, after(last_part, third_done)], 0)
        third_done.append(parts[1])
        fourth_done = [swap(after(half, third_done), "dp", near) for half in (upper, lower)]
        halves[last, far ^ pair] = [upper, lower]
        halves[last, far ^ pair ^ near] = fourth_done
        partial = run([0, *early], last, end=6)
        token_sets += share_tokens(after(parts[1], third_done), [partial, *fourth_done])
        late = list(range(len(early) + 1, len(token_sets)))
        mixes[late[0]] = mix_of(token_sets[late[0]], left_diag)
        run([0, *early], last, partial=partial, waits=[mixes[late[0]]])
        run(late, 0)
        first_rows = gather_rows(sums[0])
        summed = [sum_by_halving(first_rows)]
        run(late, last, waits=[first_rows])
    else:
        for which in range(3):
            token_sets += share_tokens(fetch_tokens(which, early_done))
        run(range(len(token_sets)), 0)
        summed = []
    summed.append(sum_by_halving(gather_rows(sums[last])))
    loss_part = sum(jnp.sum(term[2]) for terms in sums for term in terms)

    right_both = jnp.concatenate([both[..., :chunk_columns] for both in summed], -1)
    left_both = jnp.concatenate([both[..., chunk_columns:] for both in summed], -1)

    scalars = jnp.stack(
        [
            sum(jnp.sum(jnp.square(both[..., chunk_columns:])) for both in summed),
            sum(jnp.sum(jnp.square(both[..., :chunk_columns])) for both in summed),
            loss_part,
        ]
    )
    away = lax.dynamic_index_in_dim(right_both, 1 - pair_bit, 0, keepdims=False)
    kept = lax.dynamic_index_in_dim(right_both, pair_bit, 0, keepdims=False)
    other = swap(away, "dp", pair)
    right_rows = jnp.concatenate([jnp.where(pair_bit == 0, kept, other), jnp.where(pair_bit == 0, other, kept)], 1)

    rows_here = left_both.shape[1]
    left_both = left_both.reshape(2, rows_here, half_blocks, tensor_count, mids // tensor_count)
    left_both = left_both.transpose(0, 3, 1, 4, 2).reshape(2, tensor_count, -1)
    places = [dp_pos - pair_bit * pair, dp_pos + (1 - pair_bit) * pair]
    place = jnp.arange(dp_count)[:, None, None]
    outgoing = jnp.where(place == places[0], left_both[:1], jnp.where(place == places[1], left_both[1:], 0.0))
    scalars = jnp.pad(scalars, (0, 125))
    outgoing = jnp.concatenate([outgoing, jnp.broadcast_to(scalars, outgoing.shape[:2] + scalars.shape)], 2)
    incoming = lax.all_to_all(outgoing.reshape((-1,) + outgoing.shape[2:]), ("dp", "tensor"), 0, 0, tiled=True)
    sq_left, sq_right, loss_all = jnp.sum(incoming[:, -128:-125], 0)
    incoming = incoming[:, :-128].reshape(dp_count, tensor_count, rows_here, mids // tensor_count, half_blocks)
    left_both = jnp.stack([lax.dynamic_index_in_dim(incoming, p, 0, keepdims=False) for p in places])
    left_rows = left_both.transpose(2, 3, 1, 0, 4).reshape(rows_here, -1)
    dir_left = left_rows * lax.rsqrt(sq_left / (features * blocks) + epsilon)
    dir_right = right_rows * lax.rsqrt(sq_right / (mids * columns * tensor_count) + epsilon)
    loss = loss_all / (2.0 * total_tokens)
    return (dir_left, dir_right, loss)


def solution(mesh):
    in_specs = (P("dp", None), P("dp", "tensor"), P(None, "tensor"), P(None, "tensor"))
    out_specs = (P("dp", "tensor"), P("dp", "tensor"), P())
    return jax.shard_map(local, mesh=mesh, in_specs=in_specs, out_specs=out_specs, check_vma=False)
```

```python
import functools

import jax
import jax.numpy as jnp
from jax import lax
from jax.experimental import pallas as pl
from jax.experimental.pallas import tpu as pltpu
from jax.sharding import PartitionSpec as P

epsilon = 1e-06
VMEM_BYTES = 56 * 1024 * 1024
LESS_VMEM_BYTES = 36 * 1024 * 1024


def swap(value, axis, stride):
    size = lax.axis_size(axis)
    return lax.ppermute(value, axis, [(a, a ^ stride) for a in range(size)])


def after(value, results):
    return lax.optimization_barrier((value, *results))[0] if results else value


def ordered(value, axis, strides):
    position = lax.axis_index(axis)
    for stride in strides:
        other = swap(value, axis, stride)
        high = (position // stride) % 2 == 1
        value = jnp.concatenate([jnp.where(high, other, value), jnp.where(high, value, other)], 0)
    return value


def contract(a, b, a_dim, b_dim):
    return lax.dot_general(a, b, (((a_dim,), (b_dim,)), ((), ())), preferred_element_type=jnp.float32)


AHEAD = 4


def row_tile(rows):
    return max(tile for tile in range(16, 513, 16) if rows % tile == 0)


def groups_of(low, high):
    cuts = [low, min(low + 2, high)] if low < high else [low]
    while cuts[-1] < high:
        cuts.append(min(cuts[-1] + 3, high))
    return list(zip(cuts[:-1], cuts[1:]))


def products_kernel(spans, parts, resumed, finish, blocks, scale, starts_ref, right_ref, *refs):
    count = len(parts)
    sets, refs = refs[: len(spans)], refs[len(spans) :]
    mixes, refs = refs[: len(spans)], refs[len(spans) :]
    pieces, refs = refs[: sum(parts)], refs[sum(parts) :]
    if resumed:
        partial_hbm, refs = refs[0], refs[1:]
    if finish:
        right_out, left_out, loss_out, total, rows_buf, mix_buf, piece_buf, sems, slope_buf, back_buf, turned_buf = refs
    else:
        total, rows_buf, mix_buf, piece_buf, sems = refs
    tokens = rows_buf.shape[0]
    depth = piece_buf.shape[0] // count
    slots = rows_buf.shape[1] // depth
    offsets = [sum(spans[:which]) for which in range(len(spans))]
    early = count - 2 if 0 < resumed < tokens else 0

    def start_of(slot):
        return pl.multiple_of(starts_ref[slot] * depth, depth)

    def copies(slot):
        found = []
        for which, span in enumerate(spans):
            target = rows_buf.at[pl.ds(offsets[which], span), pl.ds(slot * depth, depth)]
            source = sets[which].at[:, pl.ds(start_of(slot), depth)]
            found.append(pltpu.make_async_copy(source, target, sems.at[slot * len(spans) + which]))
        if slot < count:
            first, size = sum(parts[:slot]), depth // parts[slot]
            for part in range(parts[slot]):
                target = piece_buf.at[pl.ds(slot * depth + part * size, size)]
                sem = sems.at[(slots + 1) * len(spans) + 1 + first + part]
                found.append(pltpu.make_async_copy(pieces[first + part], target, sem))
        return found

    def begin(slots_now):
        for slot in slots_now:
            if slot < slots:
                for copy in copies(slot):
                    copy.start()

    def await_slots(slots_now):
        for slot in slots_now:
            for copy in copies(slot):
                copy.wait()

    def each_tile(low, high, body):
        if low < high:
            tile = row_tile(high - low)

            @pl.loop(0, (high - low) // tile)
            def _(step):
                body(pl.ds(pl.multiple_of(low + step * tile, 16), tile))

    first = [
        pltpu.make_async_copy(mixes[which], mix_buf.at[pl.ds(offsets[which], span)], sems.at[slots * len(spans) + which])
        for which, span in enumerate(spans)
    ]
    if resumed:
        sem = sems.at[(slots + 1) * len(spans)]
        first.append(pltpu.make_async_copy(partial_hbm, total.at[pl.ds(0, resumed)], sem))
    for copy in first:
        copy.start()
    begun = AHEAD
    begin(range(begun))
    for copy in first:
        copy.wait()
    for low, high in groups_of(0, early) + groups_of(early, count):
        begin(range(begun, high + AHEAD))
        begun = max(begun, high + AHEAD)
        await_slots(range(low, high))
        here = slice(low * depth, high * depth)

        def start_rows(at):
            term = contract(rows_buf[at, here], piece_buf[here], 1, 0)
            total[at] = contract(mix_buf[at], right_ref[...], 1, 0) - term

        def go_on(at):
            total[at] = total[at] - contract(rows_buf[at, here], piece_buf[here], 1, 0)

        if low >= early:
            each_tile(0, resumed, go_on)
        each_tile(resumed, tokens, go_on if low else start_rows)
    if not finish:
        return

    columns = right_ref.shape[1]
    mids = right_ref.shape[0] // blocks
    in_size = left_out.shape[1] // mids
    loss_out[...] = jnp.zeros_like(loss_out)
    begin(range(begun, slots))

    def slopes(at):
        residual = total[at]
        loss_out[...] += jnp.sum(residual * residual, axis=0, keepdims=True)
        slope = (residual * scale).astype(jnp.bfloat16)
        slope_buf[at] = slope
        back_buf[at] = contract(slope, right_ref[...], 1, 1)

    each_tile(0, tokens, slopes)
    full_right = contract(mix_buf[...], slope_buf[...], 0, 0)
    column_block = lax.broadcasted_iota(jnp.int32, (1, columns), 1) // (columns // blocks)
    grad_right = full_right[:mids]
    for b in range(1, blocks):
        grad_right = jnp.where(column_block == b, full_right[b * mids : (b + 1) * mids], grad_right)
    right_out[...] = grad_right
    turned_buf[...] = back_buf[...].T.astype(jnp.bfloat16)
    await_slots(range(count, slots))
    mid = lax.broadcasted_iota(jnp.int32, (mids, 1), 0)
    lane = lax.broadcasted_iota(jnp.int32, (1, depth), 1)

    @pl.loop(0, slots)
    def _(slot):
        full_left = contract(turned_buf[...], rows_buf[:, pl.ds(pl.multiple_of(slot * depth, depth), depth)], 1, 0)
        same = mid == (lane + start_of(slot)) // in_size
        sums = [
            jnp.sum(jnp.where(same, full_left[b * mids : (b + 1) * mids], 0.0), axis=0, keepdims=True)
            for b in range(blocks)
        ]
        left_out[:, pl.ds(start_of(slot), depth)] = jnp.concatenate(sums, 0)


def products(sets, mixes, right_diag, pieces, starts, blocks, scale, partial=None, finish=True):
    count = len(pieces)
    parts = tuple(len(piece) for piece in pieces)
    spans = tuple(rows.shape[0] for rows in sets)
    tokens, features = sum(spans), sets[0].shape[1]
    mid_columns, columns = right_diag.shape
    depth = sum(part.shape[0] for part in pieces[0])
    slots = starts.shape[0]
    resumed = 0 if partial is None else partial.shape[0]
    vmem = pl.BlockSpec(memory_space=pltpu.VMEM)
    operands = [starts, right_diag, *sets, *mixes, *[part for piece in pieces for part in piece]]
    if partial is not None:
        operands.append(partial)
    in_specs = [pl.BlockSpec(memory_space=pltpu.SMEM), vmem]
    in_specs += [pl.BlockSpec(memory_space=pl.ANY)] * (len(operands) - 2)
    scratch = [
        pltpu.VMEM((tokens, slots * depth), jnp.bfloat16),
        pltpu.VMEM((tokens, mid_columns), jnp.bfloat16),
        pltpu.VMEM((count * depth, columns), jnp.bfloat16),
        pltpu.SemaphoreType.DMA(((slots + 1) * len(spans) + 1 + sum(parts),)),
    ]
    flops = 2 * columns * depth * tokens * count
    if finish:
        shapes = [(mid_columns // blocks, columns), (blocks, features), (1, columns)]
        scratch = [pltpu.VMEM((tokens, columns), jnp.float32)] + scratch
        scratch += [
            pltpu.VMEM((tokens, columns), jnp.bfloat16),
            pltpu.VMEM((tokens, mid_columns), jnp.float32),
            pltpu.VMEM((mid_columns, tokens), jnp.bfloat16),
        ]
        flops += 4 * tokens * columns * mid_columns + 2 * tokens * mid_columns * features
    else:
        shapes = [(tokens, columns)]
    results = pl.pallas_call(
        functools.partial(products_kernel, spans, parts, resumed, finish, blocks, scale),
        out_shape=[jax.ShapeDtypeStruct(shape, jnp.float32) for shape in shapes],
        in_specs=in_specs,
        out_specs=[vmem] * len(shapes),
        scratch_shapes=scratch,
        compiler_params=pltpu.CompilerParams(
            vmem_limit_bytes=LESS_VMEM_BYTES if resumed or not finish else VMEM_BYTES
        ),
        cost_estimate=pl.CostEstimate(
            flops=flops, bytes_accessed=2 * depth * (tokens * slots + columns * count), transcendentals=0
        ),
    )(*operands)
    return results if finish else results[0]


def mix_of(rows, left_diag):
    return jnp.dot(rows, left_diag, preferred_element_type=jnp.float32).astype(jnp.bfloat16)


def local(tokens, dense_weight, left_factor, right_factor):
    tok_rows, features = tokens.shape
    weight_rows, columns = dense_weight.shape
    dp_count = lax.axis_size("dp")
    tensor_count = lax.axis_size("tensor")
    dp_pos = lax.axis_index("dp")
    tensor_pos = lax.axis_index("tensor")
    in_size = left_factor.shape[0]
    mids = right_factor.shape[0]
    blocks = left_factor.shape[1] * tensor_count // mids
    own_blocks = blocks // tensor_count
    out_size = columns // own_blocks
    total_tokens = tok_rows * dp_count

    bits = dp_count.bit_length() - 1
    strides = [1 << b for b in range(bits)]
    grouped = max(bits - 3, 0)
    pair = strides[grouped:][len(strides[grouped:]) // 2]
    others = [s for s in reversed(strides[grouped:]) if s != pair]
    pair_bit = (dp_pos // pair) % 2
    unit_rows = weight_rows << grouped

    half_blocks = own_blocks // 2
    chunks = 2 if half_blocks % 2 == 0 else 1
    chunk_blocks = half_blocks // chunks
    chunk_columns = chunk_blocks * out_size
    half_columns = half_blocks * out_size

    def weight_piece(half, chunk, waits=()):
        start = half * half_columns + chunk * chunk_columns
        return lax.dynamic_slice_in_dim(after(dense_weight, waits), start, chunk_columns, 1)

    held = [{} for _ in range(chunks)]
    theirs = []
    for chunk in range(chunks):
        held[chunk][0] = ordered(weight_piece(pair_bit, chunk), "dp", strides[:grouped])
        theirs.append(ordered(weight_piece(1 - pair_bit, chunk), "dp", strides[:grouped]))
    far, near = others

    def send(chunk, mask, stride, waits=()):
        held[chunk][mask ^ stride] = swap(after(held[chunk][mask], waits), "dp", stride)
        return held[chunk][mask ^ stride]

    def send_pair(chunk, waits=()):
        held[chunk][pair] = swap(after(theirs[chunk], waits), "dp", pair)
        return held[chunk][pair]

    share = tok_rows // tensor_count
    first_cut = share * 7 // 15 // 16 * 16
    cuts = [0, first_cut, first_cut + (share - first_cut) // 2 // 16 * 16, share]

    def fetch_tokens(which, waits=()):
        begin, size = cuts[which], cuts[which + 1] - cuts[which]
        part = lax.dynamic_slice_in_dim(tokens, tensor_pos * share + begin, size, 0)
        return swap(after(part, waits), "dp", pair)

    def share_tokens(part, waits=()):
        stride = tensor_count // 2
        while stride:
            moved = swap(part, "tensor", stride)
            if stride == 1:
                return [part, moved]
            part = jnp.concatenate([part, after(moved, waits)], 0)
            stride, waits = stride // 2, ()
        return [part]

    last = chunks - 1
    parts = [None] * 2
    done = [send(0, 0, far), send_pair(0), send(0, 0, near)]
    if last:
        done.append(send(last, 0, near))
    first_done = done
    done = [send(0, pair, far, done), send(0, pair, near, done), send(0, far, near, done)] + (
        [send_pair(last, done)] if last else []
    )
    second_done = done

    left_blocks = after(left_factor, first_done).reshape(in_size, mids // tensor_count, blocks)
    left_blocks = lax.all_to_all(left_blocks, "tensor", split_axis=2, concat_axis=1, tiled=True)
    left_blocks = lax.dynamic_slice_in_dim(left_blocks, pair_bit * half_blocks, half_blocks, 2)
    eye_left = jnp.eye(mids, dtype=jnp.bfloat16)
    left_rows = left_blocks.transpose(1, 0, 2)
    left_diag = (left_rows[:, :, :, None] * eye_left[:, None, None, :]).reshape(features, half_blocks * mids)
    right_half = lax.dynamic_slice_in_dim(right_factor, pair_bit * half_columns, half_columns, 1)

    mixes = {0: mix_of(tokens, left_diag)}
    done = [*second_done, mixes[0]]
    parts[0] = fetch_tokens(0, done)
    done = [parts[0], send(0, far ^ pair, near, done)] + (
        [send(last, 0, far, done), send(last, pair, near, done)] if last else []
    )
    early_done = done

    row_block = jnp.arange(chunk_blocks * mids) // mids
    column_block = jnp.arange(chunk_columns) // out_size
    same_block = row_block[:, None] == column_block[None, :]

    token_sets = [tokens]
    order = [0, near, pair, far, far ^ near, pair ^ near, far ^ pair, far ^ pair ^ near]
    starts = jnp.stack([(dp_pos ^ mask) >> grouped for mask in order]).astype(jnp.int32)
    right_diags = []
    for chunk in range(chunks):
        right_chunk = right_half[:, chunk * chunk_columns : (chunk + 1) * chunk_columns]
        right_diags.append(jnp.where(same_block, jnp.tile(right_chunk, (chunk_blocks, 1)), jnp.bfloat16(0)))
    sums = [[] for _ in range(chunks)]
    halves = {}
    previous = None

    def run(which, chunk, end=len(order), partial=None, waits=()):
        nonlocal previous
        for item in which:
            if item not in mixes:
                mixes[item] = mix_of(token_sets[item], left_diag)
        waits = [*waits, *([] if previous is None else [previous])]
        mine = [mixes[item][:, chunk * chunk_blocks * mids : (chunk + 1) * chunk_blocks * mids] for item in which]
        mine[0] = after(mine[0], waits)
        pieces = [halves.get((chunk, mask), [held[chunk].get(mask)]) for mask in order[:end]]
        finish = end == len(order)
        places = starts[:end]
        if partial is not None:
            pieces, places = pieces[-2:], jnp.concatenate([starts[-2:], starts[:-2]])
        terms = products(
            [token_sets[item] for item in which], mine, right_diags[chunk], pieces, places, chunk_blocks,
            1.0 / total_tokens, partial=partial, finish=finish,
        )
        if not finish:
            previous = terms
            return terms
        previous = terms[2]
        sums[chunk].append(terms)

    def gather_rows(terms):
        right_sum, left_sum = sum(term[0] for term in terms), sum(term[1] for term in terms)
        left_sum = left_sum.reshape(chunk_blocks, mids, in_size).transpose(2, 0, 1).reshape(in_size, chunk_blocks * mids)
        both = jnp.concatenate([right_sum, left_sum], 1)
        return both.reshape((2,) * bits + (both.shape[0] // dp_count, both.shape[1]))

    def halve(both, stride, at):
        bit = (dp_pos // stride) % 2
        away = lax.dynamic_index_in_dim(both, 1 - bit, at, keepdims=False)
        kept = lax.dynamic_index_in_dim(both, bit, at, keepdims=False)
        return kept + swap(away, "dp", stride)

    def halve_near(both):
        return halve(both, near, bits - near.bit_length())

    def halve_rest(both):
        places = [s for s in reversed(strides) if s != near]
        for stride in [far] + strides[:grouped]:
            both = halve(both, stride, places.index(stride))
            places.remove(stride)
        return both

    if last:
        source, cut = held[last][pair], unit_rows // 2
        upper = swap(after(source[:cut], early_done), "dp", far)
        late_part = fetch_tokens(1, early_done)
        near_part = send(last, far, near, early_done)
        run([0], 0, waits=early_done)
        token_sets += share_tokens(after(parts[0], early_done), [previous, upper, late_part, near_part])
        lower = swap(after(source[cut:], [upper]), "dp", far)
        last_part = fetch_tokens(2, [late_part])
        third_done = [lower, previous]
        early = list(range(1, len(token_sets)))
        run(early, 0)
        third_done.append(previous)
        parts[1] = jnp.concatenate([late_part, after(last_part, third_done)], 0)
        third_done.append(parts[1])
        fourth_done = [swap(after(half, third_done), "dp", near) for half in (upper, lower)]
        halves[last, far ^ pair] = [upper, lower]
        halves[last, far ^ pair ^ near] = fourth_done
        partial = run([0, *early], last, end=6)
        token_sets += share_tokens(after(parts[1], third_done), [partial, *fourth_done])
        late = list(range(len(early) + 1, len(token_sets)))
        mixes[late[0]] = mix_of(token_sets[late[0]], left_diag)
        run(late, 0)
        first_rows = gather_rows(sums[0])
        run([0, *early], last, partial=partial, waits=[first_rows])
        first_near = halve_near(first_rows)
        run(late, last, waits=[first_near])
        summed = [halve_rest(first_near)]
    else:
        for which in range(3):
            token_sets += share_tokens(fetch_tokens(which, early_done))
        run(range(len(token_sets)), 0)
        summed = []
    summed.append(halve_rest(halve_near(gather_rows(sums[last]))))
    loss_part = jnp.sum(sum(term[2] for terms in sums for term in terms))

    right_both = jnp.concatenate([both[..., :chunk_columns] for both in summed], -1)
    left_both = jnp.concatenate([both[..., chunk_columns:] for both in summed], -1)

    scalars = jnp.stack(
        [
            sum(jnp.sum(jnp.square(both[..., chunk_columns:])) for both in summed),
            sum(jnp.sum(jnp.square(both[..., :chunk_columns])) for both in summed),
            loss_part,
        ]
    )
    away = lax.dynamic_index_in_dim(right_both, 1 - pair_bit, 0, keepdims=False)
    kept = lax.dynamic_index_in_dim(right_both, pair_bit, 0, keepdims=False)
    other = swap(away, "dp", pair)
    right_rows = jnp.concatenate([jnp.where(pair_bit == 0, kept, other), jnp.where(pair_bit == 0, other, kept)], 1)

    rows_here = left_both.shape[1]
    left_both = left_both.reshape(2, rows_here, half_blocks, tensor_count, mids // tensor_count)
    left_both = left_both.transpose(0, 3, 1, 4, 2).reshape(2, tensor_count, -1)
    places = [dp_pos - pair_bit * pair, dp_pos + (1 - pair_bit) * pair]
    place = jnp.arange(dp_count)[:, None, None]
    outgoing = jnp.where(place == places[0], left_both[:1], jnp.where(place == places[1], left_both[1:], 0.0))
    scalars = jnp.pad(scalars, (0, 125))
    outgoing = jnp.concatenate([outgoing, jnp.broadcast_to(scalars, outgoing.shape[:2] + scalars.shape)], 2)
    incoming = lax.all_to_all(outgoing.reshape((-1,) + outgoing.shape[2:]), ("dp", "tensor"), 0, 0, tiled=True)
    sq_left, sq_right, loss_all = jnp.sum(incoming[:, -128:-125], 0)
    incoming = incoming[:, :-128].reshape(dp_count, tensor_count, rows_here, mids // tensor_count, half_blocks)
    left_both = jnp.stack([lax.dynamic_index_in_dim(incoming, p, 0, keepdims=False) for p in places])
    left_rows = left_both.transpose(2, 3, 1, 0, 4).reshape(rows_here, -1)
    dir_left = left_rows * lax.rsqrt(sq_left / (features * blocks) + epsilon)
    dir_right = right_rows * lax.rsqrt(sq_right / (mids * columns * tensor_count) + epsilon)
    loss = loss_all / (2.0 * total_tokens)
    return (dir_left, dir_right, loss)


def solution(mesh):
    in_specs = (P("dp", None), P("dp", "tensor"), P(None, "tensor"), P(None, "tensor"))
    out_specs = (P("dp", "tensor"), P("dp", "tensor"), P())
    return jax.shard_map(local, mesh=mesh, in_specs=in_specs, out_specs=out_specs, check_vma=False)
```

```python
import functools

import jax
import jax.numpy as jnp
from jax import lax
from jax.experimental import pallas as pl
from jax.experimental.pallas import tpu as pltpu
from jax.sharding import PartitionSpec as P

epsilon = 1e-06
VMEM_BYTES = 56 * 1024 * 1024
LESS_VMEM_BYTES = 36 * 1024 * 1024


def swap(value, axis, stride):
    size = lax.axis_size(axis)
    return lax.ppermute(value, axis, [(a, a ^ stride) for a in range(size)])


def after(value, results):
    return lax.optimization_barrier((value, *results))[0] if results else value


def ordered(value, axis, strides):
    position = lax.axis_index(axis)
    for stride in strides:
        other = swap(value, axis, stride)
        high = (position // stride) % 2 == 1
        value = jnp.concatenate([jnp.where(high, other, value), jnp.where(high, value, other)], 0)
    return value


def contract(a, b, a_dim, b_dim):
    return lax.dot_general(a, b, (((a_dim,), (b_dim,)), ((), ())), preferred_element_type=jnp.float32)


AHEAD = 4


def row_tile(rows):
    return max(tile for tile in range(16, 513, 16) if rows % tile == 0)


def groups_of(low, high):
    cuts = [low, min(low + 2, high)] if low < high else [low]
    while cuts[-1] < high:
        cuts.append(min(cuts[-1] + 6, high))
    return list(zip(cuts[:-1], cuts[1:]))


def products_kernel(spans, parts, resumed, finish, blocks, scale, starts_ref, right_ref, *refs):
    count = len(parts)
    sets, refs = refs[: len(spans)], refs[len(spans) :]
    mixes, refs = refs[: len(spans)], refs[len(spans) :]
    pieces, refs = refs[: sum(parts)], refs[sum(parts) :]
    if resumed:
        partial_hbm, refs = refs[0], refs[1:]
    if finish:
        right_out, left_out, loss_out, total, rows_buf, mix_buf, piece_buf, sems, slope_buf, back_buf, turned_buf = refs
    else:
        total, rows_buf, mix_buf, piece_buf, sems = refs
    tokens = rows_buf.shape[0]
    depth = piece_buf.shape[0] // count
    slots = rows_buf.shape[1] // depth
    offsets = [sum(spans[:which]) for which in range(len(spans))]
    early = count - 2 if 0 < resumed < tokens else 0

    def start_of(slot):
        return pl.multiple_of(starts_ref[slot] * depth, depth)

    def copies(slot):
        found = []
        for which, span in enumerate(spans):
            target = rows_buf.at[pl.ds(offsets[which], span), pl.ds(slot * depth, depth)]
            source = sets[which].at[:, pl.ds(start_of(slot), depth)]
            found.append(pltpu.make_async_copy(source, target, sems.at[slot * len(spans) + which]))
        if slot < count:
            first, size = sum(parts[:slot]), depth // parts[slot]
            for part in range(parts[slot]):
                target = piece_buf.at[pl.ds(slot * depth + part * size, size)]
                sem = sems.at[(slots + 1) * len(spans) + 1 + first + part]
                found.append(pltpu.make_async_copy(pieces[first + part], target, sem))
        return found

    def begin(slots_now):
        for slot in slots_now:
            if slot < slots:
                for copy in copies(slot):
                    copy.start()

    def await_slots(slots_now):
        for slot in slots_now:
            for copy in copies(slot):
                copy.wait()

    def each_tile(low, high, body):
        if low < high:
            tile = row_tile(high - low)

            @pl.loop(0, (high - low) // tile)
            def _(step):
                body(pl.ds(pl.multiple_of(low + step * tile, 16), tile))

    first = [
        pltpu.make_async_copy(mixes[which], mix_buf.at[pl.ds(offsets[which], span)], sems.at[slots * len(spans) + which])
        for which, span in enumerate(spans)
    ]
    if resumed:
        sem = sems.at[(slots + 1) * len(spans)]
        first.append(pltpu.make_async_copy(partial_hbm, total.at[pl.ds(0, resumed)], sem))
    for copy in first:
        copy.start()
    begun = AHEAD
    begin(range(begun))
    for copy in first:
        copy.wait()
    for low, high in groups_of(0, early) + groups_of(early, count):
        begin(range(begun, high + AHEAD))
        begun = max(begun, high + AHEAD)
        await_slots(range(low, high))
        here = slice(low * depth, high * depth)

        def start_rows(at):
            term = contract(rows_buf[at, here], piece_buf[here], 1, 0)
            total[at] = contract(mix_buf[at], right_ref[...], 1, 0) - term

        def go_on(at):
            total[at] = total[at] - contract(rows_buf[at, here], piece_buf[here], 1, 0)

        if low >= early:
            each_tile(0, resumed, go_on)
        each_tile(resumed, tokens, go_on if low else start_rows)
    if not finish:
        return

    columns = right_ref.shape[1]
    mids = right_ref.shape[0] // blocks
    in_size = left_out.shape[1] // mids
    loss_out[...] = jnp.zeros_like(loss_out)
    begin(range(begun, slots))

    def slopes(at):
        residual = total[at]
        loss_out[...] += jnp.sum(residual * residual, axis=0, keepdims=True)
        slope = (residual * scale).astype(jnp.bfloat16)
        slope_buf[at] = slope
        back_buf[at] = contract(slope, right_ref[...], 1, 1)

    each_tile(0, tokens, slopes)
    full_right = contract(mix_buf[...], slope_buf[...], 0, 0)
    column_block = lax.broadcasted_iota(jnp.int32, (1, columns), 1) // (columns // blocks)
    grad_right = full_right[:mids]
    for b in range(1, blocks):
        grad_right = jnp.where(column_block == b, full_right[b * mids : (b + 1) * mids], grad_right)
    right_out[...] = grad_right
    turned_buf[...] = back_buf[...].T.astype(jnp.bfloat16)
    await_slots(range(count, slots))
    mid = lax.broadcasted_iota(jnp.int32, (mids, 1), 0)
    lane = lax.broadcasted_iota(jnp.int32, (1, depth), 1)

    @pl.loop(0, slots)
    def _(slot):
        full_left = contract(turned_buf[...], rows_buf[:, pl.ds(pl.multiple_of(slot * depth, depth), depth)], 1, 0)
        same = mid == (lane + start_of(slot)) // in_size
        sums = [
            jnp.sum(jnp.where(same, full_left[b * mids : (b + 1) * mids], 0.0), axis=0, keepdims=True)
            for b in range(blocks)
        ]
        left_out[:, pl.ds(start_of(slot), depth)] = jnp.concatenate(sums, 0)


def products(sets, mixes, right_diag, pieces, starts, blocks, scale, partial=None, finish=True):
    count = len(pieces)
    parts = tuple(len(piece) for piece in pieces)
    spans = tuple(rows.shape[0] for rows in sets)
    tokens, features = sum(spans), sets[0].shape[1]
    mid_columns, columns = right_diag.shape
    depth = sum(part.shape[0] for part in pieces[0])
    slots = starts.shape[0]
    resumed = 0 if partial is None else partial.shape[0]
    vmem = pl.BlockSpec(memory_space=pltpu.VMEM)
    operands = [starts, right_diag, *sets, *mixes, *[part for piece in pieces for part in piece]]
    if partial is not None:
        operands.append(partial)
    in_specs = [pl.BlockSpec(memory_space=pltpu.SMEM), vmem]
    in_specs += [pl.BlockSpec(memory_space=pl.ANY)] * (len(operands) - 2)
    scratch = [
        pltpu.VMEM((tokens, slots * depth), jnp.bfloat16),
        pltpu.VMEM((tokens, mid_columns), jnp.bfloat16),
        pltpu.VMEM((count * depth, columns), jnp.bfloat16),
        pltpu.SemaphoreType.DMA(((slots + 1) * len(spans) + 1 + sum(parts),)),
    ]
    flops = 2 * columns * depth * tokens * count
    if finish:
        shapes = [(mid_columns // blocks, columns), (blocks, features), (1, columns)]
        scratch = [pltpu.VMEM((tokens, columns), jnp.float32)] + scratch
        scratch += [
            pltpu.VMEM((tokens, columns), jnp.bfloat16),
            pltpu.VMEM((tokens, mid_columns), jnp.float32),
            pltpu.VMEM((mid_columns, tokens), jnp.bfloat16),
        ]
        flops += 4 * tokens * columns * mid_columns + 2 * tokens * mid_columns * features
    else:
        shapes = [(tokens, columns)]
    results = pl.pallas_call(
        functools.partial(products_kernel, spans, parts, resumed, finish, blocks, scale),
        out_shape=[jax.ShapeDtypeStruct(shape, jnp.float32) for shape in shapes],
        in_specs=in_specs,
        out_specs=[vmem] * len(shapes),
        scratch_shapes=scratch,
        compiler_params=pltpu.CompilerParams(
            vmem_limit_bytes=LESS_VMEM_BYTES if resumed or not finish else VMEM_BYTES
        ),
        cost_estimate=pl.CostEstimate(
            flops=flops, bytes_accessed=2 * depth * (tokens * slots + columns * count), transcendentals=0
        ),
    )(*operands)
    return results if finish else results[0]


def mix_of(rows, left_diag):
    return jnp.dot(rows, left_diag, preferred_element_type=jnp.float32).astype(jnp.bfloat16)


def local(tokens, dense_weight, left_factor, right_factor):
    tok_rows, features = tokens.shape
    weight_rows, columns = dense_weight.shape
    dp_count = lax.axis_size("dp")
    tensor_count = lax.axis_size("tensor")
    dp_pos = lax.axis_index("dp")
    tensor_pos = lax.axis_index("tensor")
    in_size = left_factor.shape[0]
    mids = right_factor.shape[0]
    blocks = left_factor.shape[1] * tensor_count // mids
    own_blocks = blocks // tensor_count
    out_size = columns // own_blocks
    total_tokens = tok_rows * dp_count

    bits = dp_count.bit_length() - 1
    strides = [1 << b for b in range(bits)]
    grouped = max(bits - 3, 0)
    pair = strides[grouped:][len(strides[grouped:]) // 2]
    others = [s for s in reversed(strides[grouped:]) if s != pair]
    pair_bit = (dp_pos // pair) % 2
    unit_rows = weight_rows << grouped

    half_blocks = own_blocks // 2
    chunks = 2 if half_blocks % 2 == 0 else 1
    chunk_blocks = half_blocks // chunks
    chunk_columns = chunk_blocks * out_size
    half_columns = half_blocks * out_size

    def weight_piece(half, chunk, waits=()):
        start = half * half_columns + chunk * chunk_columns
        return lax.dynamic_slice_in_dim(after(dense_weight, waits), start, chunk_columns, 1)

    held = [{} for _ in range(chunks)]
    theirs = []
    for chunk in range(chunks):
        held[chunk][0] = ordered(weight_piece(pair_bit, chunk), "dp", strides[:grouped])
        theirs.append(ordered(weight_piece(1 - pair_bit, chunk), "dp", strides[:grouped]))
    far, near = others

    def send(chunk, mask, stride, waits=()):
        held[chunk][mask ^ stride] = swap(after(held[chunk][mask], waits), "dp", stride)
        return held[chunk][mask ^ stride]

    def send_pair(chunk, waits=()):
        held[chunk][pair] = swap(after(theirs[chunk], waits), "dp", pair)
        return held[chunk][pair]

    share = tok_rows // tensor_count
    first_cut = share * 7 // 15 // 16 * 16
    cuts = [0, first_cut, first_cut + (share - first_cut) // 2 // 16 * 16, share]

    def fetch_tokens(which, waits=()):
        begin, size = cuts[which], cuts[which + 1] - cuts[which]
        part = lax.dynamic_slice_in_dim(tokens, tensor_pos * share + begin, size, 0)
        return swap(after(part, waits), "dp", pair)

    def share_tokens(part, waits=()):
        stride = tensor_count // 2
        while stride:
            moved = swap(part, "tensor", stride)
            if stride == 1:
                return [part, moved]
            part = jnp.concatenate([part, after(moved, waits)], 0)
            stride, waits = stride // 2, ()
        return [part]

    last = chunks - 1
    parts = [None] * 2
    done = [send(0, 0, far), send_pair(0), send(0, 0, near)]
    if last:
        done.append(send(last, 0, near))
    first_done = done
    done = [send(0, pair, far, done), send(0, pair, near, done), send(0, far, near, done)] + (
        [send_pair(last, done)] if last else []
    )
    second_done = done

    left_blocks = after(left_factor, first_done).reshape(in_size, mids // tensor_count, blocks)
    left_blocks = lax.all_to_all(left_blocks, "tensor", split_axis=2, concat_axis=1, tiled=True)
    left_blocks = lax.dynamic_slice_in_dim(left_blocks, pair_bit * half_blocks, half_blocks, 2)
    eye_left = jnp.eye(mids, dtype=jnp.bfloat16)
    left_rows = left_blocks.transpose(1, 0, 2)
    left_diag = (left_rows[:, :, :, None] * eye_left[:, None, None, :]).reshape(features, half_blocks * mids)
    right_half = lax.dynamic_slice_in_dim(right_factor, pair_bit * half_columns, half_columns, 1)

    mixes = {0: mix_of(tokens, left_diag)}
    done = [*second_done, mixes[0]]
    parts[0] = fetch_tokens(0, done)
    done = [parts[0], send(0, far ^ pair, near, done)] + (
        [send(last, 0, far, done), send(last, pair, near, done)] if last else []
    )
    early_done = done

    row_block = jnp.arange(chunk_blocks * mids) // mids
    column_block = jnp.arange(chunk_columns) // out_size
    same_block = row_block[:, None] == column_block[None, :]

    token_sets = [tokens]
    order = [0, near, pair, far, far ^ near, pair ^ near, far ^ pair, far ^ pair ^ near]
    starts = jnp.stack([(dp_pos ^ mask) >> grouped for mask in order]).astype(jnp.int32)
    right_diags = []
    for chunk in range(chunks):
        right_chunk = right_half[:, chunk * chunk_columns : (chunk + 1) * chunk_columns]
        right_diags.append(jnp.where(same_block, jnp.tile(right_chunk, (chunk_blocks, 1)), jnp.bfloat16(0)))
    sums = [[] for _ in range(chunks)]
    halves = {}
    previous = None

    def run(which, chunk, end=len(order), partial=None, waits=()):
        nonlocal previous
        for item in which:
            if item not in mixes:
                mixes[item] = mix_of(token_sets[item], left_diag)
        waits = [*waits, *([] if previous is None else [previous])]
        mine = [mixes[item][:, chunk * chunk_blocks * mids : (chunk + 1) * chunk_blocks * mids] for item in which]
        mine[0] = after(mine[0], waits)
        pieces = [halves.get((chunk, mask), [held[chunk].get(mask)]) for mask in order[:end]]
        finish = end == len(order)
        places = starts[:end]
        if partial is not None:
            pieces, places = pieces[-2:], jnp.concatenate([starts[-2:], starts[:-2]])
        terms = products(
            [token_sets[item] for item in which], mine, right_diags[chunk], pieces, places, chunk_blocks,
            1.0 / total_tokens, partial=partial, finish=finish,
        )
        if not finish:
            previous = terms
            return terms
        previous = terms[2]
        sums[chunk].append(terms)

    def gather_rows(terms):
        right_sum, left_sum = sum(term[0] for term in terms), sum(term[1] for term in terms)
        left_sum = left_sum.reshape(chunk_blocks, mids, in_size).transpose(2, 0, 1).reshape(in_size, chunk_blocks * mids)
        both = jnp.concatenate([right_sum, left_sum], 1)
        return both.reshape((2,) * bits + (both.shape[0] // dp_count, both.shape[1]))

    def halve(both, stride, at):
        bit = (dp_pos // stride) % 2
        away = lax.dynamic_index_in_dim(both, 1 - bit, at, keepdims=False)
        kept = lax.dynamic_index_in_dim(both, bit, at, keepdims=False)
        return kept + swap(away, "dp", stride)

    def halve_near(both):
        return halve(both, near, bits - near.bit_length())

    def halve_rest(both):
        places = [s for s in reversed(strides) if s != near]
        for stride in [far] + strides[:grouped]:
            both = halve(both, stride, places.index(stride))
            places.remove(stride)
        return both

    if last:
        source, cut = held[last][pair], unit_rows // 2
        upper = swap(after(source[:cut], early_done), "dp", far)
        late_part = fetch_tokens(1, early_done)
        near_part = send(last, far, near, early_done)
        run([0], 0, waits=early_done)
        token_sets += share_tokens(after(parts[0], early_done), [previous, upper, late_part, near_part])
        lower = swap(after(source[cut:], [upper]), "dp", far)
        last_part = fetch_tokens(2, [late_part])
        third_done = [lower, previous]
        early = list(range(1, len(token_sets)))
        run(early, 0)
        third_done.append(previous)
        parts[1] = jnp.concatenate([late_part, after(last_part, third_done)], 0)
        third_done.append(parts[1])
        fourth_done = [swap(after(half, third_done), "dp", near) for half in (upper, lower)]
        halves[last, far ^ pair] = [upper, lower]
        halves[last, far ^ pair ^ near] = fourth_done
        partial = run([0, *early], last, end=6)
        token_sets += share_tokens(after(parts[1], third_done), [partial, *fourth_done])
        late = list(range(len(early) + 1, len(token_sets)))
        mixes[late[0]] = mix_of(token_sets[late[0]], left_diag)
        run(late, 0)
        first_rows = gather_rows(sums[0])
        run([0, *early], last, partial=partial, waits=[first_rows])
        first_near = halve_near(first_rows)
        run(late, last, waits=[first_near])
        summed = [halve_rest(first_near)]
    else:
        for which in range(3):
            token_sets += share_tokens(fetch_tokens(which, early_done))
        run(range(len(token_sets)), 0)
        summed = []
    summed.append(halve_rest(halve_near(gather_rows(sums[last]))))
    loss_part = jnp.sum(sum(term[2] for terms in sums for term in terms))

    right_both = jnp.concatenate([both[..., :chunk_columns] for both in summed], -1)
    left_both = jnp.concatenate([both[..., chunk_columns:] for both in summed], -1)

    scalars = jnp.stack(
        [
            sum(jnp.sum(jnp.square(both[..., chunk_columns:])) for both in summed),
            sum(jnp.sum(jnp.square(both[..., :chunk_columns])) for both in summed),
            loss_part,
        ]
    )
    away = lax.dynamic_index_in_dim(right_both, 1 - pair_bit, 0, keepdims=False)
    kept = lax.dynamic_index_in_dim(right_both, pair_bit, 0, keepdims=False)
    other = swap(away, "dp", pair)
    right_rows = jnp.concatenate([jnp.where(pair_bit == 0, kept, other), jnp.where(pair_bit == 0, other, kept)], 1)

    rows_here = left_both.shape[1]
    left_both = left_both.reshape(2, rows_here, half_blocks, tensor_count, mids // tensor_count)
    left_both = left_both.transpose(0, 3, 1, 4, 2).reshape(2, tensor_count, -1)
    places = [dp_pos - pair_bit * pair, dp_pos + (1 - pair_bit) * pair]
    place = jnp.arange(dp_count)[:, None, None]
    outgoing = jnp.where(place == places[0], left_both[:1], jnp.where(place == places[1], left_both[1:], 0.0))
    scalars = jnp.pad(scalars, (0, 125))
    outgoing = jnp.concatenate([outgoing, jnp.broadcast_to(scalars, outgoing.shape[:2] + scalars.shape)], 2)
    incoming = lax.all_to_all(outgoing.reshape((-1,) + outgoing.shape[2:]), ("dp", "tensor"), 0, 0, tiled=True)
    sq_left, sq_right, loss_all = jnp.sum(incoming[:, -128:-125], 0)
    incoming = incoming[:, :-128].reshape(dp_count, tensor_count, rows_here, mids // tensor_count, half_blocks)
    left_both = jnp.stack([lax.dynamic_index_in_dim(incoming, p, 0, keepdims=False) for p in places])
    left_rows = left_both.transpose(2, 3, 1, 0, 4).reshape(rows_here, -1)
    dir_left = left_rows * lax.rsqrt(sq_left / (features * blocks) + epsilon)
    dir_right = right_rows * lax.rsqrt(sq_right / (mids * columns * tensor_count) + epsilon)
    loss = loss_all / (2.0 * total_tokens)
    return (dir_left, dir_right, loss)


def solution(mesh):
    in_specs = (P("dp", None), P("dp", "tensor"), P(None, "tensor"), P(None, "tensor"))
    out_specs = (P("dp", "tensor"), P("dp", "tensor"), P())
    return jax.shard_map(local, mesh=mesh, in_specs=in_specs, out_specs=out_specs, check_vma=False)
```
